512 devices in a mesh: branch: 4 (over x), tile: 128 (over z, y, core).
Axes of the slice: x: 4, y: 4, z: 16, core: 2. Of those that a mesh axis runs over, the one named last changes fastest.
Arguments:
- grad_first: bfloat16 [1024, 12288], P('tile', 'branch'), may hold values from -6 to 6
- grad_second: bfloat16 [512, 12288], P('tile', 'branch'), may hold values from -6 to 6
- grad_third: bfloat16 [256, 12288], P('tile', 'branch'), may hold values from -6 to 6
- grad_fourth: bfloat16 [128, 12288], P('tile', 'branch'), may hold values from -6 to 6
- pre_first: bfloat16 [1024, 12288], P('tile', 'branch'), may hold values from -6 to 6
- pre_second: bfloat16 [512, 12288], P('tile', 'branch'), may hold values from -6 to 6
- pre_third: bfloat16 [256, 12288], P('tile', 'branch'), may hold values from -6 to 6
- pre_fourth: bfloat16 [128, 12288], P('tile', 'branch'), may hold values from -6 to 6
- mid_twozero: bfloat16 [512, 6144], P('tile', 'branch'), may hold values from -6 to 6
- mid_threezero_one: bfloat16 [512, 6144], P('tile', 'branch'), may hold values from -6 to 6
- mid_threezero_two: bfloat16 [256, 3072], P('tile', 'branch'), may hold values from -6 to 6
- mid_threeone: bfloat16 [256, 6144], P('tile', 'branch'), may hold values from -6 to 6
- block_params: bfloat16 [1757952], P('tile'), may hold values from -1 to 1
Outputs:
- back_first: bfloat16 [1024, 12288], P('tile', 'branch')
- back_second: bfloat16 [512, 12288], P('tile', 'branch')
- back_third: bfloat16 [256, 12288], P('tile', 'branch')
- back_fourth: bfloat16 [128, 12288], P('tile', 'branch')
The draws below stay inside these ranges and needn't reach their ends.
All inputs are finite; a program needn't handle non-finite values.
Results may differ from the reference program's by a relative error of at most 0.013.
Values may be sent and summed in bfloat16 or wider, within the bound.
A program may use at most 128 MiB of HBM per device.

```python
import math
import jax
import jax.numpy as jnp
from jax import lax

C = 48
ROWS = 8
COLS = 256
N_TILE = 128


def weight_table_drawn(base):
    widths = [base, 2 * base, 4 * base, 8 * base]
    entries = []
    for target in range(4):
        for source in range(4):
            if target < source:
                entries.append(((target, source, 0), (widths[source], widths[target])))
            elif target > source:
                for section_no in range(target - source):
                    out_width = widths[target] if section_no == target - source - 1 else widths[source]
                    entries.append(((target, source, section_no), (3, 3, widths[source], out_width)))
    return entries


def draw_block_params(key, part):
    key = jax.random.fold_in(key, 7)
    scales = []
    for entry_key, entry_shape in weight_table_drawn(C):
        target, source, section_no = entry_key
        entry_size = math.prod(entry_shape)
        if len(entry_shape) == 2:
            deviation = 0.5 ** (source - target) / math.sqrt(entry_shape[1])
        else:
            deviation = 2.0 / (3.0 * math.sqrt(entry_shape[3]))
        scales.append(jnp.full((entry_size,), deviation, jnp.float32))
    scale_vector = jnp.concatenate(scales)
    values = jnp.clip(jax.random.normal(key, scale_vector.shape, jnp.float32), -4.0, 4.0)
    return (values * scale_vector).astype(jnp.bfloat16)


def steps_of(key, shape, cuts, least, top_value):
    level = 1.0
    for position, shards_of in cuts:
        heights = jax.random.uniform(jax.random.fold_in(jax.random.fold_in(key, 6), position), (shards_of,), jnp.float32, least / len(cuts), top_value / len(cuts))
        level = level * jnp.repeat(jnp.exp(heights), shape[position] // shards_of).reshape((-1,) + (1,) * (len(shape) - 1 - position))
    return level


def bell_draw(own_key, dims, width, reach, shards=(), kind=jnp.bfloat16):
    result = width * jax.random.normal(own_key, dims, jnp.float32)
    if shards:
        result = result * steps_of(own_key, dims, shards, -0.22, 0.18)
    return jnp.clip(result, -reach, reach).astype(kind)


def setup_inputs(seed: int = 0) -> dict:
    key_of = jax.random.split(jax.random.key(seed), 14)
    return {
        "grad_first": bell_draw(key_of[0], (ROWS * N_TILE, COLS * C), 1.0, 6.0, ((0, 128), (1, 4))),
        "grad_second": bell_draw(key_of[1], (ROWS * N_TILE // 2, COLS * C), 1.0, 6.0, ((0, 128), (1, 4))),
        "grad_third": bell_draw(key_of[2], (ROWS * N_TILE // 4, COLS * C), 1.0, 6.0, ((0, 128), (1, 4))),
        "grad_fourth": bell_draw(key_of[3], (ROWS * N_TILE // 8, COLS * C), 1.0, 6.0, ((0, 128), (1, 4))),
        "pre_first": bell_draw(key_of[4], (ROWS * N_TILE, COLS * C), 1.0, 6.0, ((0, 128), (1, 4))),
        "pre_second": bell_draw(key_of[5], (ROWS * N_TILE // 2, COLS * C), 1.0, 6.0, ((0, 128), (1, 4))),
        "pre_third": bell_draw(key_of[6], (ROWS * N_TILE // 4, COLS * C), 1.0, 6.0, ((0, 128), (1, 4))),
        "pre_fourth": bell_draw(key_of[7], (ROWS * N_TILE // 8, COLS * C), 1.0, 6.0, ((0, 128), (1, 4))),
        "mid_twozero": bell_draw(key_of[8], (ROWS * N_TILE // 2, COLS * C // 2), 1.0, 6.0, ((0, 128), (1, 4))),
        "mid_threezero_one": bell_draw(key_of[9], (ROWS * N_TILE // 2, COLS * C // 2), 1.0, 6.0, ((0, 128), (1, 4))),
        "mid_threezero_two": bell_draw(key_of[10], (ROWS * N_TILE // 4, COLS * C // 4), 1.0, 6.0, ((0, 128), (1, 4))),
        "mid_threeone": bell_draw(key_of[11], (ROWS * N_TILE // 4, COLS * C // 2), 1.0, 6.0, ((0, 128), (1, 4))),
        "block_params": draw_block_params(jax.random.fold_in(key_of[13], 71), 0),
    }


def weight_table(base):
    widths = [base, 2 * base, 4 * base, 8 * base]
    entries = []
    for target in range(4):
        for source in range(4):
            if target < source:
                entries.append(((target, source, 0), (widths[source], widths[target])))
            elif target > source:
                for section_no in range(target - source):
                    out_width = widths[target] if section_no == target - source - 1 else widths[source]
                    entries.append(((target, source, section_no), (3, 3, widths[source], out_width)))
    return entries

def unpack(flat_params, base):
    unpacked = {}
    offset = 0
    for entry_key, entry_shape in weight_table(base):
        entry_size = math.prod(entry_shape)
        unpacked[entry_key] = flat_params[offset:offset + entry_size].reshape(entry_shape)
        offset += entry_size
    return unpacked

def stride_conv(image_map, kernel):
    return lax.conv_general_dilated(image_map[None], kernel, (2, 2), ((1, 1), (1, 1)), dimension_numbers=('NHWC', 'HWIO', 'NHWC'), precision=lax.Precision.HIGHEST)[0]

def pull_back(coarse_grad, kernel, fine_shape):
    kernel_wide = kernel.astype(jnp.float32)
    _, pullback = jax.vjp(lambda image_map: stride_conv(image_map, kernel_wide), jnp.zeros(fine_shape, jnp.float32))
    return pullback(coarse_grad.astype(jnp.float32))[0]

def reference(grad_first, grad_second, grad_third, grad_fourth, pre_first, pre_second, pre_third, pre_fourth, mid_twozero, mid_threezero_one, mid_threezero_two, mid_threeone, block_params):
    kernels = unpack(block_params, C)
    widths = [C, 2 * C, 4 * C, 8 * C]
    full_rows = grad_first.shape[0]
    cotangents = [grad_first, grad_second, grad_third, grad_fourth]
    preacts = [pre_first, pre_second, pre_third, pre_fourth]
    masked = []
    for branch_no in range(4):
        chosen = jnp.where(preacts[branch_no] > 0, cotangents[branch_no], jnp.zeros_like(cotangents[branch_no]))
        masked.append(chosen.reshape(full_rows // 2 ** branch_no, COLS // 2 ** branch_no, widths[branch_no]))
    inner = {(2, 0): [mid_twozero.reshape(full_rows // 2, COLS // 2, C)], (3, 0): [mid_threezero_one.reshape(full_rows // 2, COLS // 2, C), mid_threezero_two.reshape(full_rows // 4, COLS // 4, C)], (3, 1): [mid_threeone.reshape(full_rows // 4, COLS // 4, 2 * C)]}
    totals = [masked[branch_no].astype(jnp.float32) for branch_no in range(4)]
    for target in range(4):
        for source in range(4):
            if target < source:
                factor = 2 ** (source - target)
                rows_out = full_rows // 2 ** source
                cols_out = COLS // 2 ** source
                blocks = masked[target].reshape(rows_out, factor, cols_out, factor, widths[target])
                pooled = lax.optimization_barrier(jnp.sum(blocks, axis=(1, 3), dtype=jnp.float32)).astype(jnp.bfloat16)
                term = jnp.dot(pooled.reshape(-1, widths[target]), kernels[target, source, 0].T, preferred_element_type=jnp.float32)
                totals[source] = totals[source] + term.reshape(rows_out, cols_out, widths[source])
            elif target > source:
                current = masked[target]
                for section_no in reversed(range(target - source)):
                    kernel = kernels[target, source, section_no]
                    fine_level = source + section_no
                    fine_shape = (full_rows // 2 ** fine_level, COLS // 2 ** fine_level, kernel.shape[2])
                    pulled = pull_back(current, kernel, fine_shape)
                    if section_no > 0:
                        current = jnp.where(inner[target, source][section_no - 1] > 0, pulled, 0.0).astype(jnp.bfloat16)
                    else:
                        totals[source] = totals[source] + pulled
    outputs = [totals[branch_no].reshape(full_rows // 2 ** branch_no, COLS * C).astype(jnp.bfloat16) for branch_no in range(4)]
    return (outputs[0], outputs[1], outputs[2], outputs[3])
```

```python
import jax
import jax.numpy as jnp
from jax import lax
from jax.experimental import pallas as pl
from jax.experimental.pallas import tpu as pltpu
from jax.sharding import PartitionSpec as P

BF = jnp.bfloat16
F32 = jnp.float32
MESH = pl.DeviceIdType.MESH
N_TILE = 128
N_BRANCH = 4
NZ = 16
SHARD = 13734
CELL = 384
RAW_ROWS = 112
BASE = 104
WINDOW = 464

ROW0 = {
    (0, 1, 0): 0,
    (0, 2, 0): 12,
    (0, 3, 0): 36,
    (1, 0, 0): 84,
    (1, 2, 0): 192,
    (1, 3, 0): 240,
    (2, 0, 0): 336,
    (2, 0, 1): 390,
    (2, 1, 0): 606,
    (2, 3, 0): 1038,
    (3, 0, 0): 1230,
    (3, 0, 1): 1284,
    (3, 0, 2): 1338,
    (3, 1, 0): 1770,
    (3, 1, 1): 1986,
    (3, 2, 0): 2850,
}


def remote(src, dst, send, recv, branch, tile):
    return pltpu.make_async_remote_copy(
        src_ref=src, dst_ref=dst, send_sem=send, recv_sem=recv, device_id=(branch, tile), device_id_type=MESH
    )


def gather_kernel(
    raw, g2, g3, g4, p2, p3, p4, m20, m30a, m30b, m31,
    tiles, row_in, col_in, corner_in,
    raw1, raw2, win, row_f, col_f, row_out, col_out,
    h_send, h_recv, z_send, z_recv, s_send, s_recv,
):
    b = lax.axis_index("branch")
    k = lax.axis_index("tile")
    z, y, c = k // 8, lax.rem(k // 2, 4), lax.rem(k, 2)

    def tile_of(zz, yy, cc):
        return zz * 8 + yy * 2 + cc

    def wrap(value, count):
        return lax.rem(value + count, count)

    row_f[...] = jnp.zeros_like(row_f)
    col_f[...] = jnp.zeros_like(col_f)
    at_row, at_col = 0, 0
    for g, p in ((g2, p2), (g3, p3), (g4, p4)):
        rows = g.shape[0]
        masked = jnp.where(p[...].astype(F32) > 0, g[...].astype(F32), 0.0)
        for cell in range(8):
            row_f[at_row + cell : at_row + cell + 1, :] = masked[0:1, CELL * cell : CELL * (cell + 1)]
        col_f[at_col : at_col + rows, :] = masked[:, 0:CELL]
        at_row, at_col = at_row + 8, at_col + rows
    for m, at_row, at_col in ((m20, 24, 8), (m30a, 28, 12), (m31, 32, 18), (m30b, 36, 16)):
        rows, units = m.shape[0], m.shape[1] // CELL
        value = m[...].astype(F32)
        for unit in range(units):
            row_f[at_row + unit : at_row + unit + 1, :] = value[0:1, CELL * unit : CELL * (unit + 1)]
        col_f[at_col : at_col + rows, :] = value[:, 0:CELL]
    row_out[...] = row_f[...].astype(BF)
    col_out[...] = col_f[...].astype(BF)

    left, right = wrap(b - 1, N_BRANCH), wrap(b + 1, N_BRANCH)
    up1, up2 = wrap(k - 1, N_TILE), wrap(k - 2, N_TILE)
    down1, down2 = wrap(k + 1, N_TILE), wrap(k + 2, N_TILE)
    y_prev, y_next = wrap(y - 1, 4), wrap(y + 1, 4)

    partners = [
        (b, up1), (b, up2), (b, down1), (b, down2), (left, k), (right, k), (left, up1), (right, down1),
        (b, tile_of(z, y_prev, c)), (b, tile_of(z, y_next, c)), (b, tile_of(z, y, 1 - c)),
    ]
    barrier = pltpu.get_barrier_semaphore()
    for who in partners:
        pl.semaphore_signal(barrier, inc=1, device_id=who, device_id_type=MESH)
    for step in range(1, NZ):
        pl.semaphore_signal(
            barrier, inc=1, device_id=(b, tile_of(wrap(z + step, NZ), y, c)), device_id_type=MESH
        )
    pl.semaphore_wait(barrier, len(partners) + NZ - 1)

    first = [
        remote(raw, raw1, h_send.at[0], h_recv.at[0], b, up1),
        remote(raw, raw2, h_send.at[1], h_recv.at[1], b, up2),
        remote(row_out, row_in, h_send.at[2], h_recv.at[2], b, up1),
        remote(col_out, col_in, h_send.at[3], h_recv.at[3], left, k),
        remote(col_out, corner_in, h_send.at[4], h_recv.at[4], left, up1),
    ]
    for copy in first:
        copy.start()

    group, j = k // 4, lax.rem(k, 4)
    first_tile = (7 * j) // 3
    delta = 13734 * j - 6144 * first_tile - 360 * group + BASE * 128
    win[...] = jnp.zeros_like(win)
    lane = lax.broadcasted_iota(jnp.int32, (RAW_ROWS, 128), 1)
    for d, shard in enumerate((raw, raw1, raw2)):
        if d > 0:
            first[d - 1].wait_recv()
        start = delta + SHARD * d
        q, phase = start // 128, lax.rem(start, 128)
        rolled = pltpu.roll(shard[...].astype(F32), phase, 1)
        win[pl.ds(q, RAW_ROWS), :] += jnp.where(lane >= phase, rolled, 0.0)
        win[pl.ds(q + 1, RAW_ROWS), :] += jnp.where(lane >= phase, 0.0, rolled)
    for s in range(2):
        n = 7 * j + 2 * b + s
        row_tile = 9 * group + n // 3
        offset = jnp.where(row_tile >= 124, 2, 10)
        origin = BASE + 3 * (16 * (n // 3 - first_tile) + offset) + lax.rem(n, 3)
        tiles[s, b, y, c, z] = win[pl.ds(origin, 16, stride=3), :].astype(BF)

    copies = []
    own = tiles.at[:, b, y, c, z]
    for step in range(1, NZ):
        copy = remote(
            own, own, z_send.at[step - 1], z_recv.at[step - 1], b, tile_of(wrap(z + step, NZ), y, c)
        )
        copy.start()
        copies.append(copy)
    for copy in copies:
        copy.wait_recv()

    pending = []

    class Half:
        def __init__(self, s):
            self.s = s
            self.u, self.v = (b, y) if s == 0 else (y, b)
            self.used = 36 * s

        def bundle(self, u, v, part):
            x_at, y_at = (u, v) if self.s == 0 else (v, u)
            ref = tiles.at[self.s, x_at, y_at, c]
            return ref if part is None else ref.at[pl.ds(8 * part, 8)]

        def send(self, u, v, part, to_u, to_v, other_core=False):
            x_to, y_to = (to_u, to_v) if self.s == 0 else (to_v, to_u)
            ref = self.bundle(u, v, part)
            copy = remote(
                ref, ref, s_send.at[self.used], s_recv.at[self.used], x_to,
                tile_of(z, y_to, 1 - c if other_core else c),
            )
            copy.start()
            self.used += 1
            pending.append(copy)
            return copy

        def first(self):
            u, v = self.u, self.v
            self.to_next = self.send(u, v, None, wrap(u + 1, 4), v)
            self.to_prev = self.send(u, v, None, wrap(u - 1, 4), v)
            self.second = [self.spread(u)]

        def spread(self, u_of):
            u, v = self.u, self.v
            to_next = self.send(u_of, v, None, u, wrap(v + 1, 4))
            to_prev = self.send(u_of, v, None, u, wrap(v - 1, 4))
            self.send(u_of, v, None, u, v, True)
            return u_of, to_next, to_prev

        def forward(self):
            u, v = self.u, self.v
            self.to_next.wait_recv()
            prev_u, next_u = wrap(u - 1, 4), wrap(u + 1, 4)
            self.far_next = self.send(prev_u, v, 0, next_u, v)
            self.second.append(self.spread(prev_u))
            self.to_prev.wait_recv()
            self.far_prev = self.send(next_u, v, 1, prev_u, v)
            self.second.append(self.spread(next_u))

        def far(self):
            self.far_next.wait_recv()
            self.far_prev.wait_recv()
            self.second.append(self.spread(wrap(self.u + 2, 4)))

        def finish(self, number):
            u, v = self.u, self.v
            u_of, to_next, to_prev = self.second[number]
            to_next.wait_recv()
            a = self.send(u_of, wrap(v - 1, 4), 0, u, wrap(v + 1, 4))
            self.send(u_of, wrap(v - 1, 4), None, u, v, True)
            to_prev.wait_recv()
            d = self.send(u_of, wrap(v + 1, 4), 1, u, wrap(v - 1, 4))
            self.send(u_of, wrap(v + 1, 4), None, u, v, True)
            return u_of, a, d

        def last(self, state):
            u_of, a, d = state
            a.wait_recv()
            d.wait_recv()
            self.send(u_of, wrap(self.v + 2, 4), None, self.u, self.v, True)

    halves = [Half(0), Half(1)]
    for half in halves:
        half.first()
    for half in halves:
        half.forward()
    for half in halves:
        half.far()
    states = []
    for number in range(4):
        for half in halves:
            states.append((half, half.finish(number)))
    for half, state in states:
        half.last(state)
    waited = set()
    for half in halves:
        waited.update([id(half.to_next), id(half.to_prev), id(half.far_next), id(half.far_prev)])
        for _, to_next, to_prev in half.second:
            waited.update([id(to_next), id(to_prev)])
    for _, (_, a, d) in states:
        waited.update([id(a), id(d)])
    for copy in pending:
        if id(copy) not in waited:
            copy.wait_recv()
    for copy in pending + copies + first:
        copy.wait_send()
    for copy in first[2:]:
        copy.wait_recv()


def tile_at(row_tile, jb):
    group, n = row_tile // 9, 3 * (row_tile % 9) + jb
    j, slot = n // 7, n % 7
    k = 4 * group + j
    return slot % 2, slot // 2, (k // 2) % 4, k % 2, k // 8


def dot(a, b):
    return lax.dot_general(a, b, (((1,), (0,)), ((), ())), preferred_element_type=F32)


def dot_nt(a, b):
    return lax.dot_general(a, b, (((1,), (1,)), ((), ())), preferred_element_type=F32)


def unit_matrix(rows, cols, target):
    column = lax.broadcasted_iota(jnp.int32, (1, cols), 1)
    row = lax.broadcasted_iota(jnp.int32, (rows, cols), 0)
    return jnp.where(row == target(column), 1.0, 0.0).astype(BF)


def compute_kernel(
    tiles, row_in, col_in, corner_in,
    g1, g2, g3, g4, p1, p2, p3, p4, m20, m30a, m30b, m31,
    o1, o2, o3, o4,
    e3, e2, e1, u3, u2, u1,
    wide, c0, c1, c2, c3, sg1, sg2, q20, q30a, q30b, q31, k1, k2a, k2b, nxt, out,
):
    b = lax.axis_index("branch")
    k = lax.axis_index("tile")
    has_row = k < N_TILE - 1
    has_col = b < N_BRANCH - 1

    def load_rows(row_tile, count):
        columns = [
            jnp.concatenate([tiles[tile_at(row_tile + t, jb)] for t in range(count)], axis=0) for jb in range(3)
        ]
        return jnp.concatenate(columns, axis=1)

    def rows_of(key, rows, j, at=0):
        n = CELL // j
        r0 = ROW0[key]
        row_tile, offset = (286, 0) if r0 == 0 else divmod(r0 - 10, 16)
        count = -(-(offset + rows) // 16)
        width = 256 if j == 192 else 128

        def target(col):
            part, lane = col // width, lax.rem(col, width) - at
            return jnp.where((lane >= 0) & (lane < j), part * j + lane, -1)

        split = dot(load_rows(row_tile, count), unit_matrix(CELL, n * width, target))
        parts = []
        for half in range(width // 128):
            for part in range(n):
                wide[half, pl.ds(part, 16 * count, stride=n), :] = split[
                    :, part * width + 128 * half : part * width + 128 * (half + 1)
                ]
            parts.append(wide[half, offset * n : (offset + rows) * n, :])
        return parts[0] if len(parts) == 1 else jnp.concatenate(parts, axis=1)

    def place(weights, j, low, high):
        rows = weights.shape[1]

        def target(col):
            which = col // j
            return jnp.where((which >= low) & (which < high), lax.rem(col, j), -1)

        return dot(weights, unit_matrix(rows, CELL, target))

    def taps(e, row0, pitch, weights, placed, seg, nxt_seg, nxt_width):
        count = len(placed)
        i = weights.shape[0] // 9

        def tap(value, a, bb):
            return value[(3 * a + bb) * i : (3 * a + bb + 1) * i]

        for a in range(3):
            for q in range(count):
                even = row0 + CELL * a + 2 * q * pitch
                e[even : even + i, seg : seg + CELL] = tap(placed[q], a, 1).astype(BF)
                odd = even + pitch
                value = tap(placed[q], a, 2)
                if q + 1 < count:
                    value = value + tap(placed[q + 1], a, 0)
                else:
                    e[odd : odd + i, nxt_seg : nxt_seg + nxt_width] = tap(weights, a, 0).astype(BF)
                e[odd : odd + i, seg : seg + CELL] = value.astype(BF)

    e3[...] = jnp.zeros_like(e3)
    e2[...] = jnp.zeros_like(e2)
    e1[...] = jnp.zeros_like(e1)

    for key, i, row0, pitch in (
        ((3, 2, 0), 192, 0, 192),
        ((3, 1, 1), 96, 1152, 96),
        ((3, 0, 2), 48, 1152 + 192, 48),
    ):
        r0 = ROW0[key]
        start = 124 + (r0 - 1986) // 16 if r0 >= 1986 else (r0 - 10) // 16
        for a in range(3):
            even = row0 + CELL * a
            odd = even + pitch
            for bb, at, seg in ((1, even, 0), (2, odd, 0), (0, odd, CELL)):
                first = start + (3 * a + bb) * (i // 16)
                for t in range(i // 16):
                    for jb in range(3):
                        e3[at + 16 * t : at + 16 * (t + 1), seg + 128 * jb : seg + 128 * (jb + 1)] = tiles[
                            tile_at(first + t, jb)
                        ]

    w = rows_of((2, 1, 0), 432, 192)
    taps(e2, 0, 96, w, [place(w.astype(BF), 192, q, q + 1) for q in range(2)], 0, 768, 256)
    w = rows_of((3, 1, 0), 216, 96)
    taps(e2, 0, 96, w, [place(w.astype(BF), 96, q, q + 1) for q in range(2)], 384, 1024, 128)
    w = rows_of((2, 0, 1), 216, 192)
    placed = [place(w.astype(BF), 192, q, q + 1) for q in range(2)]
    taps(e2, 1152, 96, w, placed, 0, 768, 256)
    w = rows_of((3, 0, 1), 54, 48)
    w_next = rows_of((3, 0, 1), 54, 48, 64)
    placed = [place(w.astype(BF), 48, 4 + q, 5 + q) for q in range(2)]
    taps(e2, 1152 + 48, 96, w_next, placed, 384, 1024 + 128, 128)

    w = rows_of((1, 0, 0), 108, 96)
    taps(e1, 0, 48, w, [place(w.astype(BF), 96, q, q + 1) for q in range(4)], 0, 768, 128)
    w = rows_of((2, 0, 0), 54, 48) + 0.0
    w = w + rows_of((3, 0, 0), 54, 48, 48)
    taps(e1, 0, 48, w, [place(w.astype(BF), 96, q, q + 1) for q in range(4)], 384, 896, 128)

    u3[:, 0:384] = place(rows_of((0, 3, 0), 48, 48).astype(BF), 48, 0, 8).astype(BF)
    u3[:, 384:768] = place(rows_of((1, 3, 0), 96, 96).astype(BF), 96, 0, 4).astype(BF)
    u3[:, 768:1152] = place(rows_of((2, 3, 0), 192, 192).astype(BF), 192, 0, 2).astype(BF)
    w02 = rows_of((0, 2, 0), 24, 48).astype(BF)
    w12 = rows_of((1, 2, 0), 48, 96).astype(BF)
    for q in range(2):
        u2[192 * q : 192 * (q + 1), 0:384] = place(w02, 48, 4 * q, 4 * q + 4).astype(BF)
        u2[192 * q : 192 * (q + 1), 384:768] = place(w12, 96, 2 * q, 2 * q + 2).astype(BF)
    w01 = rows_of((0, 1, 0), 12, 48).astype(BF)
    for q in range(4):
        u1[96 * q : 96 * (q + 1), :] = place(w01, 48, 2 * q, 2 * q + 2).astype(BF)

    def put(buffer, row, value):
        rows = value.shape[0]
        for l in range(3):
            buffer[l, row : row + rows, :] = value[:, 128 * l : 128 * (l + 1)]

    def spread_units(buffer, value, units):
        rows = value.shape[0]
        for unit in range(units):
            for l in range(3):
                piece = value[:, CELL * unit + 128 * l : CELL * unit + 128 * (l + 1)]
                if rows == 1:
                    buffer[l, unit : unit + 1, :] = piece
                else:
                    buffer[l, pl.ds(unit, rows, stride=units), :] = piece

    def masked(g, p):
        return jnp.where(p[...].astype(F32) > 0, g[...].astype(F32), 0.0)

    row_halo = row_in[...].astype(F32)
    col_halo = col_in[...].astype(F32)
    corner = corner_in[...].astype(F32)
    row_zero = jnp.where(has_row, row_halo, 0.0)
    col_zero = jnp.where(has_col, col_halo, 0.0)
    corner_zero = jnp.where(has_row & has_col, corner, 0.0)

    for buffer in (c1, c2, c3, sg1, sg2, q20, q30a, q30b, q31, k1, k2a, k2b, nxt):
        buffer[...] = jnp.zeros_like(buffer)
    spread_units(c0, masked(g1, p1), 8)
    at = 0
    for buffer, g, p, rows, halo in ((c1, g2, p2, 4, 0), (c2, g3, p3, 2, 8), (c3, g4, p4, 1, 16)):
        spread_units(buffer, masked(g, p), 8)
        put(buffer, 8 * rows, row_zero[halo : halo + 8])
        put(buffer, 8 * rows + 8, col_zero[at : at + rows])
        put(buffer, 8 * rows + 8 + rows, corner_zero[at : at + 1])
        at += rows

    for buffer, m, rows, units, halo, at in (
        (q20, m20, 4, 4, 24, 8), (q30a, m30a, 4, 4, 28, 12), (q31, m31, 2, 4, 32, 18), (q30b, m30b, 2, 2, 36, 16),
    ):
        spread_units(buffer, m[...].astype(F32), units)
        put(buffer, rows * units, row_halo[halo : halo + units])
        put(buffer, (rows + 1) * units, col_halo[at : at + rows])
        put(buffer, (rows + 1) * units + rows, corner[at : at + 1])

    def flags(buffer):
        whole = jnp.concatenate([buffer[l] for l in range(3)], axis=1)
        return jnp.where(whole > 0, 1.0, 0.0).astype(BF)

    def target20(shift):
        def target(col):
            part, lane = col // CELL, lax.rem(col, CELL)
            pixel, channel = lane // 96, lax.rem(lane, 96) - shift
            return jnp.where((channel >= 0) & (channel < 48), part * 192 + pixel * 48 + channel, -1)

        return target

    def target31(col):
        part, lane = col // CELL, lax.rem(col, CELL)
        return jnp.where(lane < 192, part * 192 + lane, -1)

    def target30b(col):
        part, lane = col // CELL, lax.rem(col, CELL) - 192
        return jnp.where((lane >= 0) & (lane < 96), part * 96 + lane, -1)

    def keep(buffer, value, parts, count, extra_from, extra_rows, extra_to):
        for l in range(3):
            for part in range(parts):
                lanes = slice(part * CELL + 128 * l, part * CELL + 128 * (l + 1))
                buffer[l, pl.ds(part, count, stride=parts), :] = value[0:count, lanes]
            buffer[l, extra_to : extra_to + extra_rows, :] = value[
                extra_from : extra_from + extra_rows, 128 * l : 128 * (l + 1)
            ]

    mask1 = dot(flags(q20), unit_matrix(CELL, 768, target20(0))) + dot(
        flags(q30a), unit_matrix(CELL, 768, target20(48))
    )
    keep(k1, mask1, 2, 20, 20, 5, 40)
    keep(k2a, dot(flags(q31), unit_matrix(CELL, 768, target31)), 2, 12, 12, 3, 24)
    keep(k2b, dot(flags(q30b), unit_matrix(CELL, 1536, target30b)), 4, 6, 6, 3, 24)

    def lanes_of(buffer, count=3):
        return [buffer[l] for l in range(count)]

    def shifted(buffer, rows, count):
        total = buffer.shape[1]
        pieces = []
        for l in range(count):
            nxt[l, 0 : 8 * rows, :] = buffer[l, 1 : 8 * rows + 1, :]
            for p in range(rows):
                nxt[l, 8 * p + 7 : 8 * p + 8, :] = buffer[l, 8 * rows + p : 8 * rows + p + 1, :]
            nxt[l, 8 * rows : total, :] = jnp.zeros((total - 8 * rows, 128), F32)
            pieces.append(nxt[l, 0:total, :])
        return pieces

    def lhs(pieces):
        return jnp.concatenate([piece.astype(BF) for piece in pieces], axis=1)

    def rows_out(y, a, lo, hi, lane0):
        return y[lo:hi, lane0 + CELL * a : lane0 + CELL * (a + 1)]

    def upsampled(y, p, lane0):
        even = rows_out(y, 1, 8 * p, 8 * p + 8, lane0)
        odd = rows_out(y, 2, 8 * p, 8 * p + 8, lane0) + rows_out(y, 0, 8 * p + 8, 8 * p + 16, lane0)
        return even, odd

    def section(buffer, y, rows, kept):
        base = 8 * (rows + 1)
        for p in range(rows):
            even, odd = upsampled(y, p, 1152)
            put(buffer, 16 * p, even)
            put(buffer, 16 * p + 8, odd)
        put(buffer, 16 * rows, rows_out(y, 1, 8 * rows, 8 * rows + 8, 1152))
        extra = 8 * (2 * rows + 1)
        for p in range(rows + 1):
            put(buffer, extra + 2 * p, rows_out(y, 1, base + p, base + p + 1, 1152))
            if p < rows:
                odd = rows_out(y, 2, base + p, base + p + 1, 1152) + rows_out(y, 0, base + p + 1, base + p + 2, 1152)
                put(buffer, extra + 2 * p + 1, odd)
        for l in range(3):
            buffer[l] = jnp.where(kept(l) > 0.5, buffer[l], 0.0)

    def emit(ref, rows, value):
        put(out, 0, value)
        for cell in range(8):
            for l in range(3):
                lane0 = CELL * cell + 128 * l
                if rows == 1:
                    piece = out[l, cell : cell + 1, :]
                else:
                    piece = out[l, pl.ds(cell, rows, stride=8), :]
                ref[:, lane0 : lane0 + 128] = piece.astype(BF)

    def block_sums(buffer, rows, factor):
        groups = []
        for first in range(0, rows, factor):
            pieces = []
            for l in range(3):
                total = buffer[l, 8 * first : 8 * first + 8, :]
                for p in range(first + 1, first + factor):
                    total = total + buffer[l, 8 * p : 8 * p + 8, :]
                pieces.append(total)
            groups.append(jnp.concatenate(pieces, axis=1))
        return jnp.concatenate(groups, axis=0).astype(BF)

    def own(buffer, rows):
        return jnp.concatenate([buffer[l, 0 : 8 * rows, :] for l in range(3)], axis=1)

    up = jnp.concatenate([block_sums(c0, 8, 8), block_sums(c1, 4, 4), block_sums(c2, 2, 2)], axis=1)
    emit(o4, 1, own(c3, 1) + dot_nt(up, u3[...]))

    y3 = dot_nt(lhs(lanes_of(c3) + shifted(c3, 2, 3)), e3[...])
    up = jnp.concatenate([block_sums(c0, 8, 4), block_sums(c1, 4, 2)], axis=1)
    down = jnp.concatenate(upsampled(y3, 0, 0), axis=0)
    emit(o3, 2, own(c2, 2) + dot_nt(up, u2[...]) + down)

    section(sg2, y3, 1, lambda l: k2a[l] + k2b[l])
    y2 = dot_nt(lhs(lanes_of(c2) + lanes_of(sg2) + shifted(c2, 3, 2) + shifted(sg2, 3, 2)), e2[...])
    down = jnp.concatenate(upsampled(y2, 0, 0) + upsampled(y2, 1, 0), axis=0)
    emit(o2, 4, own(c1, 4) + dot_nt(block_sums(c0, 8, 2), u1[...]) + down)

    section(sg1, y2, 2, lambda l: k1[l])
    y1 = dot_nt(lhs(lanes_of(c1) + lanes_of(sg1) + shifted(c1, 5, 1) + shifted(sg1, 5, 1)), e1[...])
    rows = []
    for p in range(4):
        rows.extend(upsampled(y1, p, 0))
    emit(o1, 8, own(c0, 8) + jnp.concatenate(rows, axis=0))


VMEM = pl.BlockSpec(memory_space=pltpu.VMEM)
TILES = (2, 4, 4, 2, NZ, 16, 128)


def exchange(*operands):
    def cells(rows):
        return pltpu.VMEM((3, rows, 128), F32)

    return pl.pallas_call(
        compute_kernel,
        out_shape=[jax.ShapeDtypeStruct(g.shape, BF) for g in operands[4:8]],
        in_specs=[VMEM] * 16,
        out_specs=[VMEM] * 4,
        scratch_shapes=[
            pltpu.VMEM((2304, 768), BF),
            pltpu.VMEM((2304, 1280), BF),
            pltpu.VMEM((1152, 1024), BF),
            pltpu.VMEM((384, 1152), BF),
            pltpu.VMEM((384, 768), BF),
            pltpu.VMEM((384, 384), BF),
            pltpu.VMEM((2, 1024, 128), F32),
            cells(64), cells(48), cells(32), cells(32), cells(48), cells(32),
            cells(32), cells(32), cells(16), cells(16), cells(48), cells(32), cells(32), cells(48), cells(64),
        ],
        compiler_params=pltpu.CompilerParams(vmem_limit_bytes=56 * 2**20),
        name="exchange",
    )(*operands)


def per_device(g1, g2, g3, g4, p1, p2, p3, p4, m20, m30a, m30b, m31, block_params):
    raw = jnp.pad(block_params, (0, RAW_ROWS * 128 - SHARD)).reshape(RAW_ROWS, 128)
    halo_types = [jax.ShapeDtypeStruct((rows, CELL), BF) for rows in (48, 32, 32)]
    gathered = pl.pallas_call(
        gather_kernel,
        out_shape=[jax.ShapeDtypeStruct(TILES, BF)] + halo_types,
        in_specs=[VMEM] * 11,
        out_specs=[VMEM] * 4,
        scratch_shapes=[
            pltpu.VMEM((RAW_ROWS, 128), BF),
            pltpu.VMEM((RAW_ROWS, 128), BF),
            pltpu.VMEM((WINDOW, 128), F32),
            pltpu.VMEM((48, CELL), F32),
            pltpu.VMEM((32, CELL), F32),
            pltpu.VMEM((48, CELL), BF),
            pltpu.VMEM((32, CELL), BF),
            pltpu.SemaphoreType.DMA((5,)),
            pltpu.SemaphoreType.DMA((5,)),
            pltpu.SemaphoreType.DMA((NZ - 1,)),
            pltpu.SemaphoreType.DMA((NZ - 1,)),
            pltpu.SemaphoreType.DMA((72,)),
            pltpu.SemaphoreType.DMA((72,)),
        ],
        compiler_params=pltpu.CompilerParams(
            collective_id=0, has_side_effects=True, vmem_limit_bytes=32 * 2**20
        ),
        name="gather",
    )(raw, g2, g3, g4, p2, p3, p4, m20, m30a, m30b, m31)

    return exchange(*gathered, g1, g2, g3, g4, p1, p2, p3, p4, m20, m30a, m30b, m31)


def solution(mesh):
    maps = P("tile", "branch")
    return jax.shard_map(
        per_device, mesh=mesh, in_specs=(maps,) * 12 + (P("tile"),), out_specs=(maps,) * 4, check_vma=False
    )
```

```python
import jax
import jax.numpy as jnp
from jax import lax
from jax.experimental import pallas as pl
from jax.experimental.pallas import tpu as pltpu
from jax.sharding import PartitionSpec as P

BF = jnp.bfloat16
F32 = jnp.float32
MESH = pl.DeviceIdType.MESH
N_TILE = 128
N_BRANCH = 4
NZ = 16
SHARD = 13734
CELL = 384
RAW_ROWS = 112
BASE = 104
WINDOW = 464

ROW0 = {
    (0, 1, 0): 0,
    (0, 2, 0): 12,
    (0, 3, 0): 36,
    (1, 0, 0): 84,
    (1, 2, 0): 192,
    (1, 3, 0): 240,
    (2, 0, 0): 336,
    (2, 0, 1): 390,
    (2, 1, 0): 606,
    (2, 3, 0): 1038,
    (3, 0, 0): 1230,
    (3, 0, 1): 1284,
    (3, 0, 2): 1338,
    (3, 1, 0): 1770,
    (3, 1, 1): 1986,
    (3, 2, 0): 2850,
}


def remote(src, dst, send, recv, branch, tile):
    return pltpu.make_async_remote_copy(
        src_ref=src, dst_ref=dst, send_sem=send, recv_sem=recv, device_id=(branch, tile), device_id_type=MESH
    )


def tile_at(row_tile, jb):
    group, n = row_tile // 9, 3 * (row_tile % 9) + jb
    j, slot = n // 7, n % 7
    k = 4 * group + j
    return slot % 2, slot // 2, (k // 2) % 4, k % 2, k // 8


def dot(a, b):
    return lax.dot_general(a, b, (((1,), (0,)), ((), ())), preferred_element_type=F32)


def dot_nt(a, b):
    return lax.dot_general(a, b, (((1,), (1,)), ((), ())), preferred_element_type=F32)


def unit_matrix(rows, cols, target):
    column = lax.broadcasted_iota(jnp.int32, (1, cols), 1)
    row = lax.broadcasted_iota(jnp.int32, (rows, cols), 0)
    return jnp.where(row == target(column), 1.0, 0.0).astype(BF)


def exchange_kernel(
    *refs,
):
    inputs, outputs, refs = refs[:13], refs[13:17], refs[17:]
    loaded, refs = refs[:13], refs[13:]
    (
        tiles, row_in, col_in, corner_in, raw1, raw2, win, row_f, col_f, row_out, col_out,
        e3, e2, e1, u3, u2, u1, wide,
        c0, c1, c2, c3, sg1, sg2, q20, q30a, q30b, q31, k1, k2a, k2b, nxt, out,
        l_sem, h_send, h_recv, z_send, z_recv, s_send, s_recv,
    ) = refs
    g1, g2, g3, g4, p1, p2, p3, p4, m20, m30a, m30b, m31, raw = loaded
    o1, o2, o3, o4 = outputs
    b = lax.axis_index("branch")
    k = lax.axis_index("tile")
    z, y, c = k // 8, lax.rem(k // 2, 4), lax.rem(k, 2)
    has_row = k < N_TILE - 1
    has_col = b < N_BRANCH - 1

    loads = [pltpu.make_async_copy(inputs[n], loaded[n], l_sem.at[n]) for n in range(13)]
    for n in (12, 1, 2, 3, 5, 6, 7, 8, 9, 10, 11, 0, 4):
        loads[n].start()

    def tile_of(zz, yy, cc):
        return zz * 8 + yy * 2 + cc

    def wrap(value, count):
        return lax.rem(value + count, count)

    left, right = wrap(b - 1, N_BRANCH), wrap(b + 1, N_BRANCH)
    up1, up2 = wrap(k - 1, N_TILE), wrap(k - 2, N_TILE)
    down1, down2 = wrap(k + 1, N_TILE), wrap(k + 2, N_TILE)
    y_prev, y_next = wrap(y - 1, 4), wrap(y + 1, 4)

    partners = [
        (b, up1), (b, up2), (b, down1), (b, down2), (left, k), (right, k), (left, up1), (right, down1),
        (b, tile_of(z, y_prev, c)), (b, tile_of(z, y_next, c)), (b, tile_of(z, y, 1 - c)),
    ]
    barrier = pltpu.get_barrier_semaphore()
    for step in range(1, NZ):
        pl.semaphore_signal(
            barrier, inc=1, device_id=(b, tile_of(wrap(z + step, NZ), y, c)), device_id_type=MESH
        )
    for who in partners:
        pl.semaphore_signal(barrier, inc=1, device_id=who, device_id_type=MESH)

    for ref in (e3, e2, e1, c1, c2, c3, sg1, sg2, q20, q30a, q30b, q31, k1, k2a, k2b, nxt, win):
        ref[...] = jnp.zeros_like(ref)

    for load in loads:
        load.wait()
    row_f[...] = jnp.zeros_like(row_f)
    col_f[...] = jnp.zeros_like(col_f)
    at_row, at_col = 0, 0
    for g, p in ((g2, p2), (g3, p3), (g4, p4)):
        rows = g.shape[0]
        masked = jnp.where(p[...].astype(F32) > 0, g[...].astype(F32), 0.0)
        for cell in range(8):
            row_f[at_row + cell : at_row + cell + 1, :] = masked[0:1, CELL * cell : CELL * (cell + 1)]
        col_f[at_col : at_col + rows, :] = masked[:, 0:CELL]
        at_row, at_col = at_row + 8, at_col + rows
    for m, at_row, at_col in ((m20, 24, 8), (m30a, 28, 12), (m31, 32, 18), (m30b, 36, 16)):
        rows, units = m.shape[0], m.shape[1] // CELL
        value = m[...].astype(F32)
        for unit in range(units):
            row_f[at_row + unit : at_row + unit + 1, :] = value[0:1, CELL * unit : CELL * (unit + 1)]
        col_f[at_col : at_col + rows, :] = value[:, 0:CELL]
    row_out[...] = row_f[...].astype(BF)
    col_out[...] = col_f[...].astype(BF)


    pl.semaphore_wait(barrier, len(partners) + NZ - 1)
    first = [
        remote(raw, raw1, h_send.at[0], h_recv.at[0], b, up1),
        remote(raw, raw2, h_send.at[1], h_recv.at[1], b, up2),
        remote(row_out, row_in, h_send.at[2], h_recv.at[2], b, up1),
        remote(col_out, col_in, h_send.at[3], h_recv.at[3], left, k),
        remote(col_out, corner_in, h_send.at[4], h_recv.at[4], left, up1),
    ]
    for copy in first:
        copy.start()

    def put(buffer, row, value):
        rows = value.shape[0]
        for l in range(3):
            buffer[l, row : row + rows, :] = value[:, 128 * l : 128 * (l + 1)]

    def spread_units(buffer, value, units):
        rows = value.shape[0]
        for unit in range(units):
            for l in range(3):
                piece = value[:, CELL * unit + 128 * l : CELL * unit + 128 * (l + 1)]
                if rows == 1:
                    buffer[l, unit : unit + 1, :] = piece
                else:
                    buffer[l, pl.ds(unit, rows, stride=units), :] = piece

    def masked(g, p):
        return jnp.where(p[...].astype(F32) > 0, g[...].astype(F32), 0.0)

    spread_units(c0, masked(g1, p1), 8)
    for buffer, g, p in ((c1, g2, p2), (c2, g3, p3), (c3, g4, p4)):
        spread_units(buffer, masked(g, p), 8)
    for buffer, m, units in ((q20, m20, 4), (q30a, m30a, 4), (q31, m31, 4), (q30b, m30b, 2)):
        spread_units(buffer, m[...].astype(F32), units)

    group, j = k // 4, lax.rem(k, 4)
    first_tile = (7 * j) // 3
    delta = 13734 * j - 6144 * first_tile - 360 * group + BASE * 128
    lane = lax.broadcasted_iota(jnp.int32, (RAW_ROWS, 128), 1)
    for d, shard in enumerate((raw, raw1, raw2)):
        if d > 0:
            first[d - 1].wait_recv()
        start = delta + SHARD * d
        q, phase = start // 128, lax.rem(start, 128)
        rolled = pltpu.roll(shard[...].astype(F32), phase, 1)
        win[pl.ds(q, RAW_ROWS), :] += jnp.where(lane >= phase, rolled, 0.0)
        win[pl.ds(q + 1, RAW_ROWS), :] += jnp.where(lane >= phase, 0.0, rolled)
    for s in range(2):
        n = 7 * j + 2 * b + s
        row_tile = 9 * group + n // 3
        offset = jnp.where(row_tile >= 124, 2, 10)
        origin = BASE + 3 * (16 * (n // 3 - first_tile) + offset) + lax.rem(n, 3)
        tiles[s, b, y, c, z] = win[pl.ds(origin, 16, stride=3), :].astype(BF)

    copies = []
    own = tiles.at[:, b, y, c, z]
    for step in (8, 7, 9, 6, 10, 5, 11, 4, 12, 3, 13, 2, 14, 1, 15):
        copy = remote(
            own, own, z_send.at[step - 1], z_recv.at[step - 1], b, tile_of(wrap(z + step, NZ), y, c)
        )
        copy.start()
        copies.append(copy)

    for copy in first[2:]:
        copy.wait_recv()
    row_halo = row_in[...].astype(F32)
    col_halo = col_in[...].astype(F32)
    corner = corner_in[...].astype(F32)
    row_zero = jnp.where(has_row, row_halo, 0.0)
    col_zero = jnp.where(has_col, col_halo, 0.0)
    corner_zero = jnp.where(has_row & has_col, corner, 0.0)
    at = 0
    for buffer, rows, halo in ((c1, 4, 0), (c2, 2, 8), (c3, 1, 16)):
        put(buffer, 8 * rows, row_zero[halo : halo + 8])
        put(buffer, 8 * rows + 8, col_zero[at : at + rows])
        put(buffer, 8 * rows + 8 + rows, corner_zero[at : at + 1])
        at += rows
    for buffer, rows, units, halo, at in ((q20, 4, 4, 24, 8), (q30a, 4, 4, 28, 12), (q31, 2, 4, 32, 18), (q30b, 2, 2, 36, 16)):
        put(buffer, rows * units, row_halo[halo : halo + units])
        put(buffer, (rows + 1) * units, col_halo[at : at + rows])
        put(buffer, (rows + 1) * units + rows, corner[at : at + 1])

    def flags(buffer):
        whole = jnp.concatenate([buffer[l] for l in range(3)], axis=1)
        return jnp.where(whole > 0, 1.0, 0.0).astype(BF)

    def target20(shift):
        def target(col):
            part, lane = col // CELL, lax.rem(col, CELL)
            pixel, channel = lane // 96, lax.rem(lane, 96) - shift
            return jnp.where((channel >= 0) & (channel < 48), part * 192 + pixel * 48 + channel, -1)

        return target

    def target31(col):
        part, lane = col // CELL, lax.rem(col, CELL)
        return jnp.where(lane < 192, part * 192 + lane, -1)

    def target30b(col):
        part, lane = col // CELL, lax.rem(col, CELL) - 192
        return jnp.where((lane >= 0) & (lane < 96), part * 96 + lane, -1)

    def keep(buffer, value, parts, count, extra_from, extra_rows, extra_to):
        for l in range(3):
            for part in range(parts):
                lanes = slice(part * CELL + 128 * l, part * CELL + 128 * (l + 1))
                buffer[l, pl.ds(part, count, stride=parts), :] = value[0:count, lanes]
            buffer[l, extra_to : extra_to + extra_rows, :] = value[
                extra_from : extra_from + extra_rows, 128 * l : 128 * (l + 1)
            ]

    mask1 = dot(flags(q20), unit_matrix(CELL, 768, target20(0))) + dot(
        flags(q30a), unit_matrix(CELL, 768, target20(48))
    )
    keep(k1, mask1, 2, 20, 20, 5, 40)
    keep(k2a, dot(flags(q31), unit_matrix(CELL, 768, target31)), 2, 12, 12, 3, 24)
    keep(k2b, dot(flags(q30b), unit_matrix(CELL, 1536, target30b)), 4, 6, 6, 3, 24)

    def load_rows(row_tile, count):
        columns = [
            jnp.concatenate([tiles[tile_at(row_tile + t, jb)] for t in range(count)], axis=0) for jb in range(3)
        ]
        return jnp.concatenate(columns, axis=1)

    def rows_of(key, rows, j, at=0):
        n = CELL // j
        r0 = ROW0[key]
        row_tile, offset = (286, 0) if r0 == 0 else divmod(r0 - 10, 16)
        count = -(-(offset + rows) // 16)
        width = 256 if j == 192 else 128

        def target(col):
            part, lane = col // width, lax.rem(col, width) - at
            return jnp.where((lane >= 0) & (lane < j), part * j + lane, -1)

        split = dot(load_rows(row_tile, count), unit_matrix(CELL, n * width, target))
        parts = []
        for half in range(width // 128):
            for part in range(n):
                wide[half, pl.ds(part, 16 * count, stride=n), :] = split[
                    :, part * width + 128 * half : part * width + 128 * (half + 1)
                ]
            parts.append(wide[half, offset * n : (offset + rows) * n, :])
        return parts[0] if len(parts) == 1 else jnp.concatenate(parts, axis=1)

    def place(weights, j, low, high):
        rows = weights.shape[1]

        def target(col):
            which = col // j
            return jnp.where((which >= low) & (which < high), lax.rem(col, j), -1)

        return dot(weights, unit_matrix(rows, CELL, target))

    def taps(e, row0, pitch, weights, placed, seg, nxt_seg, nxt_width):
        count = len(placed)
        i = weights.shape[0] // 9

        def tap(value, a, bb):
            return value[(3 * a + bb) * i : (3 * a + bb + 1) * i]

        for a in range(3):
            for q in range(count):
                even = row0 + CELL * a + 2 * q * pitch
                e[even : even + i, seg : seg + CELL] = tap(placed[q], a, 1).astype(BF)
                odd = even + pitch
                value = tap(placed[q], a, 2)
                if q + 1 < count:
                    value = value + tap(placed[q + 1], a, 0)
                else:
                    e[odd : odd + i, nxt_seg : nxt_seg + nxt_width] = tap(weights, a, 0).astype(BF)
                e[odd : odd + i, seg : seg + CELL] = value.astype(BF)

    def fill_e3():
        for key, i, row0, pitch in (
            ((3, 2, 0), 192, 0, 192),
            ((3, 1, 1), 96, 1152, 96),
            ((3, 0, 2), 48, 1152 + 192, 48),
        ):
            r0 = ROW0[key]
            start = 124 + (r0 - 1986) // 16 if r0 >= 1986 else (r0 - 10) // 16
            for a in range(3):
                even = row0 + CELL * a
                odd = even + pitch
                for bb, at, seg in ((1, even, 0), (2, odd, 0), (0, odd, CELL)):
                    first = start + (3 * a + bb) * (i // 16)
                    for t in range(i // 16):
                        for jb in range(3):
                            e3[at + 16 * t : at + 16 * (t + 1), seg + 128 * jb : seg + 128 * (jb + 1)] = tiles[
                                tile_at(first + t, jb)
                            ]

    def fill_e2():
        w = rows_of((2, 1, 0), 432, 192)
        taps(e2, 0, 96, w, [place(w.astype(BF), 192, q, q + 1) for q in range(2)], 0, 768, 256)
        w = rows_of((3, 1, 0), 216, 96)
        taps(e2, 0, 96, w, [place(w.astype(BF), 96, q, q + 1) for q in range(2)], 384, 1024, 128)
        w = rows_of((2, 0, 1), 216, 192)
        placed = [place(w.astype(BF), 192, q, q + 1) for q in range(2)]
        taps(e2, 1152, 96, w, placed, 0, 768, 256)
        w = rows_of((3, 0, 1), 54, 48)
        w_next = rows_of((3, 0, 1), 54, 48, 64)
        placed = [place(w.astype(BF), 48, 4 + q, 5 + q) for q in range(2)]
        taps(e2, 1152 + 48, 96, w_next, placed, 384, 1024 + 128, 128)

    def fill_e1():
        w = rows_of((1, 0, 0), 108, 96)
        taps(e1, 0, 48, w, [place(w.astype(BF), 96, q, q + 1) for q in range(4)], 0, 768, 128)
        w = rows_of((2, 0, 0), 54, 48) + 0.0
        w = w + rows_of((3, 0, 0), 54, 48, 48)
        taps(e1, 0, 48, w, [place(w.astype(BF), 96, q, q + 1) for q in range(4)], 384, 896, 128)

    def fill_up():
        u3[:, 0:384] = place(rows_of((0, 3, 0), 48, 48).astype(BF), 48, 0, 8).astype(BF)
        u3[:, 384:768] = place(rows_of((1, 3, 0), 96, 96).astype(BF), 96, 0, 4).astype(BF)
        u3[:, 768:1152] = place(rows_of((2, 3, 0), 192, 192).astype(BF), 192, 0, 2).astype(BF)
        w02 = rows_of((0, 2, 0), 24, 48).astype(BF)
        w12 = rows_of((1, 2, 0), 48, 96).astype(BF)
        for q in range(2):
            u2[192 * q : 192 * (q + 1), 0:384] = place(w02, 48, 4 * q, 4 * q + 4).astype(BF)
            u2[192 * q : 192 * (q + 1), 384:768] = place(w12, 96, 2 * q, 2 * q + 2).astype(BF)
        w01 = rows_of((0, 1, 0), 12, 48).astype(BF)
        for q in range(4):
            u1[96 * q : 96 * (q + 1), :] = place(w01, 48, 2 * q, 2 * q + 2).astype(BF)

    for copy in copies:
        copy.wait_recv()

    class Half:
        def __init__(self, s, lo):
            self.s, self.lo = s, lo
            self.u, self.v = (b, y) if s == 0 else (y, b)
            self.pending, self.across = [], []
            self.used = 36 * (2 * s + lo // 8)

        def bundle(self, u, v, part):
            x_at, y_at = (u, v) if self.s == 0 else (v, u)
            ref = tiles.at[self.s, x_at, y_at, c]
            return ref.at[pl.ds(self.lo, 8)] if part is None else ref.at[pl.ds(self.lo + 4 * part, 4)]

        def send(self, u, v, part, to_u, to_v, other_core=False):
            x_to, y_to = (to_u, to_v) if self.s == 0 else (to_v, to_u)
            ref = self.bundle(u, v, part)
            copy = remote(
                ref, ref, s_send.at[self.used], s_recv.at[self.used], x_to,
                tile_of(z, y_to, 1 - c if other_core else c),
            )
            copy.start()
            self.used += 1
            self.pending.append(copy)
            if other_core:
                self.across.append(copy)
            return copy

        def first(self):
            u, v = self.u, self.v
            self.to_next = self.send(u, v, None, wrap(u + 1, 4), v)
            self.to_prev = self.send(u, v, None, wrap(u - 1, 4), v)
            self.second = [self.spread(u)]

        def spread(self, u_of):
            u, v = self.u, self.v
            to_next = self.send(u_of, v, None, u, wrap(v + 1, 4))
            to_prev = self.send(u_of, v, None, u, wrap(v - 1, 4))
            self.send(u_of, v, None, u, v, True)
            return u_of, to_next, to_prev

        def forward(self):
            u, v = self.u, self.v
            self.to_next.wait_recv()
            prev_u, next_u = wrap(u - 1, 4), wrap(u + 1, 4)
            self.far_next = self.send(prev_u, v, 0, next_u, v)
            self.second.append(self.spread(prev_u))
            self.to_prev.wait_recv()
            self.far_prev = self.send(next_u, v, 1, prev_u, v)
            self.second.append(self.spread(next_u))

        def far(self):
            self.far_next.wait_recv()
            self.far_prev.wait_recv()
            self.second.append(self.spread(wrap(self.u + 2, 4)))

        def finish(self, number):
            u, v = self.u, self.v
            u_of, to_next, to_prev = self.second[number]
            to_next.wait_recv()
            a = self.send(u_of, wrap(v - 1, 4), 0, u, wrap(v + 1, 4))
            self.send(u_of, wrap(v - 1, 4), None, u, v, True)
            to_prev.wait_recv()
            d = self.send(u_of, wrap(v + 1, 4), 1, u, wrap(v - 1, 4))
            self.send(u_of, wrap(v + 1, 4), None, u, v, True)
            return u_of, a, d

        def last(self, state):
            u_of, a, d = state
            a.wait_recv()
            d.wait_recv()
            self.send(u_of, wrap(self.v + 2, 4), None, self.u, self.v, True)

        def arrived(self):
            for copy in self.across:
                copy.wait_recv()

    near, far = [Half(0, 0), Half(1, 0)], [Half(0, 8), Half(1, 8)]
    for half in near + far:
        half.first()
    for half in near + far:
        half.forward()
    for half in near + far:
        half.far()

    def finish(part, numbers):
        return [(half, half.finish(number)) for number in numbers for half in part]

    near_states = finish(near, range(4))
    for half, state in near_states:
        half.last(state)
    far_states = finish(far, range(4))
    for half in near:
        half.arrived()
    fill_e2()
    for half, state in far_states:
        half.last(state)
    fill_e1()
    for half in far:
        half.arrived()
    fill_up()
    fill_e3()

    def lanes_of(buffer, count=3):
        return [buffer[l] for l in range(count)]

    def shifted(buffer, rows, count):
        total = buffer.shape[1]
        pieces = []
        for l in range(count):
            nxt[l, 0 : 8 * rows, :] = buffer[l, 1 : 8 * rows + 1, :]
            for p in range(rows):
                nxt[l, 8 * p + 7 : 8 * p + 8, :] = buffer[l, 8 * rows + p : 8 * rows + p + 1, :]
            nxt[l, 8 * rows : total, :] = jnp.zeros((total - 8 * rows, 128), F32)
            pieces.append(nxt[l, 0:total, :])
        return pieces

    def lhs(pieces):
        return jnp.concatenate([piece.astype(BF) for piece in pieces], axis=1)

    def rows_out(y, a, lo, hi, lane0):
        return y[lo:hi, lane0 + CELL * a : lane0 + CELL * (a + 1)]

    def upsampled(y, p, lane0):
        even = rows_out(y, 1, 8 * p, 8 * p + 8, lane0)
        odd = rows_out(y, 2, 8 * p, 8 * p + 8, lane0) + rows_out(y, 0, 8 * p + 8, 8 * p + 16, lane0)
        return even, odd

    def section(buffer, y, rows, kept):
        base = 8 * (rows + 1)
        for p in range(rows):
            even, odd = upsampled(y, p, 1152)
            put(buffer, 16 * p, even)
            put(buffer, 16 * p + 8, odd)
        put(buffer, 16 * rows, rows_out(y, 1, 8 * rows, 8 * rows + 8, 1152))
        extra = 8 * (2 * rows + 1)
        for p in range(rows + 1):
            put(buffer, extra + 2 * p, rows_out(y, 1, base + p, base + p + 1, 1152))
            if p < rows:
                odd = rows_out(y, 2, base + p, base + p + 1, 1152) + rows_out(y, 0, base + p + 1, base + p + 2, 1152)
                put(buffer, extra + 2 * p + 1, odd)
        for l in range(3):
            buffer[l] = jnp.where(kept(l) > 0.5, buffer[l], 0.0)

    def emit(ref, rows, value):
        put(out, 0, value)
        for cell in range(8):
            for l in range(3):
                lane0 = CELL * cell + 128 * l
                if rows == 1:
                    piece = out[l, cell : cell + 1, :]
                else:
                    piece = out[l, pl.ds(cell, rows, stride=8), :]
                ref[:, lane0 : lane0 + 128] = piece.astype(BF)

    def block_sums(buffer, rows, factor):
        groups = []
        for first in range(0, rows, factor):
            pieces = []
            for l in range(3):
                total = buffer[l, 8 * first : 8 * first + 8, :]
                for p in range(first + 1, first + factor):
                    total = total + buffer[l, 8 * p : 8 * p + 8, :]
                pieces.append(total)
            groups.append(jnp.concatenate(pieces, axis=1))
        return jnp.concatenate(groups, axis=0).astype(BF)

    def own(buffer, rows):
        return jnp.concatenate([buffer[l, 0 : 8 * rows, :] for l in range(3)], axis=1)

    up = jnp.concatenate([block_sums(c0, 8, 8), block_sums(c1, 4, 4), block_sums(c2, 2, 2)], axis=1)
    emit(o4, 1, own(c3, 1) + dot_nt(up, u3[...]))

    y3 = dot_nt(lhs(lanes_of(c3) + shifted(c3, 2, 3)), e3[...])
    up = jnp.concatenate([block_sums(c0, 8, 4), block_sums(c1, 4, 2)], axis=1)
    down = jnp.concatenate(upsampled(y3, 0, 0), axis=0)
    emit(o3, 2, own(c2, 2) + dot_nt(up, u2[...]) + down)

    section(sg2, y3, 1, lambda l: k2a[l] + k2b[l])
    y2 = dot_nt(lhs(lanes_of(c2) + lanes_of(sg2) + shifted(c2, 3, 2) + shifted(sg2, 3, 2)), e2[...])
    down = jnp.concatenate(upsampled(y2, 0, 0) + upsampled(y2, 1, 0), axis=0)
    emit(o2, 4, own(c1, 4) + dot_nt(block_sums(c0, 8, 2), u1[...]) + down)

    section(sg1, y2, 2, lambda l: k1[l])
    y1 = dot_nt(lhs(lanes_of(c1) + lanes_of(sg1) + shifted(c1, 5, 1) + shifted(sg1, 5, 1)), e1[...])
    rows = []
    for p in range(4):
        rows.extend(upsampled(y1, p, 0))
    emit(o1, 8, own(c0, 8) + jnp.concatenate(rows, axis=0))

    for half in near + far:
        for copy in half.pending:
            copy.wait_send()
    for copy in copies + first:
        copy.wait_send()


def finish_kernel(*refs):
    sems = refs[8]
    copies = [pltpu.make_async_copy(refs[n], refs[4 + n], sems.at[n]) for n in range(4)]
    for copy in copies:
        copy.start()
    for copy in copies:
        copy.wait()


ANY = pl.BlockSpec(memory_space=pl.ANY)
VMEM = pl.BlockSpec(memory_space=pltpu.VMEM)
TILES = (2, 4, 4, 2, NZ, 16, 128)


def per_device(*operands):
    maps = operands[:12]
    raw = jnp.pad(operands[12], (0, RAW_ROWS * 128 - SHARD)).reshape(RAW_ROWS, 128)

    def cells(rows):
        return pltpu.VMEM((3, rows, 128), F32)

    def buffer(*shape):
        return pltpu.VMEM(shape, BF)

    def sems(count):
        return pltpu.SemaphoreType.DMA((count,))

    results = [jax.ShapeDtypeStruct(g.shape, BF) for g in maps[:4]]
    done = pl.pallas_call(
        exchange_kernel,
        out_shape=results,
        in_specs=[ANY] * 13,
        out_specs=[VMEM] * 4,
        scratch_shapes=[buffer(*m.shape) for m in maps] + [
            buffer(RAW_ROWS, 128),
            buffer(*TILES), buffer(48, CELL), buffer(32, CELL), buffer(32, CELL),
            buffer(RAW_ROWS, 128), buffer(RAW_ROWS, 128), pltpu.VMEM((WINDOW, 128), F32),
            pltpu.VMEM((48, CELL), F32), pltpu.VMEM((32, CELL), F32), buffer(48, CELL), buffer(32, CELL),
            buffer(2304, 768), buffer(2304, 1280), buffer(1152, 1024),
            buffer(384, 1152), buffer(384, 768), buffer(384, 384),
            pltpu.VMEM((2, 1024, 128), F32),
            cells(64), cells(48), cells(32), cells(32), cells(48), cells(32),
            cells(32), cells(32), cells(16), cells(16), cells(48), cells(32), cells(32), cells(48), cells(64),
            sems(13), sems(5), sems(5), sems(NZ - 1), sems(NZ - 1), sems(144), sems(144),
        ],
        compiler_params=pltpu.CompilerParams(
            collective_id=0, has_side_effects=True, vmem_limit_bytes=60 * 2**20
        ),
        name="exchange",
    )(*maps, raw)
    return pl.pallas_call(
        finish_kernel,
        out_shape=results,
        in_specs=[ANY] * 4,
        out_specs=[ANY] * 4,
        scratch_shapes=[sems(4)],
        compiler_params=pltpu.CompilerParams(vmem_limit_bytes=60 * 2**20),
        name="finish",
    )(*done)


def solution(mesh):
    maps = P("tile", "branch")
    return jax.shard_map(
        per_device, mesh=mesh, in_specs=(maps,) * 12 + (P("tile"),), out_specs=(maps,) * 4, check_vma=False
    )
```

```python
import jax
import jax.numpy as jnp
from jax import lax
from jax.experimental import pallas as pl
from jax.experimental.pallas import tpu as pltpu
from jax.sharding import PartitionSpec as P

BF = jnp.bfloat16
F32 = jnp.float32
MESH = pl.DeviceIdType.MESH
N_TILE = 128
N_BRANCH = 4
NZ = 16
SHARD = 13734
CELL = 384
RAW_ROWS = 112
BASE = 104
WINDOW = 464

ROW0 = {
    (0, 1, 0): 0,
    (0, 2, 0): 12,
    (0, 3, 0): 36,
    (1, 0, 0): 84,
    (1, 2, 0): 192,
    (1, 3, 0): 240,
    (2, 0, 0): 336,
    (2, 0, 1): 390,
    (2, 1, 0): 606,
    (2, 3, 0): 1038,
    (3, 0, 0): 1230,
    (3, 0, 1): 1284,
    (3, 0, 2): 1338,
    (3, 1, 0): 1770,
    (3, 1, 1): 1986,
    (3, 2, 0): 2850,
}


def remote(src, dst, send, recv, branch, tile):
    return pltpu.make_async_remote_copy(
        src_ref=src, dst_ref=dst, send_sem=send, recv_sem=recv, device_id=(branch, tile), device_id_type=MESH
    )


def tile_at(row_tile, jb):
    group, n = row_tile // 9, 3 * (row_tile % 9) + jb
    j, slot = n // 7, n % 7
    k = 4 * group + j
    return slot % 2, slot // 2, (k // 2) % 4, k % 2, k // 8


def dot(a, b):
    return lax.dot_general(a, b, (((1,), (0,)), ((), ())), preferred_element_type=F32)


def dot_nt(a, b):
    return lax.dot_general(a, b, (((1,), (1,)), ((), ())), preferred_element_type=F32)


def unit_matrix(rows, cols, target):
    column = lax.broadcasted_iota(jnp.int32, (1, cols), 1)
    row = lax.broadcasted_iota(jnp.int32, (rows, cols), 0)
    return jnp.where(row == target(column), 1.0, 0.0).astype(BF)


def exchange_kernel(
    *refs,
):
    inputs, outputs, refs = refs[:13], refs[13:17], refs[17:]
    loaded, refs = refs[:13], refs[13:]
    (
        tiles, row_in, col_in, corner_in, raw1, raw2, win, row_f, col_f, row_out, col_out,
        e3, e2, e1, u3, u2, u1, wide,
        c0, c1, c2, c3, sg1, sg2, q20, q30a, q30b, q31, k1, k2a, k2b, nxt, out,
        l_sem, h_send, h_recv, z_send, z_recv, s_send, s_recv,
    ) = refs
    g1, g2, g3, g4, p1, p2, p3, p4, m20, m30a, m30b, m31, raw = loaded
    o1, o2, o3, o4 = outputs
    b = lax.axis_index("branch")
    k = lax.axis_index("tile")
    z, y, c = k // 8, lax.rem(k // 2, 4), lax.rem(k, 2)
    has_row = k < N_TILE - 1
    has_col = b < N_BRANCH - 1

    loads = [pltpu.make_async_copy(inputs[n], loaded[n], l_sem.at[n]) for n in range(13)]
    for n in (12, 1, 2, 3, 5, 6, 7, 8, 9, 10, 11, 0, 4):
        loads[n].start()

    def tile_of(zz, yy, cc):
        return zz * 8 + yy * 2 + cc

    def wrap(value, count):
        return lax.rem(value + count, count)

    left, right = wrap(b - 1, N_BRANCH), wrap(b + 1, N_BRANCH)
    up1, up2 = wrap(k - 1, N_TILE), wrap(k - 2, N_TILE)
    down1, down2 = wrap(k + 1, N_TILE), wrap(k + 2, N_TILE)
    y_prev, y_next = wrap(y - 1, 4), wrap(y + 1, 4)

    partners = [
        (b, up1), (b, up2), (b, down1), (b, down2), (left, k), (right, k), (left, up1), (right, down1),
        (b, tile_of(z, y_prev, c)), (b, tile_of(z, y_next, c)), (b, tile_of(z, y, 1 - c)),
    ]
    barrier = pltpu.get_barrier_semaphore()
    for step in range(1, NZ):
        pl.semaphore_signal(
            barrier, inc=1, device_id=(b, tile_of(wrap(z + step, NZ), y, c)), device_id_type=MESH
        )
    for who in partners:
        pl.semaphore_signal(barrier, inc=1, device_id=who, device_id_type=MESH)

    for ref in (e3, e2, e1, c1, c2, c3, sg1, sg2, q20, q30a, q30b, q31, k1, k2a, k2b, nxt, win):
        ref[...] = jnp.zeros_like(ref)

    for load in loads:
        load.wait()
    row_f[...] = jnp.zeros_like(row_f)
    col_f[...] = jnp.zeros_like(col_f)
    at_row, at_col = 0, 0
    for g, p in ((g2, p2), (g3, p3), (g4, p4)):
        rows = g.shape[0]
        masked = jnp.where(p[...].astype(F32) > 0, g[...].astype(F32), 0.0)
        for cell in range(8):
            row_f[at_row + cell : at_row + cell + 1, :] = masked[0:1, CELL * cell : CELL * (cell + 1)]
        col_f[at_col : at_col + rows, :] = masked[:, 0:CELL]
        at_row, at_col = at_row + 8, at_col + rows
    for m, at_row, at_col in ((m20, 24, 8), (m30a, 28, 12), (m31, 32, 18), (m30b, 36, 16)):
        rows, units = m.shape[0], m.shape[1] // CELL
        value = m[...].astype(F32)
        for unit in range(units):
            row_f[at_row + unit : at_row + unit + 1, :] = value[0:1, CELL * unit : CELL * (unit + 1)]
        col_f[at_col : at_col + rows, :] = value[:, 0:CELL]
    row_out[...] = row_f[...].astype(BF)
    col_out[...] = col_f[...].astype(BF)


    pl.semaphore_wait(barrier, len(partners) + NZ - 1)
    first = [
        remote(raw, raw1, h_send.at[0], h_recv.at[0], b, up1),
        remote(raw, raw2, h_send.at[1], h_recv.at[1], b, up2),
        remote(row_out, row_in, h_send.at[2], h_recv.at[2], b, up1),
        remote(col_out, col_in, h_send.at[3], h_recv.at[3], left, k),
        remote(col_out, corner_in, h_send.at[4], h_recv.at[4], left, up1),
    ]
    for copy in first:
        copy.start()

    def put(buffer, row, value):
        rows = value.shape[0]
        for l in range(3):
            buffer[l, row : row + rows, :] = value[:, 128 * l : 128 * (l + 1)]

    def spread_units(buffer, value, units):
        rows = value.shape[0]
        for unit in range(units):
            for l in range(3):
                piece = value[:, CELL * unit + 128 * l : CELL * unit + 128 * (l + 1)]
                if rows == 1:
                    buffer[l, unit : unit + 1, :] = piece
                else:
                    buffer[l, pl.ds(unit, rows, stride=units), :] = piece

    def masked(g, p):
        return jnp.where(p[...].astype(F32) > 0, g[...].astype(F32), 0.0)

    spread_units(c0, masked(g1, p1), 8)
    for buffer, g, p in ((c1, g2, p2), (c2, g3, p3), (c3, g4, p4)):
        spread_units(buffer, masked(g, p), 8)
    for buffer, m, units in ((q20, m20, 4), (q30a, m30a, 4), (q31, m31, 4), (q30b, m30b, 2)):
        spread_units(buffer, m[...].astype(F32), units)

    group, j = k // 4, lax.rem(k, 4)
    first_tile = (7 * j) // 3
    delta = 13734 * j - 6144 * first_tile - 360 * group + BASE * 128
    lane = lax.broadcasted_iota(jnp.int32, (RAW_ROWS, 128), 1)
    for d, shard in enumerate((raw, raw1, raw2)):
        if d > 0:
            first[d - 1].wait_recv()
        start = delta + SHARD * d
        q, phase = start // 128, lax.rem(start, 128)
        rolled = pltpu.roll(shard[...].astype(F32), phase, 1)
        win[pl.ds(q, RAW_ROWS), :] += jnp.where(lane >= phase, rolled, 0.0)
        win[pl.ds(q + 1, RAW_ROWS), :] += jnp.where(lane >= phase, 0.0, rolled)
    for s in range(2):
        n = 7 * j + 2 * b + s
        row_tile = 9 * group + n // 3
        offset = jnp.where(row_tile >= 124, 2, 10)
        origin = BASE + 3 * (16 * (n // 3 - first_tile) + offset) + lax.rem(n, 3)
        tiles[s, b, y, c, z] = win[pl.ds(origin, 16, stride=3), :].astype(BF)

    copies = []
    own = tiles.at[:, b, y, c, z]
    for step in (8, 7, 9, 6, 10, 5, 11, 4, 12, 3, 13, 2, 14, 1, 15):
        copy = remote(
            own, own, z_send.at[step - 1], z_recv.at[step - 1], b, tile_of(wrap(z + step, NZ), y, c)
        )
        copy.start()
        copies.append(copy)

    for copy in first[2:]:
        copy.wait_recv()
    row_halo = row_in[...].astype(F32)
    col_halo = col_in[...].astype(F32)
    corner = corner_in[...].astype(F32)
    row_zero = jnp.where(has_row, row_halo, 0.0)
    col_zero = jnp.where(has_col, col_halo, 0.0)
    corner_zero = jnp.where(has_row & has_col, corner, 0.0)
    at = 0
    for buffer, rows, halo in ((c1, 4, 0), (c2, 2, 8), (c3, 1, 16)):
        put(buffer, 8 * rows, row_zero[halo : halo + 8])
        put(buffer, 8 * rows + 8, col_zero[at : at + rows])
        put(buffer, 8 * rows + 8 + rows, corner_zero[at : at + 1])
        at += rows
    for buffer, rows, units, halo, at in ((q20, 4, 4, 24, 8), (q30a, 4, 4, 28, 12), (q31, 2, 4, 32, 18), (q30b, 2, 2, 36, 16)):
        put(buffer, rows * units, row_halo[halo : halo + units])
        put(buffer, (rows + 1) * units, col_halo[at : at + rows])
        put(buffer, (rows + 1) * units + rows, corner[at : at + 1])

    def flags(buffer):
        whole = jnp.concatenate([buffer[l] for l in range(3)], axis=1)
        return jnp.where(whole > 0, 1.0, 0.0).astype(BF)

    def target20(shift):
        def target(col):
            part, lane = col // CELL, lax.rem(col, CELL)
            pixel, channel = lane // 96, lax.rem(lane, 96) - shift
            return jnp.where((channel >= 0) & (channel < 48), part * 192 + pixel * 48 + channel, -1)

        return target

    def target31(col):
        part, lane = col // CELL, lax.rem(col, CELL)
        return jnp.where(lane < 192, part * 192 + lane, -1)

    def target30b(col):
        part, lane = col // CELL, lax.rem(col, CELL) - 192
        return jnp.where((lane >= 0) & (lane < 96), part * 96 + lane, -1)

    def keep(buffer, value, parts, count, extra_from, extra_rows, extra_to):
        for l in range(3):
            for part in range(parts):
                lanes = slice(part * CELL + 128 * l, part * CELL + 128 * (l + 1))
                buffer[l, pl.ds(part, count, stride=parts), :] = value[0:count, lanes]
            buffer[l, extra_to : extra_to + extra_rows, :] = value[
                extra_from : extra_from + extra_rows, 128 * l : 128 * (l + 1)
            ]

    mask1 = dot(flags(q20), unit_matrix(CELL, 768, target20(0))) + dot(
        flags(q30a), unit_matrix(CELL, 768, target20(48))
    )
    keep(k1, mask1, 2, 20, 20, 5, 40)
    keep(k2a, dot(flags(q31), unit_matrix(CELL, 768, target31)), 2, 12, 12, 3, 24)
    keep(k2b, dot(flags(q30b), unit_matrix(CELL, 1536, target30b)), 4, 6, 6, 3, 24)

    def load_rows(row_tile, count):
        columns = [
            jnp.concatenate([tiles[tile_at(row_tile + t, jb)] for t in range(count)], axis=0) for jb in range(3)
        ]
        return jnp.concatenate(columns, axis=1)

    def rows_of(key, rows, j, at=0):
        n = CELL // j
        r0 = ROW0[key]
        row_tile, offset = (286, 0) if r0 == 0 else divmod(r0 - 10, 16)
        count = -(-(offset + rows) // 16)
        width = 256 if j == 192 else 128

        def target(col):
            part, lane = col // width, lax.rem(col, width) - at
            return jnp.where((lane >= 0) & (lane < j), part * j + lane, -1)

        split = dot(load_rows(row_tile, count), unit_matrix(CELL, n * width, target))
        parts = []
        for half in range(width // 128):
            for part in range(n):
                wide[half, pl.ds(part, 16 * count, stride=n), :] = split[
                    :, part * width + 128 * half : part * width + 128 * (half + 1)
                ]
            parts.append(wide[half, offset * n : (offset + rows) * n, :])
        return parts[0] if len(parts) == 1 else jnp.concatenate(parts, axis=1)

    def place(weights, j, low, high):
        rows = weights.shape[1]

        def target(col):
            which = col // j
            return jnp.where((which >= low) & (which < high), lax.rem(col, j), -1)

        return dot(weights, unit_matrix(rows, CELL, target))

    def taps(e, row0, pitch, weights, placed, seg, nxt_seg, nxt_width):
        count = len(placed)
        i = weights.shape[0] // 9

        def tap(value, a, bb):
            return value[(3 * a + bb) * i : (3 * a + bb + 1) * i]

        for a in range(3):
            for q in range(count):
                even = row0 + CELL * a + 2 * q * pitch
                e[even : even + i, seg : seg + CELL] = tap(placed[q], a, 1).astype(BF)
                odd = even + pitch
                value = tap(placed[q], a, 2)
                if q + 1 < count:
                    value = value + tap(placed[q + 1], a, 0)
                else:
                    e[odd : odd + i, nxt_seg : nxt_seg + nxt_width] = tap(weights, a, 0).astype(BF)
                e[odd : odd + i, seg : seg + CELL] = value.astype(BF)

    def fill_e3():
        for key, i, row0, pitch in (
            ((3, 2, 0), 192, 0, 192),
            ((3, 1, 1), 96, 1152, 96),
            ((3, 0, 2), 48, 1152 + 192, 48),
        ):
            r0 = ROW0[key]
            start = 124 + (r0 - 1986) // 16 if r0 >= 1986 else (r0 - 10) // 16
            for a in range(3):
                even = row0 + CELL * a
                odd = even + pitch
                for bb, at, seg in ((1, even, 0), (2, odd, 0), (0, odd, CELL)):
                    first = start + (3 * a + bb) * (i // 16)
                    for t in range(i // 16):
                        for jb in range(3):
                            e3[at + 16 * t : at + 16 * (t + 1), seg + 128 * jb : seg + 128 * (jb + 1)] = tiles[
                                tile_at(first + t, jb)
                            ]

    def fill_e2_21():
        w = rows_of((2, 1, 0), 432, 192)
        taps(e2, 0, 96, w, [place(w.astype(BF), 192, q, q + 1) for q in range(2)], 0, 384, 256)

    def fill_e2_31():
        w = rows_of((3, 1, 0), 216, 96)
        taps(e2, 0, 96, w, [place(w.astype(BF), 96, q, q + 1) for q in range(2)], 640, 1024, 128)

    def fill_e2_mid():
        w = rows_of((2, 0, 1), 216, 192)
        placed = [place(w.astype(BF), 192, q, q + 1) for q in range(2)]
        taps(e2, 1152, 96, w, placed, 0, 384, 256)
        w = rows_of((3, 0, 1), 54, 48)
        w_next = rows_of((3, 0, 1), 54, 48, 64)
        placed = [place(w.astype(BF), 48, 4 + q, 5 + q) for q in range(2)]
        taps(e2, 1152 + 48, 96, w_next, placed, 640, 1024 + 128, 128)

    def fill_e1_10():
        w = rows_of((1, 0, 0), 108, 96)
        taps(e1, 0, 48, w, [place(w.astype(BF), 96, q, q + 1) for q in range(4)], 0, 384, 128)

    def fill_e1_mid():
        w = rows_of((2, 0, 0), 54, 48) + 0.0
        w = w + rows_of((3, 0, 0), 54, 48, 48)
        taps(e1, 0, 48, w, [place(w.astype(BF), 96, q, q + 1) for q in range(4)], 512, 896, 128)

    def fill_up():
        u3[:, 0:384] = place(rows_of((0, 3, 0), 48, 48).astype(BF), 48, 0, 8).astype(BF)
        u3[:, 384:768] = place(rows_of((1, 3, 0), 96, 96).astype(BF), 96, 0, 4).astype(BF)
        u3[:, 768:1152] = place(rows_of((2, 3, 0), 192, 192).astype(BF), 192, 0, 2).astype(BF)
        w02 = rows_of((0, 2, 0), 24, 48).astype(BF)
        w12 = rows_of((1, 2, 0), 48, 96).astype(BF)
        for q in range(2):
            u2[192 * q : 192 * (q + 1), 0:384] = place(w02, 48, 4 * q, 4 * q + 4).astype(BF)
            u2[192 * q : 192 * (q + 1), 384:768] = place(w12, 96, 2 * q, 2 * q + 2).astype(BF)
        w01 = rows_of((0, 1, 0), 12, 48).astype(BF)
        for q in range(4):
            u1[96 * q : 96 * (q + 1), :] = place(w01, 48, 2 * q, 2 * q + 2).astype(BF)

    def lanes_of(buffer, count=3):
        return [buffer[l] for l in range(count)]

    def shifted(buffer, rows, count):
        total = buffer.shape[1]
        pieces = []
        for l in range(count):
            nxt[l, 0 : 8 * rows, :] = buffer[l, 1 : 8 * rows + 1, :]
            for p in range(rows):
                nxt[l, 8 * p + 7 : 8 * p + 8, :] = buffer[l, 8 * rows + p : 8 * rows + p + 1, :]
            nxt[l, 8 * rows : total, :] = jnp.zeros((total - 8 * rows, 128), F32)
            pieces.append(nxt[l, 0:total, :])
        return pieces

    def lhs(pieces):
        return jnp.concatenate([piece.astype(BF) for piece in pieces], axis=1)

    def rows_out(y, a, lo, hi, lane0):
        return y[lo:hi, lane0 + CELL * a : lane0 + CELL * (a + 1)]

    def upsampled(y, p, lane0):
        even = rows_out(y, 1, 8 * p, 8 * p + 8, lane0)
        odd = rows_out(y, 2, 8 * p, 8 * p + 8, lane0) + rows_out(y, 0, 8 * p + 8, 8 * p + 16, lane0)
        return even, odd

    def section(buffer, y, rows, kept):
        base = 8 * (rows + 1)
        for p in range(rows):
            even, odd = upsampled(y, p, 1152)
            put(buffer, 16 * p, even)
            put(buffer, 16 * p + 8, odd)
        put(buffer, 16 * rows, rows_out(y, 1, 8 * rows, 8 * rows + 8, 1152))
        extra = 8 * (2 * rows + 1)
        for p in range(rows + 1):
            put(buffer, extra + 2 * p, rows_out(y, 1, base + p, base + p + 1, 1152))
            if p < rows:
                odd = rows_out(y, 2, base + p, base + p + 1, 1152) + rows_out(y, 0, base + p + 1, base + p + 2, 1152)
                put(buffer, extra + 2 * p + 1, odd)
        for l in range(3):
            buffer[l] = jnp.where(kept(l) > 0.5, buffer[l], 0.0)

    def emit(ref, rows, value):
        put(out, 0, value)
        for cell in range(8):
            for l in range(3):
                lane0 = CELL * cell + 128 * l
                if rows == 1:
                    piece = out[l, cell : cell + 1, :]
                else:
                    piece = out[l, pl.ds(cell, rows, stride=8), :]
                ref[:, lane0 : lane0 + 128] = piece.astype(BF)

    def block_sums(buffer, rows, factor):
        groups = []
        for first in range(0, rows, factor):
            pieces = []
            for l in range(3):
                total = buffer[l, 8 * first : 8 * first + 8, :]
                for p in range(first + 1, first + factor):
                    total = total + buffer[l, 8 * p : 8 * p + 8, :]
                pieces.append(total)
            groups.append(jnp.concatenate(pieces, axis=1))
        return jnp.concatenate(groups, axis=0).astype(BF)

    def own(buffer, rows):
        return jnp.concatenate([buffer[l, 0 : 8 * rows, :] for l in range(3)], axis=1)

    for copy in copies:
        copy.wait_recv()

    class Half:
        def __init__(self, s, lo):
            self.s, self.lo = s, lo
            self.u, self.v = (b, y) if s == 0 else (y, b)
            self.pending, self.across = [], []
            self.used = 24 * (2 * s + lo // 8)

        def bundle(self, u, v, part):
            x_at, y_at = (u, v) if self.s == 0 else (v, u)
            ref = tiles.at[self.s, x_at, y_at, c]
            return ref.at[pl.ds(self.lo, 8)] if part is None else ref.at[pl.ds(self.lo + 4 * part, 4)]

        def send(self, u, v, part, to_u, to_v):
            x_to, y_to = (to_u, to_v) if self.s == 0 else (to_v, to_u)
            ref = self.bundle(u, v, part)
            copy = remote(
                ref, ref, s_send.at[self.used], s_recv.at[self.used], x_to,
                tile_of(z, y_to, c),
            )
            copy.start()
            self.used += 1
            self.pending.append(copy)
            return copy

        def first(self):
            u, v = self.u, self.v
            self.to_next = self.send(u, v, None, wrap(u + 1, 4), v)
            self.to_prev = self.send(u, v, None, wrap(u - 1, 4), v)
            self.second = [self.spread(u)]

        def spread(self, u_of):
            u, v = self.u, self.v
            to_next = self.send(u_of, v, None, u, wrap(v + 1, 4))
            to_prev = self.send(u_of, v, None, u, wrap(v - 1, 4))
            return u_of, to_next, to_prev

        def forward(self):
            u, v = self.u, self.v
            self.to_next.wait_recv()
            prev_u, next_u = wrap(u - 1, 4), wrap(u + 1, 4)
            self.far_next = self.send(prev_u, v, 0, next_u, v)
            self.second.append(self.spread(prev_u))
            self.to_prev.wait_recv()
            self.far_prev = self.send(next_u, v, 1, prev_u, v)
            self.second.append(self.spread(next_u))

        def far(self):
            self.far_next.wait_recv()
            self.far_prev.wait_recv()
            self.second.append(self.spread(wrap(self.u + 2, 4)))

        def finish(self, number):
            u, v = self.u, self.v
            u_of, to_next, to_prev = self.second[number]
            to_next.wait_recv()
            a = self.send(u_of, wrap(v - 1, 4), 0, u, wrap(v + 1, 4))
            to_prev.wait_recv()
            d = self.send(u_of, wrap(v + 1, 4), 1, u, wrap(v - 1, 4))
            return u_of, a, d

        def last(self, state):
            u_of, a, d = state
            a.wait_recv()
            d.wait_recv()
            zs = pl.ds(self.lo, 8)
            ref = tiles.at[0, u_of, :, c, zs] if self.s == 0 else tiles.at[1, :, u_of, c, zs]
            copy = remote(
                ref, ref, s_send.at[self.used], s_recv.at[self.used], b, tile_of(z, y, 1 - c)
            )
            copy.start()
            self.used += 1
            self.pending.append(copy)
            self.across.append(copy)

        def arrived(self):
            for copy in self.across:
                copy.wait_recv()

    near, far = [Half(0, 0), Half(1, 0)], [Half(0, 8), Half(1, 8)]
    for half in near + far:
        half.first()
    for half in near + far:
        half.forward()
    for half in near + far:
        half.far()

    def finish(part, numbers):
        return [(half, half.finish(number)) for number in numbers for half in part]

    near_states = finish(near, range(4))
    for half, state in near_states:
        half.last(state)
    far_states = finish(far, (0, 1))
    for half in near:
        half.arrived()
    fill_e2_21()
    far_states += finish(far, (2,))
    fill_e2_31()
    far_states += finish(far, (3,))
    fill_e2_mid()
    for half, state in far_states:
        half.last(state)
    fill_e1_10()
    fill_e1_mid()
    y2 = dot_nt(lhs(lanes_of(c2) + shifted(c2, 3, 2)), e2[:, 0:640])
    y1 = dot_nt(lhs(lanes_of(c1) + shifted(c1, 5, 1)), e1[:, 0:512])
    for half in far:
        half.arrived()
    fill_up()
    fill_e3()

    up = jnp.concatenate([block_sums(c0, 8, 8), block_sums(c1, 4, 4), block_sums(c2, 2, 2)], axis=1)
    emit(o4, 1, own(c3, 1) + dot_nt(up, u3[...]))

    y3 = dot_nt(lhs(lanes_of(c3) + shifted(c3, 2, 3)), e3[...])
    up = jnp.concatenate([block_sums(c0, 8, 4), block_sums(c1, 4, 2)], axis=1)
    down = jnp.concatenate(upsampled(y3, 0, 0), axis=0)
    emit(o3, 2, own(c2, 2) + dot_nt(up, u2[...]) + down)

    section(sg2, y3, 1, lambda l: k2a[l] + k2b[l])
    y2 = y2 + dot_nt(lhs(lanes_of(sg2) + shifted(sg2, 3, 2)), e2[:, 640:1280])
    down = jnp.concatenate(upsampled(y2, 0, 0) + upsampled(y2, 1, 0), axis=0)
    emit(o2, 4, own(c1, 4) + dot_nt(block_sums(c0, 8, 2), u1[...]) + down)

    section(sg1, y2, 2, lambda l: k1[l])
    y1 = y1 + dot_nt(lhs(lanes_of(sg1) + shifted(sg1, 5, 1)), e1[:, 512:1024])
    rows = []
    for p in range(4):
        rows.extend(upsampled(y1, p, 0))
    emit(o1, 8, own(c0, 8) + jnp.concatenate(rows, axis=0))

    for half in near + far:
        for copy in half.pending:
            copy.wait_send()
    for copy in copies + first:
        copy.wait_send()


def finish_kernel(*refs):
    for n in range(4):
        refs[4 + n][...] = refs[n][...]


ANY = pl.BlockSpec(memory_space=pl.ANY)
VMEM = pl.BlockSpec(memory_space=pltpu.VMEM)
TILES = (2, 4, 4, 2, NZ, 16, 128)


def per_device(*operands):
    maps = operands[:12]
    raw = jnp.pad(operands[12], (0, RAW_ROWS * 128 - SHARD)).reshape(RAW_ROWS, 128)

    def cells(rows):
        return pltpu.VMEM((3, rows, 128), F32)

    def buffer(*shape):
        return pltpu.VMEM(shape, BF)

    def sems(count):
        return pltpu.SemaphoreType.DMA((count,))

    results = [jax.ShapeDtypeStruct(g.shape, BF) for g in maps[:4]]
    done = pl.pallas_call(
        exchange_kernel,
        out_shape=results,
        in_specs=[ANY] * 13,
        out_specs=[VMEM] * 4,
        scratch_shapes=[buffer(*m.shape) for m in maps] + [
            buffer(RAW_ROWS, 128),
            buffer(*TILES), buffer(48, CELL), buffer(32, CELL), buffer(32, CELL),
            buffer(RAW_ROWS, 128), buffer(RAW_ROWS, 128), pltpu.VMEM((WINDOW, 128), F32),
            pltpu.VMEM((48, CELL), F32), pltpu.VMEM((32, CELL), F32), buffer(48, CELL), buffer(32, CELL),
            buffer(2304, 768), buffer(2304, 1280), buffer(1152, 1024),
            buffer(384, 1152), buffer(384, 768), buffer(384, 384),
            pltpu.VMEM((2, 1024, 128), F32),
            cells(64), cells(48), cells(32), cells(32), cells(48), cells(32),
            cells(32), cells(32), cells(16), cells(16), cells(48), cells(32), cells(32), cells(48), cells(64),
            sems(13), sems(5), sems(5), sems(NZ - 1), sems(NZ - 1), sems(96), sems(96),
        ],
        compiler_params=pltpu.CompilerParams(
            collective_id=0, has_side_effects=True, vmem_limit_bytes=60 * 2**20
        ),
        name="exchange",
    )(*maps, raw)
    return pl.pallas_call(
        finish_kernel,
        out_shape=results,
        in_specs=[VMEM] * 4,
        out_specs=[VMEM] * 4,
        compiler_params=pltpu.CompilerParams(vmem_limit_bytes=60 * 2**20),
        name="finish",
    )(*done)


def solution(mesh):
    maps = P("tile", "branch")
    return jax.shard_map(
        per_device, mesh=mesh, in_specs=(maps,) * 12 + (P("tile"),), out_specs=(maps,) * 4, check_vma=False
    )
```

```python
import jax
import jax.numpy as jnp
from jax import lax
from jax.experimental import pallas as pl
from jax.experimental.pallas import tpu as pltpu
from jax.sharding import PartitionSpec as P

BF = jnp.bfloat16
F32 = jnp.float32
MESH = pl.DeviceIdType.MESH
N_TILE = 128
N_BRANCH = 4
NZ = 16
Z_PARTS = ((0, 5), (5, 11))
SHARD = 13734
CELL = 384
RAW_ROWS = 112
BASE = 104
WINDOW = 464

ROW0 = {
    (0, 1, 0): 0,
    (0, 2, 0): 12,
    (0, 3, 0): 36,
    (1, 0, 0): 84,
    (1, 2, 0): 192,
    (1, 3, 0): 240,
    (2, 0, 0): 336,
    (2, 0, 1): 390,
    (2, 1, 0): 606,
    (2, 3, 0): 1038,
    (3, 0, 0): 1230,
    (3, 0, 1): 1284,
    (3, 0, 2): 1338,
    (3, 1, 0): 1770,
    (3, 1, 1): 1986,
    (3, 2, 0): 2850,
}


SPLITS = {(48, 0): 0, (48, 48): 1024, (48, 64): 2048, (96, 0): 3072, (192, 0): 3584}
PLACES = (
    [(48, 4 + q, 5 + q) for q in range(2)] + [(48, 0, 8), (48, 0, 4), (48, 4, 8)]
    + [(48, 2 * q, 2 * q + 2) for q in range(4)] + [(96, q, q + 1) for q in range(4)]
    + [(96, 0, 4), (96, 0, 2), (96, 2, 4), (192, 0, 1), (192, 1, 2), (192, 0, 2)]
)


def remote(src, dst, send, recv, branch, tile):
    return pltpu.make_async_remote_copy(
        src_ref=src, dst_ref=dst, send_sem=send, recv_sem=recv, device_id=(branch, tile), device_id_type=MESH
    )


def tile_at(row_tile, jb):
    group, n = row_tile // 9, 3 * (row_tile % 9) + jb
    j, slot = n // 7, n % 7
    k = 4 * group + j
    return k // 8, (slot % 2, slot // 2, (k // 2) % 4, k % 2)


def place_of(distance):
    return 2 * distance - 1 if distance > 0 else -2 * distance


def dot(a, b):
    return lax.dot_general(a, b, (((1,), (0,)), ((), ())), preferred_element_type=F32)


def dot_nt(a, b):
    return lax.dot_general(a, b, (((1,), (1,)), ((), ())), preferred_element_type=F32)


def unit_matrix(rows, cols, target):
    column = lax.broadcasted_iota(jnp.int32, (1, cols), 1)
    row = lax.broadcasted_iota(jnp.int32, (rows, cols), 0)
    return jnp.where(row == target(column), 1.0, 0.0).astype(BF)


def exchange_kernel(
    *refs,
):
    inputs, outputs, refs = refs[:13], refs[13:17], refs[17:]
    loaded, refs = refs[:13], refs[13:]
    (
        tiles, row_in, col_in, corner_in, raw1, raw2, win, row_f, col_f, row_out, col_out,
        e3, e2, e1, u3, u2, u1, wide, splits, copies_of,
        c0, c1, c2, c3, sg1, sg2, q20, q30a, q30b, q31, k1, k2a, k2b, nxt, out,
        l_sem, h_send, h_recv, z_send, z_recv, s_send, s_recv,
    ) = refs
    g1, g2, g3, g4, p1, p2, p3, p4, m20, m30a, m30b, m31, raw = loaded
    o1, o2, o3, o4 = outputs
    b = lax.axis_index("branch")
    k = lax.axis_index("tile")
    z, y, c = k // 8, lax.rem(k // 2, 4), lax.rem(k, 2)
    has_row = k < N_TILE - 1
    has_col = b < N_BRANCH - 1

    loads = [pltpu.make_async_copy(inputs[n], loaded[n], l_sem.at[n]) for n in range(13)]
    for n in (12, 1, 2, 3, 5, 6, 7, 8, 9, 10, 11, 0, 4):
        loads[n].start()

    def tile_of(zz, yy, cc):
        return zz * 8 + yy * 2 + cc

    def wrap(value, count):
        return lax.rem(value + count, count)

    left, right = wrap(b - 1, N_BRANCH), wrap(b + 1, N_BRANCH)
    up1, up2 = wrap(k - 1, N_TILE), wrap(k - 2, N_TILE)
    down1, down2 = wrap(k + 1, N_TILE), wrap(k + 2, N_TILE)

    partners = [
        (b, up1), (b, up2), (b, down1), (b, down2), (left, k), (right, k), (left, up1), (right, down1),
        (b, tile_of(z, y, 1 - c)), (wrap(b + 2, 4), k),
    ] + [(b, tile_of(z, wrap(y + d, 4), c)) for d in (1, 2, 3)]
    barrier = pltpu.get_barrier_semaphore()
    for step in range(1, NZ):
        pl.semaphore_signal(
            barrier, inc=1, device_id=(b, tile_of(wrap(z + step, NZ), y, c)), device_id_type=MESH
        )
    for who in partners:
        pl.semaphore_signal(barrier, inc=1, device_id=who, device_id_type=MESH)

    for ref in (e3, e2, e1, c1, c2, c3, sg1, sg2, q20, q30a, q30b, q31, k1, k2a, k2b, nxt, win):
        ref[...] = jnp.zeros_like(ref)

    for load in loads:
        load.wait()
    row_f[...] = jnp.zeros_like(row_f)
    col_f[...] = jnp.zeros_like(col_f)
    at_row, at_col = 0, 0
    for g, p in ((g2, p2), (g3, p3), (g4, p4)):
        rows = g.shape[0]
        masked = jnp.where(p[...].astype(F32) > 0, g[...].astype(F32), 0.0)
        for cell in range(8):
            row_f[at_row + cell : at_row + cell + 1, :] = masked[0:1, CELL * cell : CELL * (cell + 1)]
        col_f[at_col : at_col + rows, :] = masked[:, 0:CELL]
        at_row, at_col = at_row + 8, at_col + rows
    for m, at_row, at_col in ((m20, 24, 8), (m30a, 28, 12), (m31, 32, 18), (m30b, 36, 16)):
        rows, units = m.shape[0], m.shape[1] // CELL
        value = m[...].astype(F32)
        for unit in range(units):
            row_f[at_row + unit : at_row + unit + 1, :] = value[0:1, CELL * unit : CELL * (unit + 1)]
        col_f[at_col : at_col + rows, :] = value[:, 0:CELL]
    row_out[...] = row_f[...].astype(BF)
    col_out[...] = col_f[...].astype(BF)


    pl.semaphore_wait(barrier, len(partners) + NZ - 1)
    first = [
        remote(raw, raw1, h_send.at[0], h_recv.at[0], b, up1),
        remote(raw, raw2, h_send.at[1], h_recv.at[1], b, up2),
        remote(row_out, row_in, h_send.at[2], h_recv.at[2], b, up1),
        remote(col_out, col_in, h_send.at[3], h_recv.at[3], left, k),
        remote(col_out, corner_in, h_send.at[4], h_recv.at[4], left, up1),
    ]
    for copy in first:
        copy.start()

    for (j, at), lanes in SPLITS.items():
        width = 256 if j == 192 else 128

        def split_target(col):
            part, lane = col // width, lax.rem(col, width) - at
            return jnp.where((lane >= 0) & (lane < j), part * j + lane, -1)

        splits[:, lanes : lanes + CELL // j * width] = unit_matrix(CELL, CELL // j * width, split_target)
    for number, (j, low, high) in enumerate(PLACES):

        def place_target(col):
            which = col // j
            return jnp.where((which >= low) & (which < high), lax.rem(col, j), -1)

        rows = 256 if j == 192 else 128
        copies_of[0:rows, CELL * number : CELL * (number + 1)] = unit_matrix(rows, CELL, place_target)

    def put(buffer, row, value):
        rows = value.shape[0]
        for l in range(3):
            buffer[l, row : row + rows, :] = value[:, 128 * l : 128 * (l + 1)]

    def spread_units(buffer, value, units):
        rows = value.shape[0]
        for unit in range(units):
            for l in range(3):
                piece = value[:, CELL * unit + 128 * l : CELL * unit + 128 * (l + 1)]
                if rows == 1:
                    buffer[l, unit : unit + 1, :] = piece
                else:
                    buffer[l, pl.ds(unit, rows, stride=units), :] = piece

    def masked(g, p):
        return jnp.where(p[...].astype(F32) > 0, g[...].astype(F32), 0.0)

    spread_units(c0, masked(g1, p1), 8)
    for buffer, g, p in ((c1, g2, p2), (c2, g3, p3), (c3, g4, p4)):
        spread_units(buffer, masked(g, p), 8)
    for buffer, m, units in ((q20, m20, 4), (q30a, m30a, 4), (q31, m31, 4), (q30b, m30b, 2)):
        spread_units(buffer, m[...].astype(F32), units)

    group, j = k // 4, lax.rem(k, 4)
    first_tile = (7 * j) // 3
    delta = 13734 * j - 6144 * first_tile - 360 * group + BASE * 128
    lane = lax.broadcasted_iota(jnp.int32, (RAW_ROWS, 128), 1)
    for d, shard in enumerate((raw, raw1, raw2)):
        if d > 0:
            first[d - 1].wait_recv()
        start = delta + SHARD * d
        q, phase = start // 128, lax.rem(start, 128)
        rolled = pltpu.roll(shard[...].astype(F32), phase, 1)
        win[pl.ds(q, RAW_ROWS), :] += jnp.where(lane >= phase, rolled, 0.0)
        win[pl.ds(q + 1, RAW_ROWS), :] += jnp.where(lane >= phase, 0.0, rolled)
    for s in range(2):
        n = 7 * j + 2 * b + s
        row_tile = 9 * group + n // 3
        offset = jnp.where(row_tile >= 124, 2, 10)
        origin = BASE + 3 * (16 * (n // 3 - first_tile) + offset) + lax.rem(n, 3)
        tiles[s, b, y, c, 0] = win[pl.ds(origin, 16, stride=3), :].astype(BF)

    copies = {}
    for step in (1, 15, 2, 14, 3, 13, 4, 12, 5, 11, 6, 10, 7, 9, 8):
        at = place_of(-step if step <= 7 else NZ - step)
        copies[at] = remote(
            tiles.at[:, b, y, c, 0], tiles.at[:, b, y, c, at], z_send.at[at - 1], z_recv.at[at - 1],
            b, tile_of(wrap(z + step, NZ), y, c),
        )
        copies[at].start()

    for copy in first[2:]:
        copy.wait_recv()
    row_halo = row_in[...].astype(F32)
    col_halo = col_in[...].astype(F32)
    corner = corner_in[...].astype(F32)
    row_zero = jnp.where(has_row, row_halo, 0.0)
    col_zero = jnp.where(has_col, col_halo, 0.0)
    corner_zero = jnp.where(has_row & has_col, corner, 0.0)
    at = 0
    for buffer, rows, halo in ((c1, 4, 0), (c2, 2, 8), (c3, 1, 16)):
        put(buffer, 8 * rows, row_zero[halo : halo + 8])
        put(buffer, 8 * rows + 8, col_zero[at : at + rows])
        put(buffer, 8 * rows + 8 + rows, corner_zero[at : at + 1])
        at += rows
    for buffer, rows, units, halo, at in ((q20, 4, 4, 24, 8), (q30a, 4, 4, 28, 12), (q31, 2, 4, 32, 18), (q30b, 2, 2, 36, 16)):
        put(buffer, rows * units, row_halo[halo : halo + units])
        put(buffer, (rows + 1) * units, col_halo[at : at + rows])
        put(buffer, (rows + 1) * units + rows, corner[at : at + 1])

    def flags(buffer):
        whole = jnp.concatenate([buffer[l] for l in range(3)], axis=1)
        return jnp.where(whole > 0, 1.0, 0.0).astype(BF)

    def target20(shift):
        def target(col):
            part, lane = col // CELL, lax.rem(col, CELL)
            pixel, channel = lane // 96, lax.rem(lane, 96) - shift
            return jnp.where((channel >= 0) & (channel < 48), part * 192 + pixel * 48 + channel, -1)

        return target

    def target31(col):
        part, lane = col // CELL, lax.rem(col, CELL)
        return jnp.where(lane < 192, part * 192 + lane, -1)

    def target30b(col):
        part, lane = col // CELL, lax.rem(col, CELL) - 192
        return jnp.where((lane >= 0) & (lane < 96), part * 96 + lane, -1)

    def keep(buffer, value, parts, count, extra_from, extra_rows, extra_to):
        for l in range(3):
            for part in range(parts):
                lanes = slice(part * CELL + 128 * l, part * CELL + 128 * (l + 1))
                buffer[l, pl.ds(part, count, stride=parts), :] = value[0:count, lanes]
            buffer[l, extra_to : extra_to + extra_rows, :] = value[
                extra_from : extra_from + extra_rows, 128 * l : 128 * (l + 1)
            ]

    mask1 = dot(flags(q20), unit_matrix(CELL, 768, target20(0))) + dot(
        flags(q30a), unit_matrix(CELL, 768, target20(48))
    )
    keep(k1, mask1, 2, 20, 20, 5, 40)
    keep(k2a, dot(flags(q31), unit_matrix(CELL, 768, target31)), 2, 12, 12, 3, 24)
    keep(k2b, dot(flags(q30b), unit_matrix(CELL, 1536, target30b)), 4, 6, 6, 3, 24)

    distances = [lax.rem(zz - z + 23, NZ) - 7 for zz in range(NZ)]
    places = [jnp.where(d > 0, 2 * d - 1, -2 * d) for d in distances]

    def tile(row_tile, jb):
        zz, (s, x_at, y_at, c_at) = tile_at(row_tile, jb)
        return tiles[s, x_at, y_at, c_at, places[zz]]

    def load_rows(row_tile, count):
        columns = [
            jnp.concatenate([tile(row_tile + t, jb) for t in range(count)], axis=0) for jb in range(3)
        ]
        return jnp.concatenate(columns, axis=1)

    def rows_of(key, rows, j, at=0):
        n = CELL // j
        r0 = ROW0[key]
        row_tile, offset = (286, 0) if r0 == 0 else divmod(r0 - 10, 16)
        count = -(-(offset + rows) // 16)
        width = 256 if j == 192 else 128

        lanes = SPLITS[j, at]
        split = dot(load_rows(row_tile, count), splits[:, lanes : lanes + n * width])
        parts = []
        for half in range(width // 128):
            for part in range(n):
                wide[half, pl.ds(part, 16 * count, stride=n), :] = split[
                    :, part * width + 128 * half : part * width + 128 * (half + 1)
                ]
            parts.append(wide[half, offset * n : (offset + rows) * n, :])
        return parts[0] if len(parts) == 1 else jnp.concatenate(parts, axis=1)

    def place(weights, j, low, high):
        lanes = CELL * PLACES.index((j, low, high))
        return dot(weights, copies_of[0 : weights.shape[1], lanes : lanes + CELL])

    def taps(e, row0, pitch, weights, placed, seg, nxt_seg, nxt_width):
        count = len(placed)
        i = weights.shape[0] // 9

        def tap(value, a, bb):
            return value[(3 * a + bb) * i : (3 * a + bb + 1) * i]

        for a in range(3):
            for q in range(count):
                even = row0 + CELL * a + 2 * q * pitch
                e[even : even + i, seg : seg + CELL] = tap(placed[q], a, 1).astype(BF)
                odd = even + pitch
                value = tap(placed[q], a, 2)
                if q + 1 < count:
                    value = value + tap(placed[q + 1], a, 0)
                else:
                    e[odd : odd + i, nxt_seg : nxt_seg + nxt_width] = tap(weights, a, 0).astype(BF)
                e[odd : odd + i, seg : seg + CELL] = value.astype(BF)

    def fill_e3():
        for key, i, row0, pitch in (
            ((3, 2, 0), 192, 0, 192),
            ((3, 1, 1), 96, 1152, 96),
            ((3, 0, 2), 48, 1152 + 192, 48),
        ):
            r0 = ROW0[key]
            start = 124 + (r0 - 1986) // 16 if r0 >= 1986 else (r0 - 10) // 16
            for a in range(3):
                even = row0 + CELL * a
                odd = even + pitch
                for bb, at, seg in ((1, even, 0), (2, odd, 0), (0, odd, CELL)):
                    first = start + (3 * a + bb) * (i // 16)
                    for t in range(i // 16):
                        for jb in range(3):
                            e3[at + 16 * t : at + 16 * (t + 1), seg + 128 * jb : seg + 128 * (jb + 1)] = tile(
                                first + t, jb
                            )

    def fill_e2_21():
        w = rows_of((2, 1, 0), 432, 192)
        taps(e2, 0, 96, w, [place(w.astype(BF), 192, q, q + 1) for q in range(2)], 0, 384, 256)

    def fill_e2_31():
        w = rows_of((3, 1, 0), 216, 96)
        taps(e2, 0, 96, w, [place(w.astype(BF), 96, q, q + 1) for q in range(2)], 640, 1024, 128)

    def fill_e2_mid():
        w = rows_of((2, 0, 1), 216, 192)
        placed = [place(w.astype(BF), 192, q, q + 1) for q in range(2)]
        taps(e2, 1152, 96, w, placed, 0, 384, 256)
        w = rows_of((3, 0, 1), 54, 48)
        w_next = rows_of((3, 0, 1), 54, 48, 64)
        placed = [place(w.astype(BF), 48, 4 + q, 5 + q) for q in range(2)]
        taps(e2, 1152 + 48, 96, w_next, placed, 640, 1024 + 128, 128)

    def fill_e1_10():
        w = rows_of((1, 0, 0), 108, 96)
        taps(e1, 0, 48, w, [place(w.astype(BF), 96, q, q + 1) for q in range(4)], 0, 384, 128)

    def fill_e1_mid():
        w = rows_of((2, 0, 0), 54, 48) + 0.0
        w = w + rows_of((3, 0, 0), 54, 48, 48)
        taps(e1, 0, 48, w, [place(w.astype(BF), 96, q, q + 1) for q in range(4)], 512, 896, 128)

    def fill_up():
        u3[:, 0:384] = place(rows_of((0, 3, 0), 48, 48).astype(BF), 48, 0, 8).astype(BF)
        u3[:, 384:768] = place(rows_of((1, 3, 0), 96, 96).astype(BF), 96, 0, 4).astype(BF)
        u3[:, 768:1152] = place(rows_of((2, 3, 0), 192, 192).astype(BF), 192, 0, 2).astype(BF)
        w02 = rows_of((0, 2, 0), 24, 48).astype(BF)
        w12 = rows_of((1, 2, 0), 48, 96).astype(BF)
        for q in range(2):
            u2[192 * q : 192 * (q + 1), 0:384] = place(w02, 48, 4 * q, 4 * q + 4).astype(BF)
            u2[192 * q : 192 * (q + 1), 384:768] = place(w12, 96, 2 * q, 2 * q + 2).astype(BF)
        w01 = rows_of((0, 1, 0), 12, 48).astype(BF)
        for q in range(4):
            u1[96 * q : 96 * (q + 1), :] = place(w01, 48, 2 * q, 2 * q + 2).astype(BF)

    def lanes_of(buffer, count=3):
        return [buffer[l] for l in range(count)]

    def shifted(buffer, rows, count):
        total = buffer.shape[1]
        pieces = []
        for l in range(count):
            nxt[l, 0 : 8 * rows, :] = buffer[l, 1 : 8 * rows + 1, :]
            for p in range(rows):
                nxt[l, 8 * p + 7 : 8 * p + 8, :] = buffer[l, 8 * rows + p : 8 * rows + p + 1, :]
            nxt[l, 8 * rows : total, :] = jnp.zeros((total - 8 * rows, 128), F32)
            pieces.append(nxt[l, 0:total, :])
        return pieces

    def lhs(pieces):
        return jnp.concatenate([piece.astype(BF) for piece in pieces], axis=1)

    def rows_out(y, a, lo, hi, lane0):
        return y[lo:hi, lane0 + CELL * a : lane0 + CELL * (a + 1)]

    def upsampled(y, p, lane0):
        even = rows_out(y, 1, 8 * p, 8 * p + 8, lane0)
        odd = rows_out(y, 2, 8 * p, 8 * p + 8, lane0) + rows_out(y, 0, 8 * p + 8, 8 * p + 16, lane0)
        return even, odd

    def section(buffer, y, rows, kept):
        base = 8 * (rows + 1)
        for p in range(rows):
            even, odd = upsampled(y, p, 1152)
            put(buffer, 16 * p, even)
            put(buffer, 16 * p + 8, odd)
        put(buffer, 16 * rows, rows_out(y, 1, 8 * rows, 8 * rows + 8, 1152))
        extra = 8 * (2 * rows + 1)
        for p in range(rows + 1):
            put(buffer, extra + 2 * p, rows_out(y, 1, base + p, base + p + 1, 1152))
            if p < rows:
                odd = rows_out(y, 2, base + p, base + p + 1, 1152) + rows_out(y, 0, base + p + 1, base + p + 2, 1152)
                put(buffer, extra + 2 * p + 1, odd)
        for l in range(3):
            buffer[l] = jnp.where(kept(l) > 0.5, buffer[l], 0.0)

    def emit(ref, rows, value):
        put(out, 0, value)
        for cell in range(8):
            for l in range(3):
                lane0 = CELL * cell + 128 * l
                if rows == 1:
                    piece = out[l, cell : cell + 1, :]
                else:
                    piece = out[l, pl.ds(cell, rows, stride=8), :]
                ref[:, lane0 : lane0 + 128] = piece.astype(BF)

    def block_sums(buffer, rows, factor):
        groups = []
        for first in range(0, rows, factor):
            pieces = []
            for l in range(3):
                total = buffer[l, 8 * first : 8 * first + 8, :]
                for p in range(first + 1, first + factor):
                    total = total + buffer[l, 8 * p : 8 * p + 8, :]
                pieces.append(total)
            groups.append(jnp.concatenate(pieces, axis=1))
        return jnp.concatenate(groups, axis=0).astype(BF)

    def own(buffer, rows):
        return jnp.concatenate([buffer[l, 0 : 8 * rows, :] for l in range(3)], axis=1)

    class Part:
        def __init__(self, s, lo, size, sem):
            self.s, self.lo, self.size, self.used = s, lo, size, sem
            self.u, self.v = (b, y) if s == 0 else (y, b)
            self.pending, self.second = [], []

        def send(self, ref, x_to, tile_to):
            copy = remote(ref, ref, s_send.at[self.used], s_recv.at[self.used], x_to, tile_to)
            copy.start()
            self.used += 1
            self.pending.append(copy)
            return copy

        def send_bundle(self, u_of, to_u, to_v):
            zs = pl.ds(self.lo, self.size)
            if self.s == 0:
                return self.send(tiles.at[0, u_of, y, c, zs], to_u, tile_of(z, to_v, c))
            return self.send(tiles.at[1, b, u_of, c, zs], to_v, tile_of(z, to_u, c))

        def spread(self, u_of):
            self.second.append((u_of, [self.send_bundle(u_of, self.u, wrap(self.v + d, 4)) for d in (1, 3, 2)]))

        def start(self):
            self.first = [(d, self.send_bundle(self.u, wrap(self.u + d, 4), self.v)) for d in (1, 3, 2)]
            self.spread(self.u)

        def pass_on(self):
            for d, copy in self.first:
                copy.wait_recv()
                self.spread(wrap(self.u - d, 4))

        def cross(self):
            zs = pl.ds(self.lo, self.size)
            self.across = []
            for u_of, copies_in in self.second:
                for copy in copies_in:
                    copy.wait_recv()
                ref = tiles.at[0, u_of, :, c, zs] if self.s == 0 else tiles.at[1, :, u_of, c, zs]
                self.across.append(self.send(ref, b, tile_of(z, y, 1 - c)))

        def arrived(self):
            for copy in self.across:
                copy.wait_recv()

    parts = []
    for lo, size in Z_PARTS:
        for at in range(max(lo, 1), lo + size):
            copies[at].wait_recv()
        pair = [Part(s, lo, size, 19 * (len(parts) + s)) for s in range(2)]
        for part in pair:
            part.start()
        for part in pair:
            part.pass_on()
        parts += pair
    for part in parts:
        part.cross()
    for part in parts:
        part.arrived()
    fill_e2_21()
    fill_e2_31()
    fill_e2_mid()
    fill_e1_10()
    fill_e1_mid()
    y2 = dot_nt(lhs(lanes_of(c2) + shifted(c2, 3, 2)), e2[:, 0:640])
    y1 = dot_nt(lhs(lanes_of(c1) + shifted(c1, 5, 1)), e1[:, 0:512])
    fill_up()
    fill_e3()

    up = jnp.concatenate([block_sums(c0, 8, 8), block_sums(c1, 4, 4), block_sums(c2, 2, 2)], axis=1)
    emit(o4, 1, own(c3, 1) + dot_nt(up, u3[...]))

    y3 = dot_nt(lhs(lanes_of(c3) + shifted(c3, 2, 3)), e3[...])
    up = jnp.concatenate([block_sums(c0, 8, 4), block_sums(c1, 4, 2)], axis=1)
    down = jnp.concatenate(upsampled(y3, 0, 0), axis=0)
    emit(o3, 2, own(c2, 2) + dot_nt(up, u2[...]) + down)

    section(sg2, y3, 1, lambda l: k2a[l] + k2b[l])
    y2 = y2 + dot_nt(lhs(lanes_of(sg2) + shifted(sg2, 3, 2)), e2[:, 640:1280])
    down = jnp.concatenate(upsampled(y2, 0, 0) + upsampled(y2, 1, 0), axis=0)
    emit(o2, 4, own(c1, 4) + dot_nt(block_sums(c0, 8, 2), u1[...]) + down)

    section(sg1, y2, 2, lambda l: k1[l])
    y1 = y1 + dot_nt(lhs(lanes_of(sg1) + shifted(sg1, 5, 1)), e1[:, 512:1024])
    rows = []
    for p in range(4):
        rows.extend(upsampled(y1, p, 0))
    emit(o1, 8, own(c0, 8) + jnp.concatenate(rows, axis=0))

    for part in parts:
        for copy in part.pending:
            copy.wait_send()
    for copy in list(copies.values()) + first:
        copy.wait_send()


def finish_kernel(*refs):
    for n in range(4):
        refs[4 + n][...] = refs[n][...]


ANY = pl.BlockSpec(memory_space=pl.ANY)
VMEM = pl.BlockSpec(memory_space=pltpu.VMEM)
TILES = (2, 4, 4, 2, NZ, 16, 128)


def per_device(*operands):
    maps = operands[:12]
    raw = jnp.pad(operands[12], (0, RAW_ROWS * 128 - SHARD)).reshape(RAW_ROWS, 128)

    def cells(rows):
        return pltpu.VMEM((3, rows, 128), F32)

    def buffer(*shape):
        return pltpu.VMEM(shape, BF)

    def sems(count):
        return pltpu.SemaphoreType.DMA((count,))

    results = [jax.ShapeDtypeStruct(g.shape, BF) for g in maps[:4]]
    done = pl.pallas_call(
        exchange_kernel,
        out_shape=results,
        in_specs=[ANY] * 13,
        out_specs=[VMEM] * 4,
        scratch_shapes=[buffer(*m.shape) for m in maps] + [
            buffer(RAW_ROWS, 128),
            buffer(*TILES), buffer(48, CELL), buffer(32, CELL), buffer(32, CELL),
            buffer(RAW_ROWS, 128), buffer(RAW_ROWS, 128), pltpu.VMEM((WINDOW, 128), F32),
            pltpu.VMEM((48, CELL), F32), pltpu.VMEM((32, CELL), F32), buffer(48, CELL), buffer(32, CELL),
            buffer(2304, 768), buffer(2304, 1280), buffer(1152, 1024),
            buffer(384, 1152), buffer(384, 768), buffer(384, 384),
            pltpu.VMEM((2, 1024, 128), F32), buffer(CELL, 4096), buffer(256, CELL * len(PLACES)),
            cells(64), cells(48), cells(32), cells(32), cells(48), cells(32),
            cells(32), cells(32), cells(16), cells(16), cells(48), cells(32), cells(32), cells(48), cells(64),
            sems(13), sems(5), sems(5), sems(NZ - 1), sems(NZ - 1), sems(38 * len(Z_PARTS)), sems(38 * len(Z_PARTS)),
        ],
        compiler_params=pltpu.CompilerParams(
            collective_id=0, has_side_effects=True, vmem_limit_bytes=60 * 2**20
        ),
        name="exchange",
    )(*maps, raw)
    return pl.pallas_call(
        finish_kernel,
        out_shape=results,
        in_specs=[VMEM] * 4,
        out_specs=[VMEM] * 4,
        compiler_params=pltpu.CompilerParams(vmem_limit_bytes=60 * 2**20),
        name="finish",
    )(*done)


def solution(mesh):
    maps = P("tile", "branch")
    return jax.shard_map(
        per_device, mesh=mesh, in_specs=(maps,) * 12 + (P("tile"),), out_specs=(maps,) * 4, check_vma=False
    )
```

```python
import jax
import jax.numpy as jnp
from jax import lax
from jax.experimental import pallas as pl
from jax.experimental.pallas import tpu as pltpu
from jax.sharding import PartitionSpec as P

BF = jnp.bfloat16
F32 = jnp.float32
MESH = pl.DeviceIdType.MESH
N_TILE = 128
N_BRANCH = 4
NZ = 16
Z_PARTS = ((0, 5), (5, 11))
SHARD = 13734
CELL = 384
RAW_ROWS = 112
BASE = 104
WINDOW = 464

C1, C2, C3, SUMS, K1, K2, STRIP = 0, 48, 80, 112, 200, 248, 280

ROW0 = {
    (0, 1, 0): 0,
    (0, 2, 0): 12,
    (0, 3, 0): 36,
    (1, 0, 0): 84,
    (1, 2, 0): 192,
    (1, 3, 0): 240,
    (2, 0, 0): 336,
    (2, 0, 1): 390,
    (2, 1, 0): 606,
    (2, 3, 0): 1038,
    (3, 0, 0): 1230,
    (3, 0, 1): 1284,
    (3, 0, 2): 1338,
    (3, 1, 0): 1770,
    (3, 1, 1): 1986,
    (3, 2, 0): 2850,
}


SPLITS = {(48, 0): 0, (48, 48): 1024, (48, 64): 2048, (96, 0): 3072, (192, 0): 3584}
PLACES = (
    [(48, 4 + q, 5 + q) for q in range(2)] + [(48, 0, 8), (48, 0, 4), (48, 4, 8)]
    + [(48, 2 * q, 2 * q + 2) for q in range(4)] + [(96, q, q + 1) for q in range(4)]
    + [(96, 0, 4), (96, 0, 2), (96, 2, 4), (192, 0, 1), (192, 1, 2), (192, 0, 2)]
)


def remote(src, dst, send, recv, branch, tile):
    return pltpu.make_async_remote_copy(
        src_ref=src, dst_ref=dst, send_sem=send, recv_sem=recv, device_id=(branch, tile), device_id_type=MESH
    )


def tile_at(row_tile, jb):
    group, n = row_tile // 9, 3 * (row_tile % 9) + jb
    j, slot = n // 7, n % 7
    k = 4 * group + j
    return k // 8, (slot % 2 if slot < 6 else k % 2, slot // 2, (k // 2) % 4, k % 2)


def place_of(distance):
    return 2 * distance - 1 if distance > 0 else -2 * distance


def dot(a, b):
    return lax.dot_general(a, b, (((1,), (0,)), ((), ())), preferred_element_type=F32)


def dot_nt(a, b):
    return lax.dot_general(a, b, (((1,), (1,)), ((), ())), preferred_element_type=F32)


def unit_matrix(rows, cols, target):
    column = lax.broadcasted_iota(jnp.int32, (1, cols), 1)
    row = lax.broadcasted_iota(jnp.int32, (rows, cols), 0)
    return jnp.where(row == target(column), 1.0, 0.0).astype(BF)


def exchange_kernel(
    *refs,
):
    inputs, outputs, refs = refs[:13], refs[13:17], refs[17:]
    loaded, refs = refs[:13], refs[13:]
    (
        tiles, row_in, col_in, corner_in, raw, raw1, raw2, shard_f, win, row_f, col_f, row_out, col_out,
        e3, e2, e1, u3, u2, u1, wide, splits, copies_of,
        c0, c1, c2, c3, sg1, sg2, q20, q30a, q30b, q31, k1, k2a, k2b, nxt, out, strip, acc, acc_in,
        l_sem, h_send, h_recv, z_send, z_recv, s_send, s_recv, x_send, x_recv,
    ) = refs
    g1, g2, g3, g4, p1, p2, p3, p4, m20, m30a, m30b, m31, shard_in = loaded
    o1, o2, o3, o4 = outputs
    b = lax.axis_index("branch")
    k = lax.axis_index("tile")
    z, y, c = k // 8, lax.rem(k // 2, 4), lax.rem(k, 2)
    has_row = k < N_TILE - 1
    has_col = b < N_BRANCH - 1

    loads = [pltpu.make_async_copy(inputs[n], loaded[n], l_sem.at[n]) for n in range(13)]
    for n in (12, 1, 2, 3, 5, 6, 7, 8, 9, 10, 11, 0, 4):
        loads[n].start()

    def tile_of(zz, yy, cc):
        return zz * 8 + yy * 2 + cc

    def wrap(value, count):
        return lax.rem(value + count, count)

    left, right = wrap(b - 1, N_BRANCH), wrap(b + 1, N_BRANCH)
    up1, up2 = wrap(k - 1, N_TILE), wrap(k - 2, N_TILE)
    down1, down2 = wrap(k + 1, N_TILE), wrap(k + 2, N_TILE)

    partners = [
        (b, up1), (b, up2), (b, down1), (b, down2), (left, k), (right, k), (left, up1), (right, down1),
        (b, tile_of(z, y, 1 - c)), (wrap(b + 2, 4), k),
    ] + [(b, tile_of(z, wrap(y + d, 4), c)) for d in (1, 2, 3)]
    barrier = pltpu.get_barrier_semaphore()
    for step in range(1, NZ):
        pl.semaphore_signal(
            barrier, inc=1, device_id=(b, tile_of(wrap(z + step, NZ), y, c)), device_id_type=MESH
        )
    for who in partners:
        pl.semaphore_signal(barrier, inc=1, device_id=who, device_id_type=MESH)

    win[...] = jnp.zeros_like(win)
    loads[12].wait()
    whole = SHARD // 1024 * 1024
    rest = SHARD // 128 * 128
    row_at = [n // 128 for n in (whole, rest)]
    shard_f[0 : row_at[0], :] = shard_in[0:whole].astype(F32).reshape(row_at[0], 128)
    shard_f[row_at[0] : row_at[1], :] = shard_in[whole:rest].astype(F32).reshape(row_at[1] - row_at[0], 128)
    shard_f[row_at[1] : RAW_ROWS, :] = jnp.zeros((RAW_ROWS - row_at[1], 128), F32)
    shard_f[row_at[1] : row_at[1] + 1, 0 : SHARD - rest] = shard_in[rest:SHARD].astype(F32).reshape(1, SHARD - rest)
    raw[...] = shard_f[...].astype(BF)

    pl.semaphore_wait(barrier, len(partners) + NZ - 1)
    first = [
        remote(raw, raw1, h_send.at[0], h_recv.at[0], b, up1),
        remote(raw, raw2, h_send.at[1], h_recv.at[1], b, up2),
        remote(row_out, row_in, h_send.at[2], h_recv.at[2], b, up1),
        remote(col_out, col_in, h_send.at[3], h_recv.at[3], left, k),
        remote(col_out, corner_in, h_send.at[4], h_recv.at[4], left, up1),
    ]
    for copy in first[:2]:
        copy.start()

    for load in loads[:12]:
        load.wait()
    row_f[...] = jnp.zeros_like(row_f)
    col_f[...] = jnp.zeros_like(col_f)
    at_row, at_col = 0, 0
    for g, p in ((g2, p2), (g3, p3), (g4, p4)):
        rows = g.shape[0]
        masked = jnp.where(p[...].astype(F32) > 0, g[...].astype(F32), 0.0)
        for cell in range(8):
            row_f[at_row + cell : at_row + cell + 1, :] = masked[0:1, CELL * cell : CELL * (cell + 1)]
        col_f[at_col : at_col + rows, :] = masked[:, 0:CELL]
        at_row, at_col = at_row + 8, at_col + rows
    for m, at_row, at_col in ((m20, 24, 8), (m30a, 28, 12), (m31, 32, 18), (m30b, 36, 16)):
        rows, units = m.shape[0], m.shape[1] // CELL
        value = m[...].astype(F32)
        for unit in range(units):
            row_f[at_row + unit : at_row + unit + 1, :] = value[0:1, CELL * unit : CELL * (unit + 1)]
        col_f[at_col : at_col + rows, :] = value[:, 0:CELL]
    row_out[...] = row_f[...].astype(BF)
    col_out[...] = col_f[...].astype(BF)

    for copy in first[2:]:
        copy.start()

    group, j = k // 4, lax.rem(k, 4)
    first_tile = (7 * j) // 3
    delta = 13734 * j - 6144 * first_tile - 360 * group + BASE * 128
    lane = lax.broadcasted_iota(jnp.int32, (RAW_ROWS, 128), 1)
    for d, shard in enumerate((raw, raw1, raw2)):
        if d > 0:
            first[d - 1].wait_recv()
        start = delta + SHARD * d
        q, phase = start // 128, lax.rem(start, 128)
        rolled = pltpu.roll(shard[...].astype(F32), phase, 1)
        win[pl.ds(q, RAW_ROWS), :] += jnp.where(lane >= phase, rolled, 0.0)
        win[pl.ds(q + 1, RAW_ROWS), :] += jnp.where(lane >= phase, 0.0, rolled)
    for s in range(2):
        n = 7 * j + jnp.where(b == 3, 6, 2 * b + s)
        row_tile = 9 * group + n // 3
        offset = jnp.where(row_tile >= 124, 2, 10)
        origin = BASE + 3 * (16 * (n // 3 - first_tile) + offset) + lax.rem(n, 3)
        tiles[s, b, y, c, 0] = win[pl.ds(origin, 16, stride=3), :].astype(BF)

    copies = {}
    for step in (1, 15, 2, 14, 3, 13, 4, 12, 5, 11, 6, 10, 7, 9, 8):
        at = place_of(-step if step <= 7 else NZ - step)
        copies[at] = remote(
            tiles.at[:, b, y, c, 0], tiles.at[:, b, y, c, at], z_send.at[at - 1], z_recv.at[at - 1],
            b, tile_of(wrap(z + step, NZ), y, c),
        )
        copies[at].start()

    for (j, at), lanes in SPLITS.items():
        width = 256 if j == 192 else 128

        def split_target(col):
            part, lane = col // width, lax.rem(col, width) - at
            return jnp.where((lane >= 0) & (lane < j), part * j + lane, -1)

        splits[:, lanes : lanes + CELL // j * width] = unit_matrix(CELL, CELL // j * width, split_target)
    for number, (j, low, high) in enumerate(PLACES):

        def place_target(col):
            which = col // j
            return jnp.where((which >= low) & (which < high), lax.rem(col, j), -1)

        rows = 256 if j == 192 else 128
        copies_of[0:rows, CELL * number : CELL * (number + 1)] = unit_matrix(rows, CELL, place_target)

    for ref in (e3, e2, e1, c1, c2, c3, sg1, sg2, q20, q30a, q30b, q31, k1, k2a, k2b, nxt, acc):
        ref[...] = jnp.zeros_like(ref)

    def put(buffer, row, value):
        rows = value.shape[0]
        for l in range(3):
            buffer[l, row : row + rows, :] = value[:, 128 * l : 128 * (l + 1)]

    def spread_units(buffer, value, units):
        rows = value.shape[0]
        for unit in range(units):
            for l in range(3):
                piece = value[:, CELL * unit + 128 * l : CELL * unit + 128 * (l + 1)]
                if rows == 1:
                    buffer[l, unit : unit + 1, :] = piece
                else:
                    buffer[l, pl.ds(unit, rows, stride=units), :] = piece

    def masked(g, p):
        return jnp.where(p[...].astype(F32) > 0, g[...].astype(F32), 0.0)

    def flags(buffer):
        whole = jnp.concatenate([buffer[l] for l in range(3)], axis=1)
        return jnp.where(whole > 0, 1.0, 0.0).astype(BF)

    def target20(shift):
        def target(col):
            part, lane = col // CELL, lax.rem(col, CELL)
            pixel, channel = lane // 96, lax.rem(lane, 96) - shift
            return jnp.where((channel >= 0) & (channel < 48), part * 192 + pixel * 48 + channel, -1)

        return target

    def target31(col):
        part, lane = col // CELL, lax.rem(col, CELL)
        return jnp.where(lane < 192, part * 192 + lane, -1)

    def target30b(col):
        part, lane = col // CELL, lax.rem(col, CELL) - 192
        return jnp.where((lane >= 0) & (lane < 96), part * 96 + lane, -1)

    def keep(buffer, value, parts, count, extra_from, extra_rows, extra_to):
        for l in range(3):
            for part in range(parts):
                lanes = slice(part * CELL + 128 * l, part * CELL + 128 * (l + 1))
                buffer[l, pl.ds(part, count, stride=parts), :] = value[0:count, lanes]
            buffer[l, extra_to : extra_to + extra_rows, :] = value[
                extra_from : extra_from + extra_rows, 128 * l : 128 * (l + 1)
            ]

    def block_sums(buffer, rows, factor):
        groups = []
        for first in range(0, rows, factor):
            pieces = []
            for l in range(3):
                total = buffer[l, 8 * first : 8 * first + 8, :]
                for p in range(first + 1, first + factor):
                    total = total + buffer[l, 8 * p : 8 * p + 8, :]
                pieces.append(total)
            groups.append(jnp.concatenate(pieces, axis=1))
        return jnp.concatenate(groups, axis=0).astype(BF)

    def own_maps():
        spread_units(c0, masked(g1, p1), 8)
        for buffer, g, p in ((c1, g2, p2), (c2, g3, p3), (c3, g4, p4)):
            spread_units(buffer, masked(g, p), 8)
        for buffer, m, units in ((q20, m20, 4), (q30a, m30a, 4), (q31, m31, 4), (q30b, m30b, 2)):
            spread_units(buffer, m[...].astype(F32), units)

        for copy in first[2:]:
            copy.wait_recv()
        row_halo = row_in[...].astype(F32)
        col_halo = col_in[...].astype(F32)
        corner = corner_in[...].astype(F32)
        row_zero = jnp.where(has_row, row_halo, 0.0)
        col_zero = jnp.where(has_col, col_halo, 0.0)
        corner_zero = jnp.where(has_row & has_col, corner, 0.0)
        at = 0
        for buffer, rows, halo in ((c1, 4, 0), (c2, 2, 8), (c3, 1, 16)):
            put(buffer, 8 * rows, row_zero[halo : halo + 8])
            put(buffer, 8 * rows + 8, col_zero[at : at + rows])
            put(buffer, 8 * rows + 8 + rows, corner_zero[at : at + 1])
            at += rows
        for buffer, rows, units, halo, at in ((q20, 4, 4, 24, 8), (q30a, 4, 4, 28, 12), (q31, 2, 4, 32, 18), (q30b, 2, 2, 36, 16)):
            put(buffer, rows * units, row_halo[halo : halo + units])
            put(buffer, (rows + 1) * units, col_halo[at : at + rows])
            put(buffer, (rows + 1) * units + rows, corner[at : at + 1])

        mask1 = dot(flags(q20), unit_matrix(CELL, 768, target20(0))) + dot(
            flags(q30a), unit_matrix(CELL, 768, target20(48))
        )
        keep(k1, mask1, 2, 20, 20, 5, 40)
        keep(k2a, dot(flags(q31), unit_matrix(CELL, 768, target31)), 2, 12, 12, 3, 24)
        keep(k2b, dot(flags(q30b), unit_matrix(CELL, 1536, target30b)), 4, 6, 6, 3, 24)
        pooled = [block_sums(c0, 8, f) for f in (2, 4, 8)] + [block_sums(c1, 4, f) for f in (2, 4)] + [block_sums(c2, 2, 2)]
        for l in range(3):
            strip[0, l, C1 : C1 + 48, :] = c1[l]
            strip[0, l, C2 : C2 + 32, :] = c2[l]
            strip[0, l, C3 : C3 + 32, :] = c3[l]
            strip[0, l, K1 : K1 + 48, :] = k1[l]
            strip[0, l, K2 : K2 + 32, :] = k2a[l] + k2b[l]
        row = SUMS
        for value in pooled:
            rows = value.shape[0]
            for l in range(3):
                strip[0, l, row : row + rows, :] = value[:, 128 * l : 128 * (l + 1)].astype(F32)
            row += rows
        strip_copy.start()

    strip_copy = remote(
        strip.at[0], strip.at[1], x_send.at[0], x_recv.at[0], b, tile_of(z, y, 1 - c)
    )

    distances = [lax.rem(zz - z + 23, NZ) - 7 for zz in range(NZ)]
    places = [jnp.where(d > 0, 2 * d - 1, -2 * d) for d in distances]

    def tile(row_tile, jb):
        zz, (s, x_at, y_at, c_at) = tile_at(row_tile, jb)
        return tiles[s, x_at, y_at, c_at, places[zz]]

    def load_rows(row_tile, count):
        columns = [
            jnp.concatenate([tile(row_tile + t, jb) for t in range(count)], axis=0) for jb in range(3)
        ]
        return jnp.concatenate(columns, axis=1)

    def rows_of(key, rows, j, at=0):
        n = CELL // j
        r0 = ROW0[key]
        row_tile, offset = (286, 0) if r0 == 0 else divmod(r0 - 10, 16)
        count = -(-(offset + rows) // 16)
        width = 256 if j == 192 else 128

        lanes = SPLITS[j, at]
        split = dot(load_rows(row_tile, count), splits[:, lanes : lanes + n * width])
        parts = []
        for half in range(width // 128):
            for part in range(n):
                wide[half, pl.ds(part, 16 * count, stride=n), :] = split[
                    :, part * width + 128 * half : part * width + 128 * (half + 1)
                ]
            parts.append(wide[half, offset * n : (offset + rows) * n, :])
        return parts[0] if len(parts) == 1 else jnp.concatenate(parts, axis=1)

    def place(weights, j, low, high):
        lanes = CELL * PLACES.index((j, low, high))
        return dot(weights, copies_of[0 : weights.shape[1], lanes : lanes + CELL])

    def taps(e, row0, pitch, weights, placed, seg, nxt_seg, nxt_width):
        count = len(placed)
        i = weights.shape[0] // 9

        def tap(value, a, bb):
            return value[(3 * a + bb) * i : (3 * a + bb + 1) * i]

        for a in range(3):
            for q in range(count):
                even = row0 + CELL * a + 2 * q * pitch
                e[even : even + i, seg : seg + CELL] = tap(placed[q], a, 1).astype(BF)
                odd = even + pitch
                value = tap(placed[q], a, 2)
                if q + 1 < count:
                    value = value + tap(placed[q + 1], a, 0)
                else:
                    e[odd : odd + i, nxt_seg : nxt_seg + nxt_width] = tap(weights, a, 0).astype(BF)
                e[odd : odd + i, seg : seg + CELL] = value.astype(BF)

    def fill_e3(kernels):
        for key, i, row0, pitch in kernels:
            r0 = ROW0[key]
            start = 124 + (r0 - 1986) // 16 if r0 >= 1986 else (r0 - 10) // 16
            for a in range(3):
                even = row0 + CELL * a
                odd = even + pitch
                for bb, at, seg in ((1, even, 0), (2, odd, 0), (0, odd, CELL)):
                    first = start + (3 * a + bb) * (i // 16)
                    for t in range(i // 16):
                        for jb in range(3):
                            e3[at + 16 * t : at + 16 * (t + 1), seg + 128 * jb : seg + 128 * (jb + 1)] = tile(
                                first + t, jb
                            )

    def fill_e2_21():
        w = rows_of((2, 1, 0), 432, 192)
        taps(e2, 0, 96, w, [place(w.astype(BF), 192, q, q + 1) for q in range(2)], 0, 384, 256)

    def fill_e2_31():
        w = rows_of((3, 1, 0), 216, 96)
        taps(e2, 0, 96, w, [place(w.astype(BF), 96, q, q + 1) for q in range(2)], 640, 1024, 128)

    def fill_e2_mid():
        w = rows_of((2, 0, 1), 216, 192)
        placed = [place(w.astype(BF), 192, q, q + 1) for q in range(2)]
        taps(e2, 1152, 96, w, placed, 0, 384, 256)
        w = rows_of((3, 0, 1), 54, 48)
        w_next = rows_of((3, 0, 1), 54, 48, 64)
        placed = [place(w.astype(BF), 48, 4 + q, 5 + q) for q in range(2)]
        taps(e2, 1152 + 48, 96, w_next, placed, 640, 1024 + 128, 128)

    def fill_e1_10():
        w = rows_of((1, 0, 0), 108, 96)
        taps(e1, 0, 48, w, [place(w.astype(BF), 96, q, q + 1) for q in range(4)], 0, 384, 128)

    def fill_e1_mid():
        w = rows_of((2, 0, 0), 54, 48) + 0.0
        w = w + rows_of((3, 0, 0), 54, 48, 48)
        taps(e1, 0, 48, w, [place(w.astype(BF), 96, q, q + 1) for q in range(4)], 512, 896, 128)

    def fill_up():
        u3[:, 0:384] = place(rows_of((0, 3, 0), 48, 48).astype(BF), 48, 0, 8).astype(BF)
        u3[:, 384:768] = place(rows_of((1, 3, 0), 96, 96).astype(BF), 96, 0, 4).astype(BF)
        u3[:, 768:1152] = place(rows_of((2, 3, 0), 192, 192).astype(BF), 192, 0, 2).astype(BF)
        w02 = rows_of((0, 2, 0), 24, 48).astype(BF)
        w12 = rows_of((1, 2, 0), 48, 96).astype(BF)
        for q in range(2):
            u2[192 * q : 192 * (q + 1), 0:384] = place(w02, 48, 4 * q, 4 * q + 4).astype(BF)
            u2[192 * q : 192 * (q + 1), 384:768] = place(w12, 96, 2 * q, 2 * q + 2).astype(BF)
        w01 = rows_of((0, 1, 0), 12, 48).astype(BF)
        for q in range(4):
            u1[96 * q : 96 * (q + 1), :] = place(w01, 48, 2 * q, 2 * q + 2).astype(BF)

    def reader(t, base):
        return lambda l, lo, hi: strip[t, l, base + lo : base + hi, :]

    def section_reader(buffer, t):
        return lambda l, lo, hi: buffer[t, l, lo:hi, :]

    def cells_of(read, total):
        return [read(l, 0, total) for l in range(3)]

    def shifted(read, rows, total, count):
        pieces = []
        for l in range(count):
            nxt[l, 0 : 8 * rows, :] = read(l, 1, 8 * rows + 1)
            for p in range(rows):
                nxt[l, 8 * p + 7 : 8 * p + 8, :] = read(l, 8 * rows + p, 8 * rows + p + 1)
            nxt[l, 8 * rows : total, :] = jnp.zeros((total - 8 * rows, 128), F32)
            pieces.append(nxt[l, 0:total, :])
        return pieces

    def lhs(pieces):
        return jnp.concatenate([piece.astype(BF) for piece in pieces], axis=1)

    def both(make):
        return jnp.concatenate([make(t) for t in range(2)], axis=0)

    def level_three(t):
        read = reader(t, C3)
        return lhs(cells_of(read, 32) + shifted(read, 2, 32, 3))

    def level_two(t):
        read = reader(t, C2)
        return lhs(cells_of(read, 32) + shifted(read, 3, 32, 2))

    def level_one(t):
        read = reader(t, C1)
        return lhs(cells_of(read, 48) + shifted(read, 5, 48, 1))

    def sums_of(t, *blocks):
        pieces = []
        for start, rows in blocks:
            pieces += [strip[t, l, SUMS + start : SUMS + start + rows, :] for l in range(3)]
        return lhs(pieces)

    def rows_out(y, a, lo, hi):
        return y[lo:hi, CELL * a : CELL * (a + 1)]

    def upsampled(y, p, base):
        lo = base + 8 * p
        even = rows_out(y, 1, lo, lo + 8)
        return even, rows_out(y, 2, lo, lo + 8) + rows_out(y, 0, lo + 8, lo + 16)

    def section(buffer, t, y, rows, y_base, kept):
        view = buffer.at[t]
        for p in range(rows):
            even, odd = upsampled(y, p, y_base)
            put(view, 16 * p, even)
            put(view, 16 * p + 8, odd)
        put(view, 16 * rows, rows_out(y, 1, y_base + 8 * rows, y_base + 8 * rows + 8))
        extra, base = 8 * (2 * rows + 1), y_base + 8 * (rows + 1)
        for p in range(rows + 1):
            put(view, extra + 2 * p, rows_out(y, 1, base + p, base + p + 1))
            if p < rows:
                odd = rows_out(y, 2, base + p, base + p + 1) + rows_out(y, 0, base + p + 1, base + p + 2)
                put(view, extra + 2 * p + 1, odd)
        for l in range(3):
            buffer[t, l] = jnp.where(strip[t, l, kept : kept + buffer.shape[2], :] > 0.5, buffer[t, l], 0.0)

    def direct():
        fill_e2_21()
        fill_e1_10()
        fill_up()
        fill_e3((((3, 2, 0), 192, 0, 192),))
        y3 = dot_nt(both(level_three), e3[0:1152, :])
        y2 = dot_nt(both(level_two), e2[0:1152, 0:640])
        y1 = dot_nt(both(level_one), e1[:, 0:512])
        x3 = dot_nt(both(lambda t: sums_of(t, (48, 8), (72, 8), (80, 8))), u3[...])
        x2 = dot_nt(both(lambda t: sums_of(t, (32, 16), (56, 16))), u2[...])
        x1 = dot_nt(both(lambda t: sums_of(t, (0, 32))), u1[...])
        for t in (1, 0):
            view = acc.at[t]
            for p in range(4):
                even, odd = upsampled(y1, p, 48 * t)
                put(view, 16 * p, even)
                put(view, 16 * p + 8, odd)
            for p in range(2):
                even, odd = upsampled(y2, p, 32 * t)
                put(view, 64 + 16 * p, even + x1[32 * t + 16 * p : 32 * t + 16 * p + 8])
                put(view, 72 + 16 * p, odd + x1[32 * t + 16 * p + 8 : 32 * t + 16 * p + 16])
            even, odd = upsampled(y3, 0, 32 * t)
            put(view, 96, even + x2[16 * t : 16 * t + 8])
            put(view, 104, odd + x2[16 * t + 8 : 16 * t + 16])
            put(view, 112, x3[8 * t : 8 * t + 8])

    def chained():
        fill_e2_31()
        fill_e2_mid()
        fill_e1_mid()
        fill_e3((((3, 1, 1), 96, 1152, 96), ((3, 0, 2), 48, 1152 + 192, 48)))
        y2_maps = dot_nt(both(level_two), e2[1152:2304, 0:640])
        y3 = dot_nt(both(level_three), e3[1152:2304, :])
        for t in range(2):
            section(sg2, t, y3, 1, 32 * t, K2)

        def grads_two(t):
            read = section_reader(sg2, t)
            return lhs(cells_of(read, 32) + shifted(read, 3, 32, 2))

        grads = both(grads_two)
        y2 = y2_maps + dot_nt(grads, e2[1152:2304, 640:1280])
        for t in range(2):
            section(sg1, t, y2, 2, 32 * t, K1)

        def grads_one(t):
            read = section_reader(sg1, t)
            return lhs(cells_of(read, 48) + shifted(read, 5, 48, 1))

        y1 = dot_nt(both(grads_one), e1[:, 512:1024])
        y2 = dot_nt(grads, e2[0:1152, 640:1280])
        for t in (1, 0):
            view = acc.at[t]
            for p in range(4):
                even, odd = upsampled(y1, p, 48 * t)
                put(view, 16 * p, even)
                put(view, 16 * p + 8, odd)
            for p in range(2):
                even, odd = upsampled(y2, p, 32 * t)
                put(view, 64 + 16 * p, even)
                put(view, 72 + 16 * p, odd)

    def emit(ref, rows, base, maps_of):
        for l in range(3):
            out[l, 0 : 8 * rows, :] = (
                maps_of[l, 0 : 8 * rows, :] + acc[0, l, base : base + 8 * rows, :] + acc_in[l, base : base + 8 * rows, :]
            )
        for cell in range(8):
            for l in range(3):
                lane0 = CELL * cell + 128 * l
                if rows == 1:
                    piece = out[l, cell : cell + 1, :]
                else:
                    piece = out[l, pl.ds(cell, rows, stride=8), :]
                ref[:, lane0 : lane0 + 128] = piece.astype(BF)

    class Part:
        def __init__(self, s, lo, size, sem):
            self.s, self.lo, self.size, self.used = s, lo, size, sem
            self.u, self.v = (b, y) if s == 0 else (y, b)
            self.pending, self.second = [], []

        def holds(self, x_of):
            return (x_of != 3) | (c == self.s)

        def send(self, ref, x_to, tile_to, x_of=None):
            copy = remote(ref, ref, s_send.at[self.used], s_recv.at[self.used], x_to, tile_to)
            self.used += 1
            self.pending.append((copy, x_of))
            self.when(x_of, copy.start)
            return copy

        def when(self, x_of, act):
            if x_of is None:
                act()
            else:
                pl.when(self.holds(x_of))(act)

        def send_bundle(self, u_of, to_u, to_v):
            zs = pl.ds(self.lo, self.size)
            if self.s == 0:
                return self.send(tiles.at[0, u_of, y, c, zs], to_u, tile_of(z, to_v, c), u_of)
            return self.send(tiles.at[1, b, u_of, c, zs], to_v, tile_of(z, to_u, c), b)

        def spread(self, u_of):
            self.second.append((u_of, [(d, self.send_bundle(u_of, self.u, wrap(self.v + d, 4))) for d in (1, 3, 2)]))

        def start(self):
            self.first = [(d, self.send_bundle(self.u, wrap(self.u + d, 4), self.v)) for d in (1, 3, 2)]
            self.spread(self.u)

        def pass_on(self):
            for d, copy in self.first:
                u_of = wrap(self.u - d, 4)
                self.when(u_of if self.s == 0 else b, copy.wait_recv)
                self.spread(u_of)

        def cross(self):
            zs = pl.ds(self.lo, self.size)
            self.across = []
            for u_of, copies_in in self.second:
                for d, copy in copies_in:
                    self.when(u_of if self.s == 0 else wrap(b - d, 4), copy.wait_recv)
                ref = tiles.at[0, u_of, :, c, zs] if self.s == 0 else tiles.at[1, :, u_of, c, zs]
                self.across.append(self.send(ref, b, tile_of(z, y, 1 - c)))

        def arrived(self):
            for copy in self.across:
                copy.wait_recv()

        def sent(self):
            for copy, x_of in self.pending:
                self.when(x_of, copy.wait_send)

    parts = []
    for lo, size in Z_PARTS:
        for at in range(max(lo, 1), lo + size):
            copies[at].wait_recv()
        pair = [Part(s, lo, size, 19 * (len(parts) + s)) for s in range(2)]
        for part in pair:
            part.start()
        if lo == 0:
            own_maps()
        for part in pair:
            part.pass_on()
        parts += pair
    for part in parts:
        part.cross()
    strip_copy.wait_recv()
    for part in parts:
        part.arrived()
    pl.when(c == 0)(direct)
    pl.when(c == 1)(chained)
    acc_copy = remote(acc.at[1], acc_in, x_send.at[1], x_recv.at[1], b, tile_of(z, y, 1 - c))
    acc_copy.start()
    for part in parts:
        part.sent()
    for copy in list(copies.values()) + first + [strip_copy]:
        copy.wait_send()
    acc_copy.wait_recv()
    emit(o4, 1, 112, c3)
    emit(o3, 2, 96, c2)
    emit(o2, 4, 64, c1)
    emit(o1, 8, 0, c0)
    acc_copy.wait_send()


def finish_kernel(*refs):
    for n in range(4):
        refs[4 + n][...] = refs[n][...]


ANY = pl.BlockSpec(memory_space=pl.ANY)
VMEM = pl.BlockSpec(memory_space=pltpu.VMEM)
TILES = (2, 4, 4, 2, NZ, 16, 128)


def per_device(*operands):
    maps = operands[:12]

    def cells(rows):
        return pltpu.VMEM((3, rows, 128), F32)

    def buffer(*shape):
        return pltpu.VMEM(shape, BF)

    def sems(count):
        return pltpu.SemaphoreType.DMA((count,))

    results = [jax.ShapeDtypeStruct(g.shape, BF) for g in maps[:4]]
    done = pl.pallas_call(
        exchange_kernel,
        out_shape=results,
        in_specs=[ANY] * 13,
        out_specs=[VMEM] * 4,
        scratch_shapes=[buffer(*m.shape) for m in maps] + [
            buffer(SHARD),
            buffer(*TILES), buffer(48, CELL), buffer(32, CELL), buffer(32, CELL),
            buffer(RAW_ROWS, 128), buffer(RAW_ROWS, 128), buffer(RAW_ROWS, 128),
            pltpu.VMEM((RAW_ROWS, 128), F32), pltpu.VMEM((WINDOW, 128), F32),
            pltpu.VMEM((48, CELL), F32), pltpu.VMEM((32, CELL), F32), buffer(48, CELL), buffer(32, CELL),
            buffer(2304, 768), buffer(2304, 1280), buffer(1152, 1024),
            buffer(384, 1152), buffer(384, 768), buffer(384, 384),
            pltpu.VMEM((2, 1024, 128), F32), buffer(CELL, 4096), buffer(256, CELL * len(PLACES)),
            cells(64), cells(48), cells(32), cells(32),
            pltpu.VMEM((2, 3, 48, 128), F32), pltpu.VMEM((2, 3, 32, 128), F32),
            cells(32), cells(32), cells(16), cells(16), cells(48), cells(32), cells(32), cells(48), cells(64),
            pltpu.VMEM((2, 3, STRIP, 128), F32), pltpu.VMEM((2, 3, 120, 128), F32), cells(120),
            sems(13), sems(5), sems(5), sems(NZ - 1), sems(NZ - 1), sems(38 * len(Z_PARTS)), sems(38 * len(Z_PARTS)), sems(2), sems(2),
        ],
        compiler_params=pltpu.CompilerParams(
            collective_id=0, has_side_effects=True, vmem_limit_bytes=60 * 2**20
        ),
        name="exchange",
    )(*operands)
    return pl.pallas_call(
        finish_kernel,
        out_shape=results,
        in_specs=[VMEM] * 4,
        out_specs=[VMEM] * 4,
        compiler_params=pltpu.CompilerParams(vmem_limit_bytes=60 * 2**20),
        name="finish",
    )(*done)


def solution(mesh):
    maps = P("tile", "branch")
    return jax.shard_map(
        per_device, mesh=mesh, in_specs=(maps,) * 12 + (P("tile"),), out_specs=(maps,) * 4, check_vma=False
    )
```

```python
import jax
import jax.numpy as jnp
from jax import lax
from jax.experimental import pallas as pl
from jax.experimental.pallas import tpu as pltpu
from jax.sharding import PartitionSpec as P

BF = jnp.bfloat16
F32 = jnp.float32
MESH = pl.DeviceIdType.MESH
N_TILE = 128
N_BRANCH = 4
NZ = 16
Z_PARTS = ((0, 9), (9, 7))
SHARD = 13734
CELL = 384
RAW_ROWS = 112
FLAT_ROWS = 13744

C1, C2, C3, SUMS, K1, K2, STRIP = 0, 48, 80, 112, 200, 248, 280

ROW0 = {
    (0, 1, 0): 0,
    (0, 2, 0): 12,
    (0, 3, 0): 36,
    (1, 0, 0): 84,
    (1, 2, 0): 192,
    (1, 3, 0): 240,
    (2, 0, 0): 336,
    (2, 0, 1): 390,
    (2, 1, 0): 606,
    (2, 3, 0): 1038,
    (3, 0, 0): 1230,
    (3, 0, 1): 1284,
    (3, 0, 2): 1338,
    (3, 1, 0): 1770,
    (3, 1, 1): 1986,
    (3, 2, 0): 2850,
}


SPLITS = {(48, 0): 0, (48, 48): 1024, (48, 64): 2048, (96, 0): 3072, (192, 0): 3584}
PLACES = (
    [(48, 4 + q, 5 + q) for q in range(2)] + [(48, 0, 8), (48, 0, 4), (48, 4, 8)]
    + [(48, 2 * q, 2 * q + 2) for q in range(4)] + [(96, q, q + 1) for q in range(4)]
    + [(96, 0, 4), (96, 0, 2), (96, 2, 4), (192, 0, 1), (192, 1, 2), (192, 0, 2)]
)


def remote(src, dst, send, recv, branch, tile):
    return pltpu.make_async_remote_copy(
        src_ref=src, dst_ref=dst, send_sem=send, recv_sem=recv, device_id=(branch, tile), device_id_type=MESH
    )


def slots_of(k):
    return [(t % 2 if t < 6 else k % 2, t // 2, (k // 2) % 4, k % 2) for t in range(7)]


def dot(a, b):
    return lax.dot_general(a, b, (((1,), (0,)), ((), ())), preferred_element_type=F32)


def dot_nt(a, b):
    return lax.dot_general(a, b, (((1,), (1,)), ((), ())), preferred_element_type=F32)


def unit_matrix(rows, cols, target):
    column = lax.broadcasted_iota(jnp.int32, (1, cols), 1)
    row = lax.broadcasted_iota(jnp.int32, (rows, cols), 0)
    return jnp.where(row == target(column), 1.0, 0.0).astype(BF)


def exchange_kernel(
    *refs,
):
    inputs, outputs, refs = refs[:13], refs[13:17], refs[17:]
    loaded, refs = refs[:13], refs[13:]
    (
        tiles, row_in, col_in, corner_in, shard_f, flat, row_f, col_f, row_out, col_out,
        e3, e2, e1, u3, u2, u1, wide, splits, copies_of,
        c0, c1, c2, c3, sg1, sg2, q20, q30a, q30b, q31, k1, k2a, k2b, nxt, out, strip, acc, acc_in,
        l_sem, h_send, h_recv, z_send, z_recv, s_send, s_recv, x_send, x_recv,
    ) = refs
    g1, g2, g3, g4, p1, p2, p3, p4, m20, m30a, m30b, m31, shard_in = loaded
    o1, o2, o3, o4 = outputs
    b = lax.axis_index("branch")
    k = lax.axis_index("tile")
    z, y, c = k // 8, lax.rem(k // 2, 4), lax.rem(k, 2)
    has_row = k < N_TILE - 1
    has_col = b < N_BRANCH - 1

    loads = [pltpu.make_async_copy(inputs[n], loaded[n], l_sem.at[n]) for n in range(13)]
    for n in (12, 1, 2, 3, 5, 6, 7, 8, 9, 10, 11, 0, 4):
        loads[n].start()

    def tile_of(zz, yy, cc):
        return zz * 8 + yy * 2 + cc

    def wrap(value, count):
        return lax.rem(value + count, count)

    left, right = wrap(b - 1, N_BRANCH), wrap(b + 1, N_BRANCH)
    up1, down1 = wrap(k - 1, N_TILE), wrap(k + 1, N_TILE)

    partners = [
        (b, up1), (b, down1), (left, k), (right, k), (left, up1), (right, down1),
        (b, tile_of(z, y, 1 - c)), (wrap(b + 2, 4), k),
    ] + [(b, tile_of(z, wrap(y + d, 4), c)) for d in (1, 2, 3)]
    along_z = [1, -1, 2, -2, 3, -3, 4, -4]
    partners += [(b, tile_of(wrap(z + d, NZ), y, c)) for d in along_z]
    barrier = pltpu.get_barrier_semaphore()
    for who in partners:
        pl.semaphore_signal(barrier, inc=1, device_id=who, device_id_type=MESH)

    loads[12].wait()
    whole = SHARD // 1024 * 1024
    rest = SHARD // 128 * 128
    row_at = [n // 128 for n in (whole, rest)]
    shard_f[0 : row_at[0], :] = shard_in[0:whole].astype(F32).reshape(row_at[0], 128)
    shard_f[row_at[0] : row_at[1], :] = shard_in[whole:rest].astype(F32).reshape(row_at[1] - row_at[0], 128)
    shard_f[row_at[1] : RAW_ROWS, :] = jnp.zeros((RAW_ROWS - row_at[1], 128), F32)
    shard_f[row_at[1] : row_at[1] + 1, 0 : SHARD - rest] = shard_in[rest:SHARD].astype(F32).reshape(1, SHARD - rest)
    for s in range(2):
        row = jnp.where(b == 3, 96, 32 * b + 16 * s)
        tiles[s, b, y, c, 4] = shard_f[pl.ds(pl.multiple_of(row, 16), 16), :].astype(BF)

    pl.semaphore_wait(barrier, len(partners))
    near = []
    for n, d in enumerate(along_z):
        copy = remote(
            tiles.at[:, b, y, c, 4], tiles.at[:, b, y, c, 4 - d], z_send.at[n], z_recv.at[n],
            b, tile_of(wrap(z + d, NZ), y, c),
        )
        copy.start()
        near.append(copy)

    for load in loads[:12]:
        load.wait()
    row_f[...] = jnp.zeros_like(row_f)
    col_f[...] = jnp.zeros_like(col_f)
    at_row, at_col = 0, 0
    for g, p in ((g2, p2), (g3, p3), (g4, p4)):
        rows = g.shape[0]
        masked = jnp.where(p[...].astype(F32) > 0, g[...].astype(F32), 0.0)
        for cell in range(8):
            row_f[at_row + cell : at_row + cell + 1, :] = masked[0:1, CELL * cell : CELL * (cell + 1)]
        col_f[at_col : at_col + rows, :] = masked[:, 0:CELL]
        at_row, at_col = at_row + 8, at_col + rows
    for m, at_row, at_col in ((m20, 24, 8), (m30a, 28, 12), (m31, 32, 18), (m30b, 36, 16)):
        rows, units = m.shape[0], m.shape[1] // CELL
        value = m[...].astype(F32)
        for unit in range(units):
            row_f[at_row + unit : at_row + unit + 1, :] = value[0:1, CELL * unit : CELL * (unit + 1)]
        col_f[at_col : at_col + rows, :] = value[:, 0:CELL]
    row_out[...] = row_f[...].astype(BF)
    col_out[...] = col_f[...].astype(BF)

    first = [
        remote(row_out, row_in, h_send.at[0], h_recv.at[0], b, up1),
        remote(col_out, col_in, h_send.at[1], h_recv.at[1], left, k),
        remote(col_out, corner_in, h_send.at[2], h_recv.at[2], left, up1),
    ]
    for copy in first:
        copy.start()

    for (j, at), lanes in SPLITS.items():
        width = 256 if j == 192 else 128

        def split_target(col):
            part, lane = col // width, lax.rem(col, width) - at
            return jnp.where((lane >= 0) & (lane < j), part * j + lane, -1)

        splits[:, lanes : lanes + CELL // j * width] = unit_matrix(CELL, CELL // j * width, split_target)
    for number, (j, low, high) in enumerate(PLACES):

        def place_target(col):
            which = col // j
            return jnp.where((which >= low) & (which < high), lax.rem(col, j), -1)

        rows = 256 if j == 192 else 128
        copies_of[0:rows, CELL * number : CELL * (number + 1)] = unit_matrix(rows, CELL, place_target)

    for ref in (e3, e2, e1, c1, c2, c3, sg1, sg2, q20, q30a, q30b, q31, k1, k2a, k2b, nxt, acc):
        ref[...] = jnp.zeros_like(ref)

    def put(buffer, row, value):
        rows = value.shape[0]
        for l in range(3):
            buffer[l, row : row + rows, :] = value[:, 128 * l : 128 * (l + 1)]

    def spread_units(buffer, value, units):
        rows = value.shape[0]
        for unit in range(units):
            for l in range(3):
                piece = value[:, CELL * unit + 128 * l : CELL * unit + 128 * (l + 1)]
                if rows == 1:
                    buffer[l, unit : unit + 1, :] = piece
                else:
                    buffer[l, pl.ds(unit, rows, stride=units), :] = piece

    def masked(g, p):
        return jnp.where(p[...].astype(F32) > 0, g[...].astype(F32), 0.0)

    def flags(buffer):
        whole = jnp.concatenate([buffer[l] for l in range(3)], axis=1)
        return jnp.where(whole > 0, 1.0, 0.0).astype(BF)

    def target20(shift):
        def target(col):
            part, lane = col // CELL, lax.rem(col, CELL)
            pixel, channel = lane // 96, lax.rem(lane, 96) - shift
            return jnp.where((channel >= 0) & (channel < 48), part * 192 + pixel * 48 + channel, -1)

        return target

    def target31(col):
        part, lane = col // CELL, lax.rem(col, CELL)
        return jnp.where(lane < 192, part * 192 + lane, -1)

    def target30b(col):
        part, lane = col // CELL, lax.rem(col, CELL) - 192
        return jnp.where((lane >= 0) & (lane < 96), part * 96 + lane, -1)

    def keep(buffer, value, parts, count, extra_from, extra_rows, extra_to):
        for l in range(3):
            for part in range(parts):
                lanes = slice(part * CELL + 128 * l, part * CELL + 128 * (l + 1))
                buffer[l, pl.ds(part, count, stride=parts), :] = value[0:count, lanes]
            buffer[l, extra_to : extra_to + extra_rows, :] = value[
                extra_from : extra_from + extra_rows, 128 * l : 128 * (l + 1)
            ]

    def block_sums(buffer, rows, factor):
        groups = []
        for first in range(0, rows, factor):
            pieces = []
            for l in range(3):
                total = buffer[l, 8 * first : 8 * first + 8, :]
                for p in range(first + 1, first + factor):
                    total = total + buffer[l, 8 * p : 8 * p + 8, :]
                pieces.append(total)
            groups.append(jnp.concatenate(pieces, axis=1))
        return jnp.concatenate(groups, axis=0).astype(BF)

    def own_maps():
        spread_units(c0, masked(g1, p1), 8)
        for buffer, g, p in ((c1, g2, p2), (c2, g3, p3), (c3, g4, p4)):
            spread_units(buffer, masked(g, p), 8)
        for buffer, m, units in ((q20, m20, 4), (q30a, m30a, 4), (q31, m31, 4), (q30b, m30b, 2)):
            spread_units(buffer, m[...].astype(F32), units)

        for copy in first:
            copy.wait_recv()
        row_halo = row_in[...].astype(F32)
        col_halo = col_in[...].astype(F32)
        corner = corner_in[...].astype(F32)
        row_zero = jnp.where(has_row, row_halo, 0.0)
        col_zero = jnp.where(has_col, col_halo, 0.0)
        corner_zero = jnp.where(has_row & has_col, corner, 0.0)
        at = 0
        for buffer, rows, halo in ((c1, 4, 0), (c2, 2, 8), (c3, 1, 16)):
            put(buffer, 8 * rows, row_zero[halo : halo + 8])
            put(buffer, 8 * rows + 8, col_zero[at : at + rows])
            put(buffer, 8 * rows + 8 + rows, corner_zero[at : at + 1])
            at += rows
        for buffer, rows, units, halo, at in ((q20, 4, 4, 24, 8), (q30a, 4, 4, 28, 12), (q31, 2, 4, 32, 18), (q30b, 2, 2, 36, 16)):
            put(buffer, rows * units, row_halo[halo : halo + units])
            put(buffer, (rows + 1) * units, col_halo[at : at + rows])
            put(buffer, (rows + 1) * units + rows, corner[at : at + 1])

        mask1 = dot(flags(q20), unit_matrix(CELL, 768, target20(0))) + dot(
            flags(q30a), unit_matrix(CELL, 768, target20(48))
        )
        keep(k1, mask1, 2, 20, 20, 5, 40)
        keep(k2a, dot(flags(q31), unit_matrix(CELL, 768, target31)), 2, 12, 12, 3, 24)
        keep(k2b, dot(flags(q30b), unit_matrix(CELL, 1536, target30b)), 4, 6, 6, 3, 24)
        pooled = [block_sums(c0, 8, f) for f in (2, 4, 8)] + [block_sums(c1, 4, f) for f in (2, 4)] + [block_sums(c2, 2, 2)]
        for l in range(3):
            strip[0, l, C1 : C1 + 48, :] = c1[l]
            strip[0, l, C2 : C2 + 32, :] = c2[l]
            strip[0, l, C3 : C3 + 32, :] = c3[l]
            strip[0, l, K1 : K1 + 48, :] = k1[l]
            strip[0, l, K2 : K2 + 32, :] = k2a[l] + k2b[l]
        row = SUMS
        for value in pooled:
            rows = value.shape[0]
            for l in range(3):
                strip[0, l, row : row + rows, :] = value[:, 128 * l : 128 * (l + 1)].astype(F32)
            row += rows
        strip_copy.start()

    strip_copy = remote(
        strip.at[0], strip.at[1], x_send.at[0], x_recv.at[0], b, tile_of(z, y, 1 - c)
    )

    places = [lax.rem(zz - z + 4 + NZ, NZ) for zz in range(NZ)]
    lane_no = lax.broadcasted_iota(jnp.int32, (RAW_ROWS, 128), 1)

    def line_up(ranges):
        for shard in range(N_TILE):
            first_row, phase = divmod(SHARD * shard, 128)
            if not any(first_row < 3 * hi and first_row + 109 > 3 * lo for lo, hi in ranges):
                continue
            blocks = [tiles[s, x_at, y_at, c_at, places[shard // 8]] for s, x_at, y_at, c_at in slots_of(shard)]
            value = jnp.concatenate(blocks, axis=0).astype(F32)
            if phase == 0:
                flat[first_row : first_row + RAW_ROWS, :] = value
                continue
            value = pltpu.roll(value, phase, 1)
            pltpu.store(flat.at[first_row : first_row + RAW_ROWS, :], value, mask=lane_no >= phase)
            pltpu.store(flat.at[first_row + 1 : first_row + 1 + RAW_ROWS, :], value, mask=lane_no < phase)

    def load_rows(row, count):
        return [flat[pl.ds(3 * row + jb, count, stride=3), :].astype(BF) for jb in range(3)]

    def rows_of(key, rows, j, at=0):
        n = CELL // j
        width = 256 if j == 192 else 128

        lanes = SPLITS[j, at]
        whole = jnp.concatenate(load_rows(ROW0[key], rows), axis=1)
        split = dot(whole, splits[:, lanes : lanes + n * width])
        parts = []
        for half in range(width // 128):
            for part in range(n):
                wide[half, pl.ds(part, rows, stride=n), :] = split[
                    :, part * width + 128 * half : part * width + 128 * (half + 1)
                ]
            parts.append(wide[half, 0 : rows * n, :])
        return parts[0] if len(parts) == 1 else jnp.concatenate(parts, axis=1)

    def place(weights, j, low, high):
        lanes = CELL * PLACES.index((j, low, high))
        return dot(weights, copies_of[0 : weights.shape[1], lanes : lanes + CELL])

    def taps(e, row0, pitch, weights, placed, seg, nxt_seg, nxt_width):
        count = len(placed)
        i = weights.shape[0] // 9

        def tap(value, a, bb):
            return value[(3 * a + bb) * i : (3 * a + bb + 1) * i]

        for a in range(3):
            for q in range(count):
                even = row0 + CELL * a + 2 * q * pitch
                e[even : even + i, seg : seg + CELL] = tap(placed[q], a, 1).astype(BF)
                odd = even + pitch
                value = tap(placed[q], a, 2)
                if q + 1 < count:
                    value = value + tap(placed[q + 1], a, 0)
                else:
                    e[odd : odd + i, nxt_seg : nxt_seg + nxt_width] = tap(weights, a, 0).astype(BF)
                e[odd : odd + i, seg : seg + CELL] = value.astype(BF)

    def fill_e3(kernels):
        for key, i, row0, pitch in kernels:
            for a in range(3):
                even = row0 + CELL * a
                odd = even + pitch
                for bb, at, seg in ((1, even, 0), (2, odd, 0), (0, odd, CELL)):
                    for jb, piece in enumerate(load_rows(ROW0[key] + (3 * a + bb) * i, i)):
                        e3[at : at + i, seg + 128 * jb : seg + 128 * (jb + 1)] = piece

    def fill_e2_21():
        w = rows_of((2, 1, 0), 432, 192)
        taps(e2, 0, 96, w, [place(w.astype(BF), 192, q, q + 1) for q in range(2)], 0, 384, 256)

    def fill_e2_31():
        w = rows_of((3, 1, 0), 216, 96)
        taps(e2, 0, 96, w, [place(w.astype(BF), 96, q, q + 1) for q in range(2)], 640, 1024, 128)

    def fill_e2_mid():
        w = rows_of((2, 0, 1), 216, 192)
        placed = [place(w.astype(BF), 192, q, q + 1) for q in range(2)]
        taps(e2, 1152, 96, w, placed, 0, 384, 256)
        w = rows_of((3, 0, 1), 54, 48)
        w_next = rows_of((3, 0, 1), 54, 48, 64)
        placed = [place(w.astype(BF), 48, 4 + q, 5 + q) for q in range(2)]
        taps(e2, 1152 + 48, 96, w_next, placed, 640, 1024 + 128, 128)

    def fill_e1_10():
        w = rows_of((1, 0, 0), 108, 96)
        taps(e1, 0, 48, w, [place(w.astype(BF), 96, q, q + 1) for q in range(4)], 0, 384, 128)

    def fill_e1_mid():
        w = rows_of((2, 0, 0), 54, 48) + 0.0
        w = w + rows_of((3, 0, 0), 54, 48, 48)
        taps(e1, 0, 48, w, [place(w.astype(BF), 96, q, q + 1) for q in range(4)], 512, 896, 128)

    def fill_up():
        u3[:, 0:384] = place(rows_of((0, 3, 0), 48, 48).astype(BF), 48, 0, 8).astype(BF)
        u3[:, 384:768] = place(rows_of((1, 3, 0), 96, 96).astype(BF), 96, 0, 4).astype(BF)
        u3[:, 768:1152] = place(rows_of((2, 3, 0), 192, 192).astype(BF), 192, 0, 2).astype(BF)
        w02 = rows_of((0, 2, 0), 24, 48).astype(BF)
        w12 = rows_of((1, 2, 0), 48, 96).astype(BF)
        for q in range(2):
            u2[192 * q : 192 * (q + 1), 0:384] = place(w02, 48, 4 * q, 4 * q + 4).astype(BF)
            u2[192 * q : 192 * (q + 1), 384:768] = place(w12, 96, 2 * q, 2 * q + 2).astype(BF)
        w01 = rows_of((0, 1, 0), 12, 48).astype(BF)
        for q in range(4):
            u1[96 * q : 96 * (q + 1), :] = place(w01, 48, 2 * q, 2 * q + 2).astype(BF)

    def reader(t, base):
        return lambda l, lo, hi: strip[t, l, base + lo : base + hi, :]

    def section_reader(buffer, t):
        return lambda l, lo, hi: buffer[t, l, lo:hi, :]

    def cells_of(read, total):
        return [read(l, 0, total) for l in range(3)]

    def shifted(read, rows, total, count):
        pieces = []
        for l in range(count):
            nxt[l, 0 : 8 * rows, :] = read(l, 1, 8 * rows + 1)
            for p in range(rows):
                nxt[l, 8 * p + 7 : 8 * p + 8, :] = read(l, 8 * rows + p, 8 * rows + p + 1)
            nxt[l, 8 * rows : total, :] = jnp.zeros((total - 8 * rows, 128), F32)
            pieces.append(nxt[l, 0:total, :])
        return pieces

    def lhs(pieces):
        return jnp.concatenate([piece.astype(BF) for piece in pieces], axis=1)

    def both(make):
        return jnp.concatenate([make(t) for t in range(2)], axis=0)

    def level_three(t):
        read = reader(t, C3)
        return lhs(cells_of(read, 32) + shifted(read, 2, 32, 3))

    def level_two(t):
        read = reader(t, C2)
        return lhs(cells_of(read, 32) + shifted(read, 3, 32, 2))

    def level_one(t):
        read = reader(t, C1)
        return lhs(cells_of(read, 48) + shifted(read, 5, 48, 1))

    def sums_of(t, *blocks):
        pieces = []
        for start, rows in blocks:
            pieces += [strip[t, l, SUMS + start : SUMS + start + rows, :] for l in range(3)]
        return lhs(pieces)

    def rows_out(y, a, lo, hi):
        return y[lo:hi, CELL * a : CELL * (a + 1)]

    def upsampled(y, p, base):
        lo = base + 8 * p
        even = rows_out(y, 1, lo, lo + 8)
        return even, rows_out(y, 2, lo, lo + 8) + rows_out(y, 0, lo + 8, lo + 16)

    def section(buffer, t, y, rows, y_base, kept):
        view = buffer.at[t]
        for p in range(rows):
            even, odd = upsampled(y, p, y_base)
            put(view, 16 * p, even)
            put(view, 16 * p + 8, odd)
        put(view, 16 * rows, rows_out(y, 1, y_base + 8 * rows, y_base + 8 * rows + 8))
        extra, base = 8 * (2 * rows + 1), y_base + 8 * (rows + 1)
        for p in range(rows + 1):
            put(view, extra + 2 * p, rows_out(y, 1, base + p, base + p + 1))
            if p < rows:
                odd = rows_out(y, 2, base + p, base + p + 1) + rows_out(y, 0, base + p + 1, base + p + 2)
                put(view, extra + 2 * p + 1, odd)
        for l in range(3):
            buffer[t, l] = jnp.where(strip[t, l, kept : kept + buffer.shape[2], :] > 0.5, buffer[t, l], 0.0)

    def direct():
        line_up(((0, 336), (606, 1230), (2850, 4578)))
        fill_e2_21()
        fill_e1_10()
        fill_up()
        fill_e3((((3, 2, 0), 192, 0, 192),))
        y3 = dot_nt(both(level_three), e3[0:1152, :])
        y2 = dot_nt(both(level_two), e2[0:1152, 0:640])
        y1 = dot_nt(both(level_one), e1[:, 0:512])
        x3 = dot_nt(both(lambda t: sums_of(t, (48, 8), (72, 8), (80, 8))), u3[...])
        x2 = dot_nt(both(lambda t: sums_of(t, (32, 16), (56, 16))), u2[...])
        x1 = dot_nt(both(lambda t: sums_of(t, (0, 32))), u1[...])
        for t in (1, 0):
            view = acc.at[t]
            for p in range(4):
                even, odd = upsampled(y1, p, 48 * t)
                put(view, 16 * p, even)
                put(view, 16 * p + 8, odd)
            for p in range(2):
                even, odd = upsampled(y2, p, 32 * t)
                put(view, 64 + 16 * p, even + x1[32 * t + 16 * p : 32 * t + 16 * p + 8])
                put(view, 72 + 16 * p, odd + x1[32 * t + 16 * p + 8 : 32 * t + 16 * p + 16])
            even, odd = upsampled(y3, 0, 32 * t)
            put(view, 96, even + x2[16 * t : 16 * t + 8])
            put(view, 104, odd + x2[16 * t + 8 : 16 * t + 16])
            put(view, 112, x3[8 * t : 8 * t + 8])

    def chained():
        line_up(((336, 606), (1230, 2850)))
        fill_e2_31()
        fill_e2_mid()
        fill_e1_mid()
        fill_e3((((3, 1, 1), 96, 1152, 96), ((3, 0, 2), 48, 1152 + 192, 48)))
        y2_maps = dot_nt(both(level_two), e2[1152:2304, 0:640])
        y3 = dot_nt(both(level_three), e3[1152:2304, :])
        for t in range(2):
            section(sg2, t, y3, 1, 32 * t, K2)

        def grads_two(t):
            read = section_reader(sg2, t)
            return lhs(cells_of(read, 32) + shifted(read, 3, 32, 2))

        grads = both(grads_two)
        y2 = y2_maps + dot_nt(grads, e2[1152:2304, 640:1280])
        for t in range(2):
            section(sg1, t, y2, 2, 32 * t, K1)

        def grads_one(t):
            read = section_reader(sg1, t)
            return lhs(cells_of(read, 48) + shifted(read, 5, 48, 1))

        y1 = dot_nt(both(grads_one), e1[:, 512:1024])
        y2 = dot_nt(grads, e2[0:1152, 640:1280])
        for t in (1, 0):
            view = acc.at[t]
            for p in range(4):
                even, odd = upsampled(y1, p, 48 * t)
                put(view, 16 * p, even)
                put(view, 16 * p + 8, odd)
            for p in range(2):
                even, odd = upsampled(y2, p, 32 * t)
                put(view, 64 + 16 * p, even)
                put(view, 72 + 16 * p, odd)

    def emit(ref, rows, base, maps_of):
        for l in range(3):
            out[l, 0 : 8 * rows, :] = (
                maps_of[l, 0 : 8 * rows, :] + acc[0, l, base : base + 8 * rows, :] + acc_in[l, base : base + 8 * rows, :]
            )
        for cell in range(8):
            for l in range(3):
                lane0 = CELL * cell + 128 * l
                if rows == 1:
                    piece = out[l, cell : cell + 1, :]
                else:
                    piece = out[l, pl.ds(cell, rows, stride=8), :]
                ref[:, lane0 : lane0 + 128] = piece.astype(BF)

    class Part:
        def __init__(self, s, lo, size, sem):
            self.s, self.lo, self.size, self.used = s, lo, size, sem
            self.u, self.v = (b, y) if s == 0 else (y, b)
            self.pending, self.second = [], []

        def holds(self, x_of):
            return (x_of != 3) | (c == self.s)

        def send(self, ref, x_to, tile_to, x_of=None):
            copy = remote(ref, ref, s_send.at[self.used], s_recv.at[self.used], x_to, tile_to)
            self.used += 1
            self.pending.append((copy, x_of))
            self.when(x_of, copy.start)
            return copy

        def when(self, x_of, act):
            if x_of is None:
                act()
            else:
                pl.when(self.holds(x_of))(act)

        def send_bundle(self, u_of, to_u, to_v):
            zs = pl.ds(self.lo, self.size)
            if self.s == 0:
                return self.send(tiles.at[0, u_of, y, c, zs], to_u, tile_of(z, to_v, c), u_of)
            return self.send(tiles.at[1, b, u_of, c, zs], to_v, tile_of(z, to_u, c), b)

        def spread(self, u_of):
            self.second.append((u_of, [(d, self.send_bundle(u_of, self.u, wrap(self.v + d, 4))) for d in (1, 3, 2)]))

        def start(self):
            self.first = [(d, self.send_bundle(self.u, wrap(self.u + d, 4), self.v)) for d in (1, 3, 2)]
            self.spread(self.u)

        def pass_on(self):
            for d, copy in self.first:
                u_of = wrap(self.u - d, 4)
                self.when(u_of if self.s == 0 else b, copy.wait_recv)
                self.spread(u_of)

        def cross(self):
            zs = pl.ds(self.lo, self.size)
            self.across = []
            for u_of, copies_in in self.second:
                for d, copy in copies_in:
                    self.when(u_of if self.s == 0 else wrap(b - d, 4), copy.wait_recv)
                ref = tiles.at[0, u_of, :, c, zs] if self.s == 0 else tiles.at[1, :, u_of, c, zs]
                self.across.append(self.send(ref, b, tile_of(z, y, 1 - c)))

        def arrived(self):
            for copy in self.across:
                copy.wait_recv()

        def sent(self):
            for copy, x_of in self.pending:
                self.when(x_of, copy.wait_send)

    for copy in near:
        copy.wait_recv()
    far = [
        remote(
            tiles.at[:, b, y, c, pl.ds(lo, size)], tiles.at[:, b, y, c, pl.ds(to, size)], z_send.at[8 + n], z_recv.at[8 + n],
            b, tile_of(wrap(z + d, NZ), y, c),
        )
        for n, (lo, size, to, d) in enumerate(((5, 4, 9, -4), (1, 3, 13, 4)))
    ]
    for copy in far:
        copy.start()
    parts = [Part(s, lo, size, 19 * (2 * n + s)) for n, (lo, size) in enumerate(Z_PARTS) for s in range(2)]
    for part in parts[:2]:
        part.start()
    own_maps()
    for part in parts[:2]:
        part.pass_on()
    for copy in far:
        copy.wait_recv()
    for part in parts[2:]:
        part.start()
    for part in parts[2:]:
        part.pass_on()
    for part in parts:
        part.cross()
    strip_copy.wait_recv()
    for part in parts:
        part.arrived()
    pl.when(c == 0)(direct)
    pl.when(c == 1)(chained)
    acc_copy = remote(acc.at[1], acc_in, x_send.at[1], x_recv.at[1], b, tile_of(z, y, 1 - c))
    acc_copy.start()
    for part in parts:
        part.sent()
    for copy in near + far + first + [strip_copy]:
        copy.wait_send()
    acc_copy.wait_recv()
    emit(o4, 1, 112, c3)
    emit(o3, 2, 96, c2)
    emit(o2, 4, 64, c1)
    emit(o1, 8, 0, c0)
    acc_copy.wait_send()


def finish_kernel(*refs):
    for n in range(4):
        refs[4 + n][...] = refs[n][...]


ANY = pl.BlockSpec(memory_space=pl.ANY)
VMEM = pl.BlockSpec(memory_space=pltpu.VMEM)
TILES = (2, 4, 4, 2, NZ, 16, 128)


def per_device(*operands):
    maps = operands[:12]

    def cells(rows):
        return pltpu.VMEM((3, rows, 128), F32)

    def buffer(*shape):
        return pltpu.VMEM(shape, BF)

    def sems(count):
        return pltpu.SemaphoreType.DMA((count,))

    results = [jax.ShapeDtypeStruct(g.shape, BF) for g in maps[:4]]
    done = pl.pallas_call(
        exchange_kernel,
        out_shape=results,
        in_specs=[ANY] * 13,
        out_specs=[VMEM] * 4,
        scratch_shapes=[buffer(*m.shape) for m in maps] + [
            buffer(SHARD),
            buffer(*TILES), buffer(48, CELL), buffer(32, CELL), buffer(32, CELL),
            pltpu.VMEM((RAW_ROWS, 128), F32), pltpu.VMEM((FLAT_ROWS, 128), F32),
            pltpu.VMEM((48, CELL), F32), pltpu.VMEM((32, CELL), F32), buffer(48, CELL), buffer(32, CELL),
            buffer(2304, 768), buffer(2304, 1280), buffer(1152, 1024),
            buffer(384, 1152), buffer(384, 768), buffer(384, 384),
            pltpu.VMEM((2, 1024, 128), F32), buffer(CELL, 4096), buffer(256, CELL * len(PLACES)),
            cells(64), cells(48), cells(32), cells(32),
            pltpu.VMEM((2, 3, 48, 128), F32), pltpu.VMEM((2, 3, 32, 128), F32),
            cells(32), cells(32), cells(16), cells(16), cells(48), cells(32), cells(32), cells(48), cells(64),
            pltpu.VMEM((2, 3, STRIP, 128), F32), pltpu.VMEM((2, 3, 120, 128), F32), cells(120),
            sems(13), sems(3), sems(3), sems(10), sems(10), sems(38 * len(Z_PARTS)), sems(38 * len(Z_PARTS)), sems(2), sems(2),
        ],
        compiler_params=pltpu.CompilerParams(
            collective_id=0, has_side_effects=True, vmem_limit_bytes=60 * 2**20
        ),
        name="exchange",
    )(*operands)
    return pl.pallas_call(
        finish_kernel,
        out_shape=results,
        in_specs=[VMEM] * 4,
        out_specs=[VMEM] * 4,
        compiler_params=pltpu.CompilerParams(vmem_limit_bytes=60 * 2**20),
        name="finish",
    )(*done)


def solution(mesh):
    maps = P("tile", "branch")
    return jax.shard_map(
        per_device, mesh=mesh, in_specs=(maps,) * 12 + (P("tile"),), out_specs=(maps,) * 4, check_vma=False
    )
```

```python
import jax
import jax.numpy as jnp
from jax import lax
from jax.experimental import pallas as pl
from jax.experimental.pallas import tpu as pltpu
from jax.sharding import PartitionSpec as P

BF = jnp.bfloat16
F32 = jnp.float32
MESH = pl.DeviceIdType.MESH
N_TILE = 128
N_BRANCH = 4
NZ = 16
Z_PARTS = ((0, 9), (9, 7))
SHARD = 13734
CELL = 384
RAW_ROWS = 112
FLAT_ROWS = 13744

C1, C2, C3, SUMS, K1, K2, STRIP = 0, 48, 80, 112, 200, 248, 280

ROW0 = {
    (0, 1, 0): 0,
    (0, 2, 0): 12,
    (0, 3, 0): 36,
    (1, 0, 0): 84,
    (1, 2, 0): 192,
    (1, 3, 0): 240,
    (2, 0, 0): 336,
    (2, 0, 1): 390,
    (2, 1, 0): 606,
    (2, 3, 0): 1038,
    (3, 0, 0): 1230,
    (3, 0, 1): 1284,
    (3, 0, 2): 1338,
    (3, 1, 0): 1770,
    (3, 1, 1): 1986,
    (3, 2, 0): 2850,
}


SPLITS = {(48, 0): 0, (48, 48): 1024, (48, 64): 2048, (96, 0): 3072, (192, 0): 3584}
PLACES = (
    [(48, 4 + q, 5 + q) for q in range(2)] + [(48, 0, 8), (48, 0, 4), (48, 4, 8)]
    + [(48, 2 * q, 2 * q + 2) for q in range(4)] + [(96, q, q + 1) for q in range(4)]
    + [(96, 0, 4), (96, 0, 2), (96, 2, 4), (192, 0, 1), (192, 1, 2), (192, 0, 2)]
)


def remote(src, dst, send, recv, branch, tile):
    return pltpu.make_async_remote_copy(
        src_ref=src, dst_ref=dst, send_sem=send, recv_sem=recv, device_id=(branch, tile), device_id_type=MESH
    )


def slots_of(k):
    return [(t % 2 if t < 6 else k % 2, t // 2, (k // 2) % 4, k % 2) for t in range(7)]


def dot(a, b):
    return lax.dot_general(a, b, (((1,), (0,)), ((), ())), preferred_element_type=F32)


def dot_nt(a, b):
    return lax.dot_general(a, b, (((1,), (1,)), ((), ())), preferred_element_type=F32)


def unit_matrix(rows, cols, target):
    column = lax.broadcasted_iota(jnp.int32, (1, cols), 1)
    row = lax.broadcasted_iota(jnp.int32, (rows, cols), 0)
    return jnp.where(row == target(column), 1.0, 0.0).astype(BF)


def exchange_kernel(
    *refs,
):
    inputs, outputs, refs = refs[:13], refs[13:17], refs[17:]
    loaded, refs = refs[:13], refs[13:]
    (
        tiles, row_in, col_in, corner_in, shard_f, flat, row_f, col_f, row_out, col_out,
        e3, e2, e1, u3, u2, u1, wide, splits, copies_of,
        c0, c1, c2, c3, sg1, sg2, q20, q30a, q30b, q31, k1, k2a, k2b, nxt, out, strip, acc, acc_in,
        l_sem, h_send, h_recv, z_send, z_recv, s_send, s_recv, x_send, x_recv,
    ) = refs
    g1, g2, g3, g4, p1, p2, p3, p4, m20, m30a, m30b, m31, shard_in = loaded
    o1, o2, o3, o4 = outputs
    b = lax.axis_index("branch")
    k = lax.axis_index("tile")
    z, y, c = k // 8, lax.rem(k // 2, 4), lax.rem(k, 2)
    has_row = k < N_TILE - 1
    has_col = b < N_BRANCH - 1

    loads = [pltpu.make_async_copy(inputs[n], loaded[n], l_sem.at[n]) for n in range(13)]
    loads[12].start()

    def tile_of(zz, yy, cc):
        return zz * 8 + yy * 2 + cc

    def wrap(value, count):
        return lax.rem(value + count, count)

    left, right = wrap(b - 1, N_BRANCH), wrap(b + 1, N_BRANCH)
    up1, down1 = wrap(k - 1, N_TILE), wrap(k + 1, N_TILE)

    partners = [
        (b, up1), (b, down1), (left, k), (right, k), (left, up1), (right, down1),
        (b, tile_of(z, y, 1 - c)), (wrap(b + 2, 4), k),
    ] + [(b, tile_of(z, wrap(y + d, 4), c)) for d in (1, 2, 3)]
    along_z = [1, -1, 2, -2, 3, -3, 4, -4]
    partners += [(b, tile_of(wrap(z + d, NZ), y, c)) for d in along_z]
    barrier = pltpu.get_barrier_semaphore()
    for who in partners:
        pl.semaphore_signal(barrier, inc=1, device_id=who, device_id_type=MESH)
    for n in (1, 2, 3, 5, 6, 7, 8, 9, 10, 11, 0, 4):
        loads[n].start()

    loads[12].wait()
    whole = SHARD // 1024 * 1024
    rest = SHARD // 128 * 128
    row_at = [n // 128 for n in (whole, rest)]
    shard_f[0 : row_at[0], :] = shard_in[0:whole].astype(F32).reshape(row_at[0], 128)
    shard_f[row_at[0] : row_at[1], :] = shard_in[whole:rest].astype(F32).reshape(row_at[1] - row_at[0], 128)
    shard_f[row_at[1] : RAW_ROWS, :] = jnp.zeros((RAW_ROWS - row_at[1], 128), F32)
    shard_f[row_at[1] : row_at[1] + 1, 0 : SHARD - rest] = shard_in[rest:SHARD].astype(F32).reshape(1, SHARD - rest)
    for s in range(2):
        row = jnp.where(b == 3, 96, 32 * b + 16 * s)
        tiles[s, b, y, c, 4] = shard_f[pl.ds(pl.multiple_of(row, 16), 16), :].astype(BF)

    pl.semaphore_wait(barrier, len(partners))
    near = []
    for n, d in enumerate(along_z):
        copy = remote(
            tiles.at[:, b, y, c, 4], tiles.at[:, b, y, c, 4 - d], z_send.at[n], z_recv.at[n],
            b, tile_of(wrap(z + d, NZ), y, c),
        )
        copy.start()
        near.append(copy)

    for load in loads[:12]:
        load.wait()
    row_f[...] = jnp.zeros_like(row_f)
    col_f[...] = jnp.zeros_like(col_f)
    at_row, at_col = 0, 0
    for g, p in ((g2, p2), (g3, p3), (g4, p4)):
        rows = g.shape[0]
        masked = jnp.where(p[...].astype(F32) > 0, g[...].astype(F32), 0.0)
        for cell in range(8):
            row_f[at_row + cell : at_row + cell + 1, :] = masked[0:1, CELL * cell : CELL * (cell + 1)]
        col_f[at_col : at_col + rows, :] = masked[:, 0:CELL]
        at_row, at_col = at_row + 8, at_col + rows
    for m, at_row, at_col in ((m20, 24, 8), (m30a, 28, 12), (m31, 32, 18), (m30b, 36, 16)):
        rows, units = m.shape[0], m.shape[1] // CELL
        value = m[...].astype(F32)
        for unit in range(units):
            row_f[at_row + unit : at_row + unit + 1, :] = value[0:1, CELL * unit : CELL * (unit + 1)]
        col_f[at_col : at_col + rows, :] = value[:, 0:CELL]
    row_out[...] = row_f[...].astype(BF)
    col_out[...] = col_f[...].astype(BF)

    first = [
        remote(row_out, row_in, h_send.at[0], h_recv.at[0], b, up1),
        remote(col_out, col_in, h_send.at[1], h_recv.at[1], left, k),
        remote(col_out, corner_in, h_send.at[2], h_recv.at[2], left, up1),
    ]
    for copy in first:
        copy.start()

    for ref in (e3, e2, e1, c1, c2, c3, sg1, sg2, q20, q30a, q30b, q31, k1, k2a, k2b, nxt, acc):
        ref[...] = jnp.zeros_like(ref)

    def put(buffer, row, value):
        rows = value.shape[0]
        for l in range(3):
            buffer[l, row : row + rows, :] = value[:, 128 * l : 128 * (l + 1)]

    def spread_units(buffer, value, units):
        rows = value.shape[0]
        for unit in range(units):
            for l in range(3):
                piece = value[:, CELL * unit + 128 * l : CELL * unit + 128 * (l + 1)]
                if rows == 1:
                    buffer[l, unit : unit + 1, :] = piece
                else:
                    buffer[l, pl.ds(unit, rows, stride=units), :] = piece

    def masked(g, p):
        return jnp.where(p[...].astype(F32) > 0, g[...].astype(F32), 0.0)

    def flags(buffer):
        whole = jnp.concatenate([buffer[l] for l in range(3)], axis=1)
        return jnp.where(whole > 0, 1.0, 0.0).astype(BF)

    def target20(shift):
        def target(col):
            part, lane = col // CELL, lax.rem(col, CELL)
            pixel, channel = lane // 96, lax.rem(lane, 96) - shift
            return jnp.where((channel >= 0) & (channel < 48), part * 192 + pixel * 48 + channel, -1)

        return target

    def target31(col):
        part, lane = col // CELL, lax.rem(col, CELL)
        return jnp.where(lane < 192, part * 192 + lane, -1)

    def target30b(col):
        part, lane = col // CELL, lax.rem(col, CELL) - 192
        return jnp.where((lane >= 0) & (lane < 96), part * 96 + lane, -1)

    def keep(buffer, value, parts, count, extra_from, extra_rows, extra_to):
        for l in range(3):
            for part in range(parts):
                lanes = slice(part * CELL + 128 * l, part * CELL + 128 * (l + 1))
                buffer[l, pl.ds(part, count, stride=parts), :] = value[0:count, lanes]
            buffer[l, extra_to : extra_to + extra_rows, :] = value[
                extra_from : extra_from + extra_rows, 128 * l : 128 * (l + 1)
            ]

    def block_sums(buffer, rows, factor):
        groups = []
        for first in range(0, rows, factor):
            pieces = []
            for l in range(3):
                total = buffer[l, 8 * first : 8 * first + 8, :]
                for p in range(first + 1, first + factor):
                    total = total + buffer[l, 8 * p : 8 * p + 8, :]
                pieces.append(total)
            groups.append(jnp.concatenate(pieces, axis=1))
        return jnp.concatenate(groups, axis=0).astype(BF)

    def own_maps():
        spread_units(c0, masked(g1, p1), 8)
        for buffer, g, p in ((c1, g2, p2), (c2, g3, p3), (c3, g4, p4)):
            spread_units(buffer, masked(g, p), 8)
        for buffer, m, units in ((q20, m20, 4), (q30a, m30a, 4), (q31, m31, 4), (q30b, m30b, 2)):
            spread_units(buffer, m[...].astype(F32), units)

        for copy in first:
            copy.wait_recv()
        row_halo = row_in[...].astype(F32)
        col_halo = col_in[...].astype(F32)
        corner = corner_in[...].astype(F32)
        row_zero = jnp.where(has_row, row_halo, 0.0)
        col_zero = jnp.where(has_col, col_halo, 0.0)
        corner_zero = jnp.where(has_row & has_col, corner, 0.0)
        at = 0
        for buffer, rows, halo in ((c1, 4, 0), (c2, 2, 8), (c3, 1, 16)):
            put(buffer, 8 * rows, row_zero[halo : halo + 8])
            put(buffer, 8 * rows + 8, col_zero[at : at + rows])
            put(buffer, 8 * rows + 8 + rows, corner_zero[at : at + 1])
            at += rows
        for buffer, rows, units, halo, at in ((q20, 4, 4, 24, 8), (q30a, 4, 4, 28, 12), (q31, 2, 4, 32, 18), (q30b, 2, 2, 36, 16)):
            put(buffer, rows * units, row_halo[halo : halo + units])
            put(buffer, (rows + 1) * units, col_halo[at : at + rows])
            put(buffer, (rows + 1) * units + rows, corner[at : at + 1])

        mask1 = dot(flags(q20), unit_matrix(CELL, 768, target20(0))) + dot(
            flags(q30a), unit_matrix(CELL, 768, target20(48))
        )
        keep(k1, mask1, 2, 20, 20, 5, 40)
        keep(k2a, dot(flags(q31), unit_matrix(CELL, 768, target31)), 2, 12, 12, 3, 24)
        keep(k2b, dot(flags(q30b), unit_matrix(CELL, 1536, target30b)), 4, 6, 6, 3, 24)
        pooled = [block_sums(c0, 8, f) for f in (2, 4, 8)] + [block_sums(c1, 4, f) for f in (2, 4)] + [block_sums(c2, 2, 2)]
        for l in range(3):
            strip[0, l, C1 : C1 + 48, :] = c1[l]
            strip[0, l, C2 : C2 + 32, :] = c2[l]
            strip[0, l, C3 : C3 + 32, :] = c3[l]
            strip[0, l, K1 : K1 + 48, :] = k1[l]
            strip[0, l, K2 : K2 + 32, :] = k2a[l] + k2b[l]
        row = SUMS
        for value in pooled:
            rows = value.shape[0]
            for l in range(3):
                strip[0, l, row : row + rows, :] = value[:, 128 * l : 128 * (l + 1)].astype(F32)
            row += rows
        strip_copy.start()

    strip_copy = remote(
        strip.at[0], strip.at[1], x_send.at[0], x_recv.at[0], b, tile_of(z, y, 1 - c)
    )

    places = [lax.rem(zz - z + 4 + NZ, NZ) for zz in range(NZ)]
    lane_no = lax.broadcasted_iota(jnp.int32, (RAW_ROWS, 128), 1)

    def line_up(ranges):
        for shard in range(N_TILE):
            first_row, phase = divmod(SHARD * shard, 128)
            if not any(first_row < 3 * hi and first_row + 109 > 3 * lo for lo, hi in ranges):
                continue
            blocks = [tiles[s, x_at, y_at, c_at, places[shard // 8]] for s, x_at, y_at, c_at in slots_of(shard)]
            value = jnp.concatenate(blocks, axis=0).astype(F32)
            if phase == 0:
                flat[first_row : first_row + RAW_ROWS, :] = value
                continue
            value = pltpu.roll(value, phase, 1)
            pltpu.store(flat.at[first_row : first_row + RAW_ROWS, :], value, mask=lane_no >= phase)
            pltpu.store(flat.at[first_row + 1 : first_row + 1 + RAW_ROWS, :], value, mask=lane_no < phase)

    def load_rows(row, count):
        return [flat[pl.ds(3 * row + jb, count, stride=3), :].astype(BF) for jb in range(3)]

    def rows_of(key, rows, j, at=0):
        n = CELL // j
        width = 256 if j == 192 else 128

        lanes = SPLITS[j, at]
        whole = jnp.concatenate(load_rows(ROW0[key], rows), axis=1)
        split = dot(whole, splits[:, lanes : lanes + n * width])
        parts = []
        for half in range(width // 128):
            for part in range(n):
                wide[half, pl.ds(part, rows, stride=n), :] = split[
                    :, part * width + 128 * half : part * width + 128 * (half + 1)
                ]
            parts.append(wide[half, 0 : rows * n, :])
        return parts[0] if len(parts) == 1 else jnp.concatenate(parts, axis=1)

    def place(weights, j, low, high):
        lanes = CELL * PLACES.index((j, low, high))
        return dot(weights, copies_of[0 : weights.shape[1], lanes : lanes + CELL])

    def taps(e, row0, pitch, weights, placed, seg, nxt_seg, nxt_width):
        count = len(placed)
        i = weights.shape[0] // 9

        def tap(value, a, bb):
            return value[(3 * a + bb) * i : (3 * a + bb + 1) * i]

        for a in range(3):
            for q in range(count):
                even = row0 + CELL * a + 2 * q * pitch
                e[even : even + i, seg : seg + CELL] = tap(placed[q], a, 1).astype(BF)
                odd = even + pitch
                value = tap(placed[q], a, 2)
                if q + 1 < count:
                    value = value + tap(placed[q + 1], a, 0)
                else:
                    e[odd : odd + i, nxt_seg : nxt_seg + nxt_width] = tap(weights, a, 0).astype(BF)
                e[odd : odd + i, seg : seg + CELL] = value.astype(BF)

    def fill_e3(kernels):
        for key, i, row0, pitch in kernels:
            for a in range(3):
                even = row0 + CELL * a
                odd = even + pitch
                for bb, at, seg in ((1, even, 0), (2, odd, 0), (0, odd, CELL)):
                    for jb, piece in enumerate(load_rows(ROW0[key] + (3 * a + bb) * i, i)):
                        e3[at : at + i, seg + 128 * jb : seg + 128 * (jb + 1)] = piece

    def fill_e2_21():
        w = rows_of((2, 1, 0), 432, 192)
        taps(e2, 0, 96, w, [place(w.astype(BF), 192, q, q + 1) for q in range(2)], 0, 384, 256)

    def fill_e2_31():
        w = rows_of((3, 1, 0), 216, 96)
        taps(e2, 0, 96, w, [place(w.astype(BF), 96, q, q + 1) for q in range(2)], 640, 1024, 128)

    def fill_e2_mid():
        w = rows_of((2, 0, 1), 216, 192)
        placed = [place(w.astype(BF), 192, q, q + 1) for q in range(2)]
        taps(e2, 1152, 96, w, placed, 0, 384, 256)
        w = rows_of((3, 0, 1), 54, 48)
        w_next = rows_of((3, 0, 1), 54, 48, 64)
        placed = [place(w.astype(BF), 48, 4 + q, 5 + q) for q in range(2)]
        taps(e2, 1152 + 48, 96, w_next, placed, 640, 1024 + 128, 128)

    def fill_e1_10():
        w = rows_of((1, 0, 0), 108, 96)
        taps(e1, 0, 48, w, [place(w.astype(BF), 96, q, q + 1) for q in range(4)], 0, 384, 128)

    def fill_e1_mid():
        w = rows_of((2, 0, 0), 54, 48) + 0.0
        w = w + rows_of((3, 0, 0), 54, 48, 48)
        taps(e1, 0, 48, w, [place(w.astype(BF), 96, q, q + 1) for q in range(4)], 512, 896, 128)

    def fill_up():
        u3[:, 0:384] = place(rows_of((0, 3, 0), 48, 48).astype(BF), 48, 0, 8).astype(BF)
        u3[:, 384:768] = place(rows_of((1, 3, 0), 96, 96).astype(BF), 96, 0, 4).astype(BF)
        u3[:, 768:1152] = place(rows_of((2, 3, 0), 192, 192).astype(BF), 192, 0, 2).astype(BF)
        w02 = rows_of((0, 2, 0), 24, 48).astype(BF)
        w12 = rows_of((1, 2, 0), 48, 96).astype(BF)
        for q in range(2):
            u2[192 * q : 192 * (q + 1), 0:384] = place(w02, 48, 4 * q, 4 * q + 4).astype(BF)
            u2[192 * q : 192 * (q + 1), 384:768] = place(w12, 96, 2 * q, 2 * q + 2).astype(BF)
        w01 = rows_of((0, 1, 0), 12, 48).astype(BF)
        for q in range(4):
            u1[96 * q : 96 * (q + 1), :] = place(w01, 48, 2 * q, 2 * q + 2).astype(BF)

    def reader(t, base):
        return lambda l, lo, hi: strip[t, l, base + lo : base + hi, :]

    def section_reader(buffer, t):
        return lambda l, lo, hi: buffer[t, l, lo:hi, :]

    def cells_of(read, total):
        return [read(l, 0, total) for l in range(3)]

    def shifted(read, rows, total, count):
        pieces = []
        for l in range(count):
            nxt[l, 0 : 8 * rows, :] = read(l, 1, 8 * rows + 1)
            for p in range(rows):
                nxt[l, 8 * p + 7 : 8 * p + 8, :] = read(l, 8 * rows + p, 8 * rows + p + 1)
            nxt[l, 8 * rows : total, :] = jnp.zeros((total - 8 * rows, 128), F32)
            pieces.append(nxt[l, 0:total, :])
        return pieces

    def lhs(pieces):
        return jnp.concatenate([piece.astype(BF) for piece in pieces], axis=1)

    def both(make):
        return jnp.concatenate([make(t) for t in range(2)], axis=0)

    def level_three(t):
        read = reader(t, C3)
        return lhs(cells_of(read, 32) + shifted(read, 2, 32, 3))

    def level_two(t):
        read = reader(t, C2)
        return lhs(cells_of(read, 32) + shifted(read, 3, 32, 2))

    def level_one(t):
        read = reader(t, C1)
        return lhs(cells_of(read, 48) + shifted(read, 5, 48, 1))

    def sums_of(t, *blocks):
        pieces = []
        for start, rows in blocks:
            pieces += [strip[t, l, SUMS + start : SUMS + start + rows, :] for l in range(3)]
        return lhs(pieces)

    def taps_of(own, own_weights, after, after_weights):
        whole = dot_nt(own, own_weights)
        last = dot_nt(after, jnp.concatenate([after_weights[CELL * a + 256 : CELL * (a + 1)] for a in range(3)], axis=0))
        pieces = []
        for a in range(3):
            pieces.append(whole[:, CELL * a : CELL * a + 256])
            pieces.append(whole[:, CELL * a + 256 : CELL * (a + 1)] + last[:, 128 * a : 128 * (a + 1)])
        return jnp.concatenate(pieces, axis=1)

    def rows_out(y, a, lo, hi):
        return y[lo:hi, CELL * a : CELL * (a + 1)]

    def upsampled(y, p, base):
        lo = base + 8 * p
        even = rows_out(y, 1, lo, lo + 8)
        return even, rows_out(y, 2, lo, lo + 8) + rows_out(y, 0, lo + 8, lo + 16)

    def section(buffer, t, y, rows, y_base, kept):
        view = buffer.at[t]
        for p in range(rows):
            even, odd = upsampled(y, p, y_base)
            put(view, 16 * p, even)
            put(view, 16 * p + 8, odd)
        put(view, 16 * rows, rows_out(y, 1, y_base + 8 * rows, y_base + 8 * rows + 8))
        extra, base = 8 * (2 * rows + 1), y_base + 8 * (rows + 1)
        for p in range(rows + 1):
            put(view, extra + 2 * p, rows_out(y, 1, base + p, base + p + 1))
            if p < rows:
                odd = rows_out(y, 2, base + p, base + p + 1) + rows_out(y, 0, base + p + 1, base + p + 2)
                put(view, extra + 2 * p + 1, odd)
        for l in range(3):
            buffer[t, l] = jnp.where(strip[t, l, kept : kept + buffer.shape[2], :] > 0.5, buffer[t, l], 0.0)

    def direct():
        line_up(((0, 336), (606, 1230), (2850, 4578)))
        fill_e2_21()
        fill_e1_10()
        fill_up()
        fill_e3((((3, 2, 0), 192, 0, 192),))
        y3 = dot_nt(both(level_three), e3[0:1152, :])
        maps_two, maps_one = both(level_two), both(level_one)
        y2 = taps_of(maps_two[:, 0:384], e2[0:1152, 0:384], maps_two[:, 384:640], e2[0:1152, 384:640])
        y1 = taps_of(maps_one[:, 0:384], e1[:, 0:384], maps_one[:, 384:512], e1[:, 384:512])
        x3 = dot_nt(both(lambda t: sums_of(t, (48, 8), (72, 8), (80, 8))), u3[...])
        x2 = dot_nt(both(lambda t: sums_of(t, (32, 16), (56, 16))), u2[...])
        x1 = dot_nt(both(lambda t: sums_of(t, (0, 32))), u1[...])
        for t in (1, 0):
            view = acc.at[t]
            for p in range(4):
                even, odd = upsampled(y1, p, 48 * t)
                put(view, 16 * p, even)
                put(view, 16 * p + 8, odd)
            for p in range(2):
                even, odd = upsampled(y2, p, 32 * t)
                put(view, 64 + 16 * p, even + x1[32 * t + 16 * p : 32 * t + 16 * p + 8])
                put(view, 72 + 16 * p, odd + x1[32 * t + 16 * p + 8 : 32 * t + 16 * p + 16])
            even, odd = upsampled(y3, 0, 32 * t)
            put(view, 96, even + x2[16 * t : 16 * t + 8])
            put(view, 104, odd + x2[16 * t + 8 : 16 * t + 16])
            put(view, 112, x3[8 * t : 8 * t + 8])

    def chained():
        line_up(((336, 606), (1230, 2850)))
        fill_e2_31()
        fill_e2_mid()
        fill_e1_mid()
        fill_e3((((3, 1, 1), 96, 1152, 96), ((3, 0, 2), 48, 1152 + 192, 48)))
        maps_two = both(level_two)
        y2_maps = taps_of(maps_two[:, 0:384], e2[1152:2304, 0:384], maps_two[:, 384:640], e2[1152:2304, 384:640])
        y3 = dot_nt(both(level_three), e3[1152:2304, :])
        for t in range(2):
            section(sg2, t, y3, 1, 32 * t, K2)

        def grads_two(t):
            read = section_reader(sg2, t)
            return lhs(cells_of(read, 32) + shifted(read, 3, 32, 2))

        grads = both(grads_two)
        y2 = y2_maps + taps_of(
            grads[:, 128:384], e2[1152:2304, 768:1024], grads[:, 512:640], e2[1152:2304, 1152:1280]
        )
        for t in range(2):
            section(sg1, t, y2, 2, 32 * t, K1)

        def grads_one(t):
            read = section_reader(sg1, t)
            return lhs(cells_of(read, 48) + shifted(read, 5, 48, 1))

        ones = both(grads_one)
        y1 = taps_of(ones[:, 0:384], e1[:, 512:896], ones[:, 384:512], e1[:, 896:1024])
        y2 = taps_of(grads[:, 0:256], e2[0:1152, 640:896], grads[:, 384:512], e2[0:1152, 1024:1152])
        for t in (1, 0):
            view = acc.at[t]
            for p in range(4):
                even, odd = upsampled(y1, p, 48 * t)
                put(view, 16 * p, even)
                put(view, 16 * p + 8, odd)
            for p in range(2):
                even, odd = upsampled(y2, p, 32 * t)
                put(view, 64 + 16 * p, even)
                put(view, 72 + 16 * p, odd)

    def emit(ref, rows, base, maps_of):
        for l in range(3):
            out[l, 0 : 8 * rows, :] = (
                maps_of[l, 0 : 8 * rows, :] + acc[0, l, base : base + 8 * rows, :] + acc_in[l, base : base + 8 * rows, :]
            )
        for cell in range(8):
            for l in range(3):
                lane0 = CELL * cell + 128 * l
                if rows == 1:
                    piece = out[l, cell : cell + 1, :]
                else:
                    piece = out[l, pl.ds(cell, rows, stride=8), :]
                ref[:, lane0 : lane0 + 128] = piece.astype(BF)

    class Part:
        def __init__(self, s, lo, size, sem):
            self.s, self.lo, self.size, self.used = s, lo, size, sem
            self.u, self.v = (b, y) if s == 0 else (y, b)
            self.pending, self.second = [], []

        def holds(self, x_of):
            return (x_of != 3) | (c == self.s)

        def send(self, ref, x_to, tile_to, x_of=None):
            copy = remote(ref, ref, s_send.at[self.used], s_recv.at[self.used], x_to, tile_to)
            self.used += 1
            self.pending.append((copy, x_of))
            self.when(x_of, copy.start)
            return copy

        def when(self, x_of, act):
            if x_of is None:
                act()
            else:
                pl.when(self.holds(x_of))(act)

        def send_bundle(self, u_of, to_u, to_v):
            zs = pl.ds(self.lo, self.size)
            if self.s == 0:
                return self.send(tiles.at[0, u_of, y, c, zs], to_u, tile_of(z, to_v, c), u_of)
            return self.send(tiles.at[1, b, u_of, c, zs], to_v, tile_of(z, to_u, c), b)

        def spread(self, u_of):
            self.second.append((u_of, [(d, self.send_bundle(u_of, self.u, wrap(self.v + d, 4))) for d in (1, 3, 2)]))

        def start(self):
            self.first = [(d, self.send_bundle(self.u, wrap(self.u + d, 4), self.v)) for d in (1, 3, 2)]
            self.spread(self.u)

        def pass_on(self):
            for d, copy in self.first:
                u_of = wrap(self.u - d, 4)
                self.when(u_of if self.s == 0 else b, copy.wait_recv)
                self.spread(u_of)

        def cross(self):
            zs = pl.ds(self.lo, self.size)
            self.across = []
            for u_of, copies_in in self.second:
                for d, copy in copies_in:
                    self.when(u_of if self.s == 0 else wrap(b - d, 4), copy.wait_recv)
                ref = tiles.at[0, u_of, :, c, zs] if self.s == 0 else tiles.at[1, :, u_of, c, zs]
                self.across.append(self.send(ref, b, tile_of(z, y, 1 - c)))

        def arrived(self):
            for copy in self.across:
                copy.wait_recv()

        def sent(self):
            for copy, x_of in self.pending:
                self.when(x_of, copy.wait_send)

    for copy in near:
        copy.wait_recv()
    far = [
        remote(
            tiles.at[:, b, y, c, pl.ds(lo, size)], tiles.at[:, b, y, c, pl.ds(to, size)], z_send.at[8 + n], z_recv.at[8 + n],
            b, tile_of(wrap(z + d, NZ), y, c),
        )
        for n, (lo, size, to, d) in enumerate(((5, 4, 9, -4), (1, 3, 13, 4)))
    ]
    for copy in far:
        copy.start()
    parts = [Part(s, lo, size, 19 * (2 * n + s)) for n, (lo, size) in enumerate(Z_PARTS) for s in range(2)]
    for part in parts[:2]:
        part.start()
    own_maps()
    for (j, at), lanes in SPLITS.items():
        width = 256 if j == 192 else 128

        def split_target(col):
            part, lane = col // width, lax.rem(col, width) - at
            return jnp.where((lane >= 0) & (lane < j), part * j + lane, -1)

        splits[:, lanes : lanes + CELL // j * width] = unit_matrix(CELL, CELL // j * width, split_target)
    for number, (j, low, high) in enumerate(PLACES):

        def place_target(col):
            which = col // j
            return jnp.where((which >= low) & (which < high), lax.rem(col, j), -1)

        rows = 256 if j == 192 else 128
        copies_of[0:rows, CELL * number : CELL * (number + 1)] = unit_matrix(rows, CELL, place_target)

    for part in parts[:2]:
        part.pass_on()
    for copy in far:
        copy.wait_recv()
    for part in parts[2:]:
        part.start()
    for part in parts[2:]:
        part.pass_on()
    for part in parts:
        part.cross()
    strip_copy.wait_recv()
    for part in parts:
        part.arrived()
    pl.when(c == 0)(direct)
    pl.when(c == 1)(chained)
    acc_copy = remote(acc.at[1], acc_in, x_send.at[1], x_recv.at[1], b, tile_of(z, y, 1 - c))
    acc_copy.start()
    for part in parts:
        part.sent()
    for copy in near + far + first + [strip_copy]:
        copy.wait_send()
    acc_copy.wait_recv()
    emit(o4, 1, 112, c3)
    emit(o3, 2, 96, c2)
    emit(o2, 4, 64, c1)
    emit(o1, 8, 0, c0)
    acc_copy.wait_send()


def finish_kernel(*refs):
    for n in range(4):
        refs[4 + n][...] = refs[n][...]


HBM = pl.BlockSpec(memory_space=pltpu.HBM)
VMEM = pl.BlockSpec(memory_space=pltpu.VMEM)
TILES = (2, 4, 4, 2, NZ, 16, 128)


def per_device(*operands):
    maps = operands[:12]

    def cells(rows):
        return pltpu.VMEM((3, rows, 128), F32)

    def buffer(*shape):
        return pltpu.VMEM(shape, BF)

    def sems(count):
        return pltpu.SemaphoreType.DMA((count,))

    results = [jax.ShapeDtypeStruct(g.shape, BF) for g in maps[:4]]
    done = pl.pallas_call(
        exchange_kernel,
        out_shape=results,
        in_specs=[HBM] * 13,
        out_specs=[VMEM] * 4,
        scratch_shapes=[buffer(*m.shape) for m in maps] + [
            buffer(SHARD),
            buffer(*TILES), buffer(48, CELL), buffer(32, CELL), buffer(32, CELL),
            pltpu.VMEM((RAW_ROWS, 128), F32), pltpu.VMEM((FLAT_ROWS, 128), F32),
            pltpu.VMEM((48, CELL), F32), pltpu.VMEM((32, CELL), F32), buffer(48, CELL), buffer(32, CELL),
            buffer(2304, 768), buffer(2304, 1280), buffer(1152, 1024),
            buffer(384, 1152), buffer(384, 768), buffer(384, 384),
            pltpu.VMEM((2, 1024, 128), F32), buffer(CELL, 4096), buffer(256, CELL * len(PLACES)),
            cells(64), cells(48), cells(32), cells(32),
            pltpu.VMEM((2, 3, 48, 128), F32), pltpu.VMEM((2, 3, 32, 128), F32),
            cells(32), cells(32), cells(16), cells(16), cells(48), cells(32), cells(32), cells(48), cells(64),
            pltpu.VMEM((2, 3, STRIP, 128), F32), pltpu.VMEM((2, 3, 120, 128), F32), cells(120),
            sems(13), sems(3), sems(3), sems(10), sems(10), sems(38 * len(Z_PARTS)), sems(38 * len(Z_PARTS)), sems(2), sems(2),
        ],
        compiler_params=pltpu.CompilerParams(
            collective_id=0, has_side_effects=True, vmem_limit_bytes=46 * 2**20
        ),
        name="exchange",
    )(*operands)
    return pl.pallas_call(
        finish_kernel,
        out_shape=results,
        in_specs=[VMEM] * 4,
        out_specs=[VMEM] * 4,
        compiler_params=pltpu.CompilerParams(vmem_limit_bytes=4 * 2**20),
        name="finish",
    )(*done)


def solution(mesh):
    maps = P("tile", "branch")
    return jax.shard_map(
        per_device, mesh=mesh, in_specs=(maps,) * 12 + (P("tile"),), out_specs=(maps,) * 4, check_vma=False
    )
```

```python
import jax
import jax.numpy as jnp
from jax import lax
from jax.experimental import pallas as pl
from jax.experimental.pallas import tpu as pltpu
from jax.sharding import PartitionSpec as P

BF = jnp.bfloat16
F32 = jnp.float32
MESH = pl.DeviceIdType.MESH
N_TILE = 128
N_BRANCH = 4
NZ = 16
Z_PARTS = ((0, 9), (9, 7))
SHARD = 13734
CELL = 384
RAW_ROWS = 112
FLAT_ROWS = 13744

C1, C2, C3, SUMS, K1, K2, STRIP = 0, 48, 80, 112, 200, 248, 280

ROW0 = {
    (0, 1, 0): 0,
    (0, 2, 0): 12,
    (0, 3, 0): 36,
    (1, 0, 0): 84,
    (1, 2, 0): 192,
    (1, 3, 0): 240,
    (2, 0, 0): 336,
    (2, 0, 1): 390,
    (2, 1, 0): 606,
    (2, 3, 0): 1038,
    (3, 0, 0): 1230,
    (3, 0, 1): 1284,
    (3, 0, 2): 1338,
    (3, 1, 0): 1770,
    (3, 1, 1): 1986,
    (3, 2, 0): 2850,
}


SPLITS = {(48, 0): 0, (48, 48): 1024, (48, 64): 2048, (96, 0): 3072, (192, 0): 3584}
PLACES = (
    [(48, 4 + q, 5 + q) for q in range(2)] + [(48, 0, 8), (48, 0, 4), (48, 4, 8)]
    + [(48, 2 * q, 2 * q + 2) for q in range(4)] + [(96, q, q + 1) for q in range(4)]
    + [(96, 0, 4), (96, 0, 2), (96, 2, 4), (192, 0, 1), (192, 1, 2), (192, 0, 2)]
)


def remote(src, dst, send, recv, branch, tile):
    return pltpu.make_async_remote_copy(
        src_ref=src, dst_ref=dst, send_sem=send, recv_sem=recv, device_id=(branch, tile), device_id_type=MESH
    )


def slots_of(k):
    return [(t % 2 if t < 6 else k % 2, t // 2, (k // 2) % 4, k % 2) for t in range(7)]


def dot(a, b):
    return lax.dot_general(a, b, (((1,), (0,)), ((), ())), preferred_element_type=F32)


def dot_nt(a, b):
    return lax.dot_general(a, b, (((1,), (1,)), ((), ())), preferred_element_type=F32)


def unit_matrix(rows, cols, target):
    column = lax.broadcasted_iota(jnp.int32, (1, cols), 1)
    row = lax.broadcasted_iota(jnp.int32, (rows, cols), 0)
    return jnp.where(row == target(column), 1.0, 0.0).astype(BF)


def exchange_kernel(
    *refs,
):
    inputs, outputs, refs = refs[:13], refs[13:17], refs[17:]
    loaded, refs = refs[:13], refs[13:]
    (
        tiles, row_in, col_in, corner_in, shard_f, flat, row_f, col_f, row_out, col_out,
        e3, e2, e1, u3, u2, u1, wide, splits, copies_of,
        c0, c1, c2, c3, sg1, sg2, q20, q30a, q30b, q31, k1, k2a, k2b, nxt, out, strip, acc, acc_in,
        l_sem, h_send, h_recv, z_send, z_recv, s_send, s_recv, x_send, x_recv,
    ) = refs
    g1, g2, g3, g4, p1, p2, p3, p4, m20, m30a, m30b, m31, shard_in = loaded
    o1, o2, o3, o4 = outputs
    b = lax.axis_index("branch")
    k = lax.axis_index("tile")
    z, y, c = k // 8, lax.rem(k // 2, 4), lax.rem(k, 2)
    has_row = k < N_TILE - 1
    has_col = b < N_BRANCH - 1

    loads = [pltpu.make_async_copy(inputs[n], loaded[n], l_sem.at[n]) for n in range(13)]
    loads[12].start()

    def tile_of(zz, yy, cc):
        return zz * 8 + yy * 2 + cc

    def wrap(value, count):
        return lax.rem(value + count, count)

    left, right = wrap(b - 1, N_BRANCH), wrap(b + 1, N_BRANCH)
    up1, down1 = wrap(k - 1, N_TILE), wrap(k + 1, N_TILE)

    partners = [
        (b, up1), (b, down1), (left, k), (right, k), (left, up1), (right, down1),
        (b, tile_of(z, y, 1 - c)), (wrap(b + 2, 4), k),
    ] + [(b, tile_of(z, wrap(y + d, 4), c)) for d in (1, 2, 3)]
    along_z = [1, -1, 2, -2, 3, -3, 4, -4]
    partners += [(b, tile_of(wrap(z + d, NZ), y, c)) for d in along_z]
    barrier = pltpu.get_barrier_semaphore()
    for who in partners:
        pl.semaphore_signal(barrier, inc=1, device_id=who, device_id_type=MESH)
    for n in (1, 2, 3, 5, 6, 7, 8, 9, 10, 11, 0, 4):
        loads[n].start()

    loads[12].wait()
    whole = SHARD // 1024 * 1024
    rest = SHARD // 128 * 128
    row_at = [n // 128 for n in (whole, rest)]
    shard_f[0 : row_at[0], :] = shard_in[0:whole].astype(F32).reshape(row_at[0], 128)
    shard_f[row_at[0] : row_at[1], :] = shard_in[whole:rest].astype(F32).reshape(row_at[1] - row_at[0], 128)
    shard_f[row_at[1] : RAW_ROWS, :] = jnp.zeros((RAW_ROWS - row_at[1], 128), F32)
    shard_f[row_at[1] : row_at[1] + 1, 0 : SHARD - rest] = shard_in[rest:SHARD].astype(F32).reshape(1, SHARD - rest)
    for s in range(2):
        row = jnp.where(b == 3, 96, 32 * b + 16 * s)
        tiles[s, b, y, c, 4] = shard_f[pl.ds(pl.multiple_of(row, 16), 16), :].astype(BF)

    pl.semaphore_wait(barrier, len(partners))
    near = []
    for n, d in enumerate(along_z):
        copy = remote(
            tiles.at[:, b, y, c, 4], tiles.at[:, b, y, c, 4 - d], z_send.at[n], z_recv.at[n],
            b, tile_of(wrap(z + d, NZ), y, c),
        )
        copy.start()
        near.append(copy)

    for load in loads[:12]:
        load.wait()
    row_f[...] = jnp.zeros_like(row_f)
    col_f[...] = jnp.zeros_like(col_f)
    at_row, at_col = 0, 0
    for g, p in ((g2, p2), (g3, p3), (g4, p4)):
        rows = g.shape[0]
        masked = jnp.where(p[...].astype(F32) > 0, g[...].astype(F32), 0.0)
        for cell in range(8):
            row_f[at_row + cell : at_row + cell + 1, :] = masked[0:1, CELL * cell : CELL * (cell + 1)]
        col_f[at_col : at_col + rows, :] = masked[:, 0:CELL]
        at_row, at_col = at_row + 8, at_col + rows
    for m, at_row, at_col in ((m20, 24, 8), (m30a, 28, 12), (m31, 32, 18), (m30b, 36, 16)):
        rows, units = m.shape[0], m.shape[1] // CELL
        value = m[...].astype(F32)
        for unit in range(units):
            row_f[at_row + unit : at_row + unit + 1, :] = value[0:1, CELL * unit : CELL * (unit + 1)]
        col_f[at_col : at_col + rows, :] = value[:, 0:CELL]
    row_out[...] = row_f[...].astype(BF)
    col_out[...] = col_f[...].astype(BF)

    first = [
        remote(row_out, row_in, h_send.at[0], h_recv.at[0], b, up1),
        remote(col_out, col_in, h_send.at[1], h_recv.at[1], left, k),
        remote(col_out, corner_in, h_send.at[2], h_recv.at[2], left, up1),
    ]
    for copy in first:
        copy.start()

    for ref in (e3, e2, e1, c1, c2, c3, sg1, sg2, q20, q30a, q30b, q31, k1, k2a, k2b, nxt, acc):
        ref[...] = jnp.zeros_like(ref)

    def put(buffer, row, value):
        rows = value.shape[0]
        for l in range(3):
            buffer[l, row : row + rows, :] = value[:, 128 * l : 128 * (l + 1)]

    def spread_units(buffer, value, units):
        rows = value.shape[0]
        for unit in range(units):
            for l in range(3):
                piece = value[:, CELL * unit + 128 * l : CELL * unit + 128 * (l + 1)]
                if rows == 1:
                    buffer[l, unit : unit + 1, :] = piece
                else:
                    buffer[l, pl.ds(unit, rows, stride=units), :] = piece

    def masked(g, p):
        return jnp.where(p[...].astype(F32) > 0, g[...].astype(F32), 0.0)

    def flags(buffer):
        whole = jnp.concatenate([buffer[l] for l in range(3)], axis=1)
        return jnp.where(whole > 0, 1.0, 0.0).astype(BF)

    def target20(shift):
        def target(col):
            part, lane = col // CELL, lax.rem(col, CELL)
            pixel, channel = lane // 96, lax.rem(lane, 96) - shift
            return jnp.where((channel >= 0) & (channel < 48), part * 192 + pixel * 48 + channel, -1)

        return target

    def target31(col):
        part, lane = col // CELL, lax.rem(col, CELL)
        return jnp.where(lane < 192, part * 192 + lane, -1)

    def target30b(col):
        part, lane = col // CELL, lax.rem(col, CELL) - 192
        return jnp.where((lane >= 0) & (lane < 96), part * 96 + lane, -1)

    def keep(buffer, value, parts, count, extra_from, extra_rows, extra_to):
        for l in range(3):
            for part in range(parts):
                lanes = slice(part * CELL + 128 * l, part * CELL + 128 * (l + 1))
                buffer[l, pl.ds(part, count, stride=parts), :] = value[0:count, lanes]
            buffer[l, extra_to : extra_to + extra_rows, :] = value[
                extra_from : extra_from + extra_rows, 128 * l : 128 * (l + 1)
            ]

    def block_sums(buffer, rows, factor):
        groups = []
        for first in range(0, rows, factor):
            pieces = []
            for l in range(3):
                total = buffer[l, 8 * first : 8 * first + 8, :]
                for p in range(first + 1, first + factor):
                    total = total + buffer[l, 8 * p : 8 * p + 8, :]
                pieces.append(total)
            groups.append(jnp.concatenate(pieces, axis=1))
        return jnp.concatenate(groups, axis=0).astype(BF)

    def own_maps():
        spread_units(c0, masked(g1, p1), 8)
        for buffer, g, p in ((c1, g2, p2), (c2, g3, p3), (c3, g4, p4)):
            spread_units(buffer, masked(g, p), 8)
        for buffer, m, units in ((q20, m20, 4), (q30a, m30a, 4), (q31, m31, 4), (q30b, m30b, 2)):
            spread_units(buffer, m[...].astype(F32), units)

        for copy in first:
            copy.wait_recv()
        row_halo = row_in[...].astype(F32)
        col_halo = col_in[...].astype(F32)
        corner = corner_in[...].astype(F32)
        row_zero = jnp.where(has_row, row_halo, 0.0)
        col_zero = jnp.where(has_col, col_halo, 0.0)
        corner_zero = jnp.where(has_row & has_col, corner, 0.0)
        at = 0
        for buffer, rows, halo in ((c1, 4, 0), (c2, 2, 8), (c3, 1, 16)):
            put(buffer, 8 * rows, row_zero[halo : halo + 8])
            put(buffer, 8 * rows + 8, col_zero[at : at + rows])
            put(buffer, 8 * rows + 8 + rows, corner_zero[at : at + 1])
            at += rows
        for buffer, rows, units, halo, at in ((q20, 4, 4, 24, 8), (q30a, 4, 4, 28, 12), (q31, 2, 4, 32, 18), (q30b, 2, 2, 36, 16)):
            put(buffer, rows * units, row_halo[halo : halo + units])
            put(buffer, (rows + 1) * units, col_halo[at : at + rows])
            put(buffer, (rows + 1) * units + rows, corner[at : at + 1])

        mask1 = dot(flags(q20), unit_matrix(CELL, 768, target20(0))) + dot(
            flags(q30a), unit_matrix(CELL, 768, target20(48))
        )
        keep(k1, mask1, 2, 20, 20, 5, 40)
        keep(k2a, dot(flags(q31), unit_matrix(CELL, 768, target31)), 2, 12, 12, 3, 24)
        keep(k2b, dot(flags(q30b), unit_matrix(CELL, 1536, target30b)), 4, 6, 6, 3, 24)
        pooled = [block_sums(c0, 8, f) for f in (2, 4, 8)] + [block_sums(c1, 4, f) for f in (2, 4)] + [block_sums(c2, 2, 2)]
        for l in range(3):
            strip[0, l, C1 : C1 + 48, :] = c1[l]
            strip[0, l, C2 : C2 + 32, :] = c2[l]
            strip[0, l, C3 : C3 + 32, :] = c3[l]
            strip[0, l, K1 : K1 + 48, :] = k1[l]
            strip[0, l, K2 : K2 + 32, :] = k2a[l] + k2b[l]
        row = SUMS
        for value in pooled:
            rows = value.shape[0]
            for l in range(3):
                strip[0, l, row : row + rows, :] = value[:, 128 * l : 128 * (l + 1)].astype(F32)
            row += rows
        strip_copy.start()

    strip_copy = remote(
        strip.at[0], strip.at[1], x_send.at[0], x_recv.at[0], b, tile_of(z, y, 1 - c)
    )

    places = [lax.rem(zz - z + 4 + NZ, NZ) for zz in range(NZ)]
    lane_no = lax.broadcasted_iota(jnp.int32, (RAW_ROWS, 128), 1)

    def line_up(ranges):
        for shard in range(N_TILE):
            first_row, phase = divmod(SHARD * shard, 128)
            if not any(first_row < 3 * hi and first_row + 109 > 3 * lo for lo, hi in ranges):
                continue
            blocks = [tiles[s, x_at, y_at, c_at, places[shard // 8]] for s, x_at, y_at, c_at in slots_of(shard)]
            value = jnp.concatenate(blocks, axis=0).astype(F32)
            if phase == 0:
                flat[first_row : first_row + RAW_ROWS, :] = value
                continue
            value = pltpu.roll(value, phase, 1)
            pltpu.store(flat.at[first_row : first_row + RAW_ROWS, :], value, mask=lane_no >= phase)
            pltpu.store(flat.at[first_row + 1 : first_row + 1 + RAW_ROWS, :], value, mask=lane_no < phase)

    def load_rows(row, count):
        return [flat[pl.ds(3 * row + jb, count, stride=3), :].astype(BF) for jb in range(3)]

    def rows_of(key, rows, j, at=0):
        n = CELL // j
        width = 256 if j == 192 else 128

        lanes = SPLITS[j, at]
        whole = jnp.concatenate(load_rows(ROW0[key], rows), axis=1)
        split = dot(whole, splits[:, lanes : lanes + n * width])
        parts = []
        for half in range(width // 128):
            for part in range(n):
                wide[half, pl.ds(part, rows, stride=n), :] = split[
                    :, part * width + 128 * half : part * width + 128 * (half + 1)
                ]
            parts.append(wide[half, 0 : rows * n, :])
        return parts[0] if len(parts) == 1 else jnp.concatenate(parts, axis=1)

    def place(weights, j, low, high):
        lanes = CELL * PLACES.index((j, low, high))
        return dot(weights, copies_of[0 : weights.shape[1], lanes : lanes + CELL])

    def taps(e, row0, pitch, weights, placed, seg, nxt_seg, nxt_width):
        count = len(placed)
        i = weights.shape[0] // 9

        def tap(value, a, bb):
            return value[(3 * a + bb) * i : (3 * a + bb + 1) * i]

        for a in range(3):
            for q in range(count):
                even = row0 + CELL * a + 2 * q * pitch
                e[even : even + i, seg : seg + CELL] = tap(placed[q], a, 1).astype(BF)
                odd = even + pitch
                value = tap(placed[q], a, 2)
                if q + 1 < count:
                    value = value + tap(placed[q + 1], a, 0)
                else:
                    e[odd : odd + i, nxt_seg : nxt_seg + nxt_width] = tap(weights, a, 0).astype(BF)
                e[odd : odd + i, seg : seg + CELL] = value.astype(BF)

    def fill_e3(kernels):
        for key, i, row0, pitch in kernels:
            for a in range(3):
                even = row0 + CELL * a
                odd = even + pitch
                for bb, at, seg in ((1, even, 0), (2, odd, 0), (0, odd, CELL)):
                    for jb, piece in enumerate(load_rows(ROW0[key] + (3 * a + bb) * i, i)):
                        e3[at : at + i, seg + 128 * jb : seg + 128 * (jb + 1)] = piece

    def fill_e2_21():
        w = rows_of((2, 1, 0), 432, 192)
        taps(e2, 0, 96, w, [place(w.astype(BF), 192, q, q + 1) for q in range(2)], 0, 384, 256)

    def fill_e2_31():
        w = rows_of((3, 1, 0), 216, 96)
        taps(e2, 0, 96, w, [place(w.astype(BF), 96, q, q + 1) for q in range(2)], 640, 1024, 128)

    def fill_e2_mid():
        w = rows_of((2, 0, 1), 216, 192)
        placed = [place(w.astype(BF), 192, q, q + 1) for q in range(2)]
        taps(e2, 1152, 96, w, placed, 0, 384, 256)
        w = rows_of((3, 0, 1), 54, 48)
        w_next = rows_of((3, 0, 1), 54, 48, 64)
        placed = [place(w.astype(BF), 48, 4 + q, 5 + q) for q in range(2)]
        taps(e2, 1152 + 48, 96, w_next, placed, 640, 1024 + 128, 128)

    def fill_e1_10():
        w = rows_of((1, 0, 0), 108, 96)
        taps(e1, 0, 48, w, [place(w.astype(BF), 96, q, q + 1) for q in range(4)], 0, 384, 128)

    def fill_e1_mid():
        w = rows_of((2, 0, 0), 54, 48) + 0.0
        w = w + rows_of((3, 0, 0), 54, 48, 48)
        taps(e1, 0, 48, w, [place(w.astype(BF), 96, q, q + 1) for q in range(4)], 512, 896, 128)

    def fill_up():
        u3[:, 0:384] = place(rows_of((0, 3, 0), 48, 48).astype(BF), 48, 0, 8).astype(BF)
        u3[:, 384:768] = place(rows_of((1, 3, 0), 96, 96).astype(BF), 96, 0, 4).astype(BF)
        u3[:, 768:1152] = place(rows_of((2, 3, 0), 192, 192).astype(BF), 192, 0, 2).astype(BF)
        w02 = rows_of((0, 2, 0), 24, 48).astype(BF)
        w12 = rows_of((1, 2, 0), 48, 96).astype(BF)
        for q in range(2):
            u2[192 * q : 192 * (q + 1), 0:384] = place(w02, 48, 4 * q, 4 * q + 4).astype(BF)
            u2[192 * q : 192 * (q + 1), 384:768] = place(w12, 96, 2 * q, 2 * q + 2).astype(BF)
        w01 = rows_of((0, 1, 0), 12, 48).astype(BF)
        for q in range(4):
            u1[96 * q : 96 * (q + 1), :] = place(w01, 48, 2 * q, 2 * q + 2).astype(BF)

    def reader(t, base):
        return lambda l, lo, hi: strip[t, l, base + lo : base + hi, :]

    def section_reader(buffer, t):
        return lambda l, lo, hi: buffer[t, l, lo:hi, :]

    def cells_of(read, total):
        return [read(l, 0, total) for l in range(3)]

    def shifted(read, rows, total, count):
        pieces = []
        for l in range(count):
            nxt[l, 0 : 8 * rows, :] = read(l, 1, 8 * rows + 1)
            for p in range(rows):
                nxt[l, 8 * p + 7 : 8 * p + 8, :] = read(l, 8 * rows + p, 8 * rows + p + 1)
            nxt[l, 8 * rows : total, :] = jnp.zeros((total - 8 * rows, 128), F32)
            pieces.append(nxt[l, 0:total, :])
        return pieces

    def lhs(pieces):
        return jnp.concatenate([piece.astype(BF) for piece in pieces], axis=1)

    def both(make):
        return jnp.concatenate([make(t) for t in range(2)], axis=0)

    def level_three(t):
        read = reader(t, C3)
        return lhs(cells_of(read, 32) + shifted(read, 2, 32, 3))

    def level_two(t):
        read = reader(t, C2)
        return lhs(cells_of(read, 32) + shifted(read, 3, 32, 2))

    def level_one(t):
        read = reader(t, C1)
        return lhs(cells_of(read, 48) + shifted(read, 5, 48, 1))

    def sums_of(t, *blocks):
        pieces = []
        for start, rows in blocks:
            pieces += [strip[t, l, SUMS + start : SUMS + start + rows, :] for l in range(3)]
        return lhs(pieces)

    def taps_of(own, own_weights, after, after_weights):
        whole = dot_nt(own, own_weights)
        last = dot_nt(after, jnp.concatenate([after_weights[CELL * a + 256 : CELL * (a + 1)] for a in range(3)], axis=0))
        pieces = []
        for a in range(3):
            pieces.append(whole[:, CELL * a : CELL * a + 256])
            pieces.append(whole[:, CELL * a + 256 : CELL * (a + 1)] + last[:, 128 * a : 128 * (a + 1)])
        return jnp.concatenate(pieces, axis=1)

    def rows_out(y, a, lo, hi):
        return y[lo:hi, CELL * a : CELL * (a + 1)]

    def upsampled(y, p, base):
        lo = base + 8 * p
        even = rows_out(y, 1, lo, lo + 8)
        return even, rows_out(y, 2, lo, lo + 8) + rows_out(y, 0, lo + 8, lo + 16)

    def section(buffer, t, y, rows, y_base, kept):
        view = buffer.at[t]
        for p in range(rows):
            even, odd = upsampled(y, p, y_base)
            put(view, 16 * p, even)
            put(view, 16 * p + 8, odd)
        put(view, 16 * rows, rows_out(y, 1, y_base + 8 * rows, y_base + 8 * rows + 8))
        extra, base = 8 * (2 * rows + 1), y_base + 8 * (rows + 1)
        for p in range(rows + 1):
            put(view, extra + 2 * p, rows_out(y, 1, base + p, base + p + 1))
            if p < rows:
                odd = rows_out(y, 2, base + p, base + p + 1) + rows_out(y, 0, base + p + 1, base + p + 2)
                put(view, extra + 2 * p + 1, odd)
        for l in range(3):
            buffer[t, l] = jnp.where(strip[t, l, kept : kept + buffer.shape[2], :] > 0.5, buffer[t, l], 0.0)

    def direct():
        line_up(((0, 336), (606, 1230), (2850, 4578)))
        fill_e2_21()
        fill_e1_10()
        fill_up()
        fill_e3((((3, 2, 0), 192, 0, 192),))
        y3 = dot_nt(both(level_three), e3[0:1152, :])
        maps_two, maps_one = both(level_two), both(level_one)
        y2 = taps_of(maps_two[:, 0:384], e2[0:1152, 0:384], maps_two[:, 384:640], e2[0:1152, 384:640])
        y1 = taps_of(maps_one[:, 0:384], e1[:, 0:384], maps_one[:, 384:512], e1[:, 384:512])
        x3 = dot_nt(both(lambda t: sums_of(t, (48, 8), (72, 8), (80, 8))), u3[...])
        x2 = dot_nt(both(lambda t: sums_of(t, (32, 16), (56, 16))), u2[...])
        x1 = dot_nt(both(lambda t: sums_of(t, (0, 32))), u1[...])
        for t in (1, 0):
            view = acc.at[t]
            for p in range(4):
                even, odd = upsampled(y1, p, 48 * t)
                put(view, 16 * p, even)
                put(view, 16 * p + 8, odd)
            for p in range(2):
                even, odd = upsampled(y2, p, 32 * t)
                put(view, 64 + 16 * p, even + x1[32 * t + 16 * p : 32 * t + 16 * p + 8])
                put(view, 72 + 16 * p, odd + x1[32 * t + 16 * p + 8 : 32 * t + 16 * p + 16])
            even, odd = upsampled(y3, 0, 32 * t)
            put(view, 96, even + x2[16 * t : 16 * t + 8])
            put(view, 104, odd + x2[16 * t + 8 : 16 * t + 16])
            put(view, 112, x3[8 * t : 8 * t + 8])

    def chained():
        line_up(((336, 606), (1230, 2850)))
        fill_e2_31()
        fill_e2_mid()
        fill_e1_mid()
        fill_e3((((3, 1, 1), 96, 1152, 96), ((3, 0, 2), 48, 1152 + 192, 48)))
        maps_two = both(level_two)
        y2_maps = taps_of(maps_two[:, 0:384], e2[1152:2304, 0:384], maps_two[:, 384:640], e2[1152:2304, 384:640])
        y3 = dot_nt(both(level_three), e3[1152:2304, :])
        for t in range(2):
            section(sg2, t, y3, 1, 32 * t, K2)

        def grads_two(t):
            read = section_reader(sg2, t)
            return lhs(cells_of(read, 32) + shifted(read, 3, 32, 2))

        grads = both(grads_two)
        y2 = y2_maps + taps_of(
            grads[:, 128:384], e2[1152:2304, 768:1024], grads[:, 512:640], e2[1152:2304, 1152:1280]
        )
        for t in range(2):
            section(sg1, t, y2, 2, 32 * t, K1)

        def grads_one(t):
            read = section_reader(sg1, t)
            return lhs(cells_of(read, 48) + shifted(read, 5, 48, 1))

        ones = both(grads_one)
        y1 = taps_of(ones[:, 0:384], e1[:, 512:896], ones[:, 384:512], e1[:, 896:1024])
        y2 = taps_of(grads[:, 0:256], e2[0:1152, 640:896], grads[:, 384:512], e2[0:1152, 1024:1152])
        for t in (1, 0):
            view = acc.at[t]
            for p in range(4):
                even, odd = upsampled(y1, p, 48 * t)
                put(view, 16 * p, even)
                put(view, 16 * p + 8, odd)
            for p in range(2):
                even, odd = upsampled(y2, p, 32 * t)
                put(view, 64 + 16 * p, even)
                put(view, 72 + 16 * p, odd)

    def emit(ref, rows, base, maps_of):
        for l in range(3):
            out[l, 0 : 8 * rows, :] = (
                maps_of[l, 0 : 8 * rows, :] + acc[0, l, base : base + 8 * rows, :] + acc_in[l, base : base + 8 * rows, :]
            )
        for cell in range(8):
            for l in range(3):
                lane0 = CELL * cell + 128 * l
                if rows == 1:
                    piece = out[l, cell : cell + 1, :]
                else:
                    piece = out[l, pl.ds(cell, rows, stride=8), :]
                ref[:, lane0 : lane0 + 128] = piece.astype(BF)

    class Part:
        def __init__(self, s, lo, size, sem):
            self.s, self.lo, self.size, self.used = s, lo, size, sem
            self.u, self.v = (b, y) if s == 0 else (y, b)
            self.pending, self.second = [], []

        def holds(self, x_of):
            return (x_of != 3) | (c == self.s)

        def send(self, ref, x_to, tile_to, x_of=None):
            copy = remote(ref, ref, s_send.at[self.used], s_recv.at[self.used], x_to, tile_to)
            self.used += 1
            self.pending.append((copy, x_of))
            self.when(x_of, copy.start)
            return copy

        def when(self, x_of, act):
            if x_of is None:
                act()
            else:
                pl.when(self.holds(x_of))(act)

        def send_bundle(self, u_of, to_u, to_v):
            zs = pl.ds(self.lo, self.size)
            if self.s == 0:
                return self.send(tiles.at[0, u_of, y, c, zs], to_u, tile_of(z, to_v, c), u_of)
            return self.send(tiles.at[1, b, u_of, c, zs], to_v, tile_of(z, to_u, c), b)

        def spread(self, u_of):
            self.second.append((u_of, [(d, self.send_bundle(u_of, self.u, wrap(self.v + d, 4))) for d in (1, 3, 2)]))

        def start(self):
            self.first = [(d, self.send_bundle(self.u, wrap(self.u + d, 4), self.v)) for d in (1, 3, 2)]
            self.spread(self.u)

        def pass_on(self):
            for d, copy in self.first:
                u_of = wrap(self.u - d, 4)
                self.when(u_of if self.s == 0 else b, copy.wait_recv)
                self.spread(u_of)

        def cross(self):
            zs = pl.ds(self.lo, self.size)
            self.across = []
            for u_of, copies_in in self.second:
                for d, copy in copies_in:
                    self.when(u_of if self.s == 0 else wrap(b - d, 4), copy.wait_recv)
                ref = tiles.at[0, u_of, :, c, zs] if self.s == 0 else tiles.at[1, :, u_of, c, zs]
                self.across.append(self.send(ref, b, tile_of(z, y, 1 - c)))

        def arrived(self):
            for copy in self.across:
                copy.wait_recv()

        def sent(self):
            for copy, x_of in self.pending:
                self.when(x_of, copy.wait_send)

    for copy in near:
        copy.wait_recv()
    far = [
        remote(
            tiles.at[:, b, y, c, pl.ds(lo, size)], tiles.at[:, b, y, c, pl.ds(to, size)], z_send.at[8 + n], z_recv.at[8 + n],
            b, tile_of(wrap(z + d, NZ), y, c),
        )
        for n, (lo, size, to, d) in enumerate(((5, 4, 9, -4), (1, 3, 13, 4)))
    ]
    for copy in far:
        copy.start()
    parts = [Part(s, lo, size, 19 * (2 * n + s)) for n, (lo, size) in enumerate(Z_PARTS) for s in range(2)]
    for part in parts[:2]:
        part.start()
    own_maps()
    for (j, at), lanes in SPLITS.items():
        width = 256 if j == 192 else 128

        def split_target(col):
            part, lane = col // width, lax.rem(col, width) - at
            return jnp.where((lane >= 0) & (lane < j), part * j + lane, -1)

        splits[:, lanes : lanes + CELL // j * width] = unit_matrix(CELL, CELL // j * width, split_target)
    for number, (j, low, high) in enumerate(PLACES):

        def place_target(col):
            which = col // j
            return jnp.where((which >= low) & (which < high), lax.rem(col, j), -1)

        rows = 256 if j == 192 else 128
        copies_of[0:rows, CELL * number : CELL * (number + 1)] = unit_matrix(rows, CELL, place_target)

    for part in parts[:2]:
        part.pass_on()
    for copy in far:
        copy.wait_recv()
    for part in parts[2:]:
        part.start()
    for part in parts[2:]:
        part.pass_on()
    for part in parts:
        part.cross()
    strip_copy.wait_recv()
    for part in parts:
        part.arrived()
    pl.when(c == 0)(direct)
    pl.when(c == 1)(chained)
    acc_copy = remote(acc.at[1], acc_in, x_send.at[1], x_recv.at[1], b, tile_of(z, y, 1 - c))
    acc_copy.start()
    for part in parts:
        part.sent()
    for copy in near + far + first + [strip_copy]:
        copy.wait_send()
    acc_copy.wait_recv()
    emit(o4, 1, 112, c3)
    emit(o3, 2, 96, c2)
    emit(o2, 4, 64, c1)
    emit(o1, 8, 0, c0)
    acc_copy.wait_send()


def finish_kernel(*refs):
    for n in range(4):
        refs[4 + n][...] = refs[n][...]


ANY = pl.BlockSpec(memory_space=pl.ANY)
VMEM = pl.BlockSpec(memory_space=pltpu.VMEM)
TILES = (2, 4, 4, 2, NZ, 16, 128)


def per_device(*operands):
    maps = operands[:12]

    def cells(rows):
        return pltpu.VMEM((3, rows, 128), F32)

    def buffer(*shape):
        return pltpu.VMEM(shape, BF)

    def sems(count):
        return pltpu.SemaphoreType.DMA((count,))

    results = [jax.ShapeDtypeStruct(g.shape, BF) for g in maps[:4]]
    done = pl.pallas_call(
        exchange_kernel,
        out_shape=[pltpu.VMEM(g.shape, BF) for g in maps[:4]],
        in_specs=[ANY] * 13,
        out_specs=[VMEM] * 4,
        scratch_shapes=[buffer(*m.shape) for m in maps] + [
            buffer(SHARD),
            buffer(*TILES), buffer(48, CELL), buffer(32, CELL), buffer(32, CELL),
            pltpu.VMEM((RAW_ROWS, 128), F32), pltpu.VMEM((FLAT_ROWS, 128), F32),
            pltpu.VMEM((48, CELL), F32), pltpu.VMEM((32, CELL), F32), buffer(48, CELL), buffer(32, CELL),
            buffer(2304, 768), buffer(2304, 1280), buffer(1152, 1024),
            buffer(384, 1152), buffer(384, 768), buffer(384, 384),
            pltpu.VMEM((2, 1024, 128), F32), buffer(CELL, 4096), buffer(256, CELL * len(PLACES)),
            cells(64), cells(48), cells(32), cells(32),
            pltpu.VMEM((2, 3, 48, 128), F32), pltpu.VMEM((2, 3, 32, 128), F32),
            cells(32), cells(32), cells(16), cells(16), cells(48), cells(32), cells(32), cells(48), cells(64),
            pltpu.VMEM((2, 3, STRIP, 128), F32), pltpu.VMEM((2, 3, 120, 128), F32), cells(120),
            sems(13), sems(3), sems(3), sems(10), sems(10), sems(38 * len(Z_PARTS)), sems(38 * len(Z_PARTS)), sems(2), sems(2),
        ],
        compiler_params=pltpu.CompilerParams(
            collective_id=0, has_side_effects=True, vmem_limit_bytes=60 * 2**20
        ),
        name="exchange",
    )(*operands)
    return pl.pallas_call(
        finish_kernel,
        out_shape=results,
        in_specs=[VMEM] * 4,
        out_specs=[VMEM] * 4,
        compiler_params=pltpu.CompilerParams(vmem_limit_bytes=4 * 2**20),
        name="finish",
    )(*done)


def solution(mesh):
    maps = P("tile", "branch")
    return jax.shard_map(
        per_device, mesh=mesh, in_specs=(maps,) * 12 + (P("tile"),), out_specs=(maps,) * 4, check_vma=False
    )
```

```python
import jax
import jax.numpy as jnp
from jax import lax
from jax.experimental import pallas as pl
from jax.experimental.pallas import tpu as pltpu
from jax.sharding import PartitionSpec as P

BF = jnp.bfloat16
F32 = jnp.float32
MESH = pl.DeviceIdType.MESH
N_TILE = 128
N_BRANCH = 4
NZ = 16
Z_PARTS = ((0, 9), (9, 7))
SHARD = 13734
CELL = 384
RAW_ROWS = 112
FLAT_ROWS = 13744

C1, C2, C3, SUMS, K1, K2, STRIP = 0, 48, 80, 112, 200, 248, 280

ROW0 = {
    (0, 1, 0): 0,
    (0, 2, 0): 12,
    (0, 3, 0): 36,
    (1, 0, 0): 84,
    (1, 2, 0): 192,
    (1, 3, 0): 240,
    (2, 0, 0): 336,
    (2, 0, 1): 390,
    (2, 1, 0): 606,
    (2, 3, 0): 1038,
    (3, 0, 0): 1230,
    (3, 0, 1): 1284,
    (3, 0, 2): 1338,
    (3, 1, 0): 1770,
    (3, 1, 1): 1986,
    (3, 2, 0): 2850,
}


SPLITS = {(48, 0): 0, (48, 48): 1024, (48, 64): 2048, (96, 0): 3072, (192, 0): 3584}
PLACES = (
    [(48, 4 + q, 5 + q) for q in range(2)] + [(48, 0, 8), (48, 0, 4), (48, 4, 8)]
    + [(48, 2 * q, 2 * q + 2) for q in range(4)] + [(96, q, q + 1) for q in range(4)]
    + [(96, 0, 4), (96, 0, 2), (96, 2, 4), (192, 0, 1), (192, 1, 2), (192, 0, 2)]
)


def remote(src, dst, send, recv, branch, tile):
    return pltpu.make_async_remote_copy(
        src_ref=src, dst_ref=dst, send_sem=send, recv_sem=recv, device_id=(branch, tile), device_id_type=MESH
    )


def slots_of(k):
    return [(t % 2 if t < 6 else k % 2, t // 2, (k // 2) % 4, k % 2) for t in range(7)]


def dot(a, b):
    return lax.dot_general(a, b, (((1,), (0,)), ((), ())), preferred_element_type=F32)


def dot_nt(a, b):
    return lax.dot_general(a, b, (((1,), (1,)), ((), ())), preferred_element_type=F32)


def unit_matrix(rows, cols, target):
    column = lax.broadcasted_iota(jnp.int32, (1, cols), 1)
    row = lax.broadcasted_iota(jnp.int32, (rows, cols), 0)
    return jnp.where(row == target(column), 1.0, 0.0).astype(BF)


def exchange_kernel(
    *refs,
):
    inputs, outputs, refs = refs[:13], refs[13:17], refs[17:]
    loaded, refs = refs[:13], refs[13:]
    (
        tiles, row_in, col_in, corner_in, shard_f, flat, row_f, col_f, row_out, col_out,
        e3, e2, e1, u3, u2, u1, wide, splits, copies_of,
        c0, c1, c2, c3, sg1, sg2, q20, q30a, q30b, q31, k1, k2a, k2b, nxt, out, strip, acc, acc_in,
        l_sem, h_send, h_recv, z_send, z_recv, s_send, s_recv, x_send, x_recv,
    ) = refs
    g1, g2, g3, g4, p1, p2, p3, p4, m20, m30a, m30b, m31, shard_in = loaded
    o1, o2, o3, o4 = outputs
    b = lax.axis_index("branch")
    k = lax.axis_index("tile")
    z, y, c = k // 8, lax.rem(k // 2, 4), lax.rem(k, 2)
    has_row = k < N_TILE - 1
    has_col = b < N_BRANCH - 1

    loads = [pltpu.make_async_copy(inputs[n], loaded[n], l_sem.at[n]) for n in range(13)]
    loads[12].start()

    def tile_of(zz, yy, cc):
        return zz * 8 + yy * 2 + cc

    def wrap(value, count):
        return lax.rem(value + count, count)

    left, right = wrap(b - 1, N_BRANCH), wrap(b + 1, N_BRANCH)
    up1, down1 = wrap(k - 1, N_TILE), wrap(k + 1, N_TILE)

    partners = [
        (b, up1), (b, down1), (left, k), (right, k), (left, up1), (right, down1),
        (b, tile_of(z, y, 1 - c)), (wrap(b + 2, 4), k),
    ] + [(b, tile_of(z, wrap(y + d, 4), c)) for d in (1, 2, 3)]
    along_z = [4, -4, 3, -3, 2, -2, 1, -1]
    partners += [(b, tile_of(wrap(z + d, NZ), y, c)) for d in along_z]
    barrier = pltpu.get_barrier_semaphore()
    for who in partners:
        pl.semaphore_signal(barrier, inc=1, device_id=who, device_id_type=MESH)
    for n in (1, 2, 3, 5, 6, 7, 8, 9, 10, 11, 0, 4):
        loads[n].start()

    loads[12].wait()
    whole = SHARD // 1024 * 1024
    rest = SHARD // 128 * 128
    row_at = [n // 128 for n in (whole, rest)]
    shard_f[0 : row_at[0], :] = shard_in[0:whole].astype(F32).reshape(row_at[0], 128)
    shard_f[row_at[0] : row_at[1], :] = shard_in[whole:rest].astype(F32).reshape(row_at[1] - row_at[0], 128)
    shard_f[row_at[1] : RAW_ROWS, :] = jnp.zeros((RAW_ROWS - row_at[1], 128), F32)
    shard_f[row_at[1] : row_at[1] + 1, 0 : SHARD - rest] = shard_in[rest:SHARD].astype(F32).reshape(1, SHARD - rest)
    for s in range(2):
        row = jnp.where(b == 3, 96, 32 * b + 16 * s)
        tiles[s, b, y, c, 4] = shard_f[pl.ds(pl.multiple_of(row, 16), 16), :].astype(BF)

    pl.semaphore_wait(barrier, len(partners))
    near = []
    for n, d in enumerate(along_z):
        copy = remote(
            tiles.at[:, b, y, c, 4], tiles.at[:, b, y, c, 4 - d], z_send.at[n], z_recv.at[n],
            b, tile_of(wrap(z + d, NZ), y, c),
        )
        copy.start()
        near.append(copy)

    for load in loads[:12]:
        load.wait()
    row_f[...] = jnp.zeros_like(row_f)
    col_f[...] = jnp.zeros_like(col_f)
    at_row, at_col = 0, 0
    for g, p in ((g2, p2), (g3, p3), (g4, p4)):
        rows = g.shape[0]
        masked = jnp.where(p[...].astype(F32) > 0, g[...].astype(F32), 0.0)
        for cell in range(8):
            row_f[at_row + cell : at_row + cell + 1, :] = masked[0:1, CELL * cell : CELL * (cell + 1)]
        col_f[at_col : at_col + rows, :] = masked[:, 0:CELL]
        at_row, at_col = at_row + 8, at_col + rows
    for m, at_row, at_col in ((m20, 24, 8), (m30a, 28, 12), (m31, 32, 18), (m30b, 36, 16)):
        rows, units = m.shape[0], m.shape[1] // CELL
        value = m[...].astype(F32)
        for unit in range(units):
            row_f[at_row + unit : at_row + unit + 1, :] = value[0:1, CELL * unit : CELL * (unit + 1)]
        col_f[at_col : at_col + rows, :] = value[:, 0:CELL]
    row_out[...] = row_f[...].astype(BF)
    col_out[...] = col_f[...].astype(BF)

    first = [
        remote(row_out, row_in, h_send.at[0], h_recv.at[0], b, up1),
        remote(col_out, col_in, h_send.at[1], h_recv.at[1], left, k),
        remote(col_out, corner_in, h_send.at[2], h_recv.at[2], left, up1),
    ]
    for copy in first:
        copy.start()

    for ref in (e3, e2, e1, c1, c2, c3, sg1, sg2, q20, q30a, q30b, q31, k1, k2a, k2b, nxt, acc):
        ref[...] = jnp.zeros_like(ref)

    def put(buffer, row, value):
        rows = value.shape[0]
        for l in range(3):
            buffer[l, row : row + rows, :] = value[:, 128 * l : 128 * (l + 1)]

    def spread_units(buffer, value, units):
        rows = value.shape[0]
        for unit in range(units):
            for l in range(3):
                piece = value[:, CELL * unit + 128 * l : CELL * unit + 128 * (l + 1)]
                if rows == 1:
                    buffer[l, unit : unit + 1, :] = piece
                else:
                    buffer[l, pl.ds(unit, rows, stride=units), :] = piece

    def masked(g, p):
        return jnp.where(p[...].astype(F32) > 0, g[...].astype(F32), 0.0)

    def flags(buffer):
        whole = jnp.concatenate([buffer[l] for l in range(3)], axis=1)
        return jnp.where(whole > 0, 1.0, 0.0).astype(BF)

    def target20(shift):
        def target(col):
            part, lane = col // CELL, lax.rem(col, CELL)
            pixel, channel = lane // 96, lax.rem(lane, 96) - shift
            return jnp.where((channel >= 0) & (channel < 48), part * 192 + pixel * 48 + channel, -1)

        return target

    def target31(col):
        part, lane = col // CELL, lax.rem(col, CELL)
        return jnp.where(lane < 192, part * 192 + lane, -1)

    def target30b(col):
        part, lane = col // CELL, lax.rem(col, CELL) - 192
        return jnp.where((lane >= 0) & (lane < 96), part * 96 + lane, -1)

    def keep(buffer, value, parts, count, extra_from, extra_rows, extra_to):
        for l in range(3):
            for part in range(parts):
                lanes = slice(part * CELL + 128 * l, part * CELL + 128 * (l + 1))
                buffer[l, pl.ds(part, count, stride=parts), :] = value[0:count, lanes]
            buffer[l, extra_to : extra_to + extra_rows, :] = value[
                extra_from : extra_from + extra_rows, 128 * l : 128 * (l + 1)
            ]

    def block_sums(buffer, rows, factor):
        groups = []
        for first in range(0, rows, factor):
            pieces = []
            for l in range(3):
                total = buffer[l, 8 * first : 8 * first + 8, :]
                for p in range(first + 1, first + factor):
                    total = total + buffer[l, 8 * p : 8 * p + 8, :]
                pieces.append(total)
            groups.append(jnp.concatenate(pieces, axis=1))
        return jnp.concatenate(groups, axis=0).astype(BF)

    def own_maps():
        spread_units(c0, masked(g1, p1), 8)
        for buffer, g, p in ((c1, g2, p2), (c2, g3, p3), (c3, g4, p4)):
            spread_units(buffer, masked(g, p), 8)
        for buffer, m, units in ((q20, m20, 4), (q30a, m30a, 4), (q31, m31, 4), (q30b, m30b, 2)):
            spread_units(buffer, m[...].astype(F32), units)

        for copy in first:
            copy.wait_recv()
        row_halo = row_in[...].astype(F32)
        col_halo = col_in[...].astype(F32)
        corner = corner_in[...].astype(F32)
        row_zero = jnp.where(has_row, row_halo, 0.0)
        col_zero = jnp.where(has_col, col_halo, 0.0)
        corner_zero = jnp.where(has_row & has_col, corner, 0.0)
        at = 0
        for buffer, rows, halo in ((c1, 4, 0), (c2, 2, 8), (c3, 1, 16)):
            put(buffer, 8 * rows, row_zero[halo : halo + 8])
            put(buffer, 8 * rows + 8, col_zero[at : at + rows])
            put(buffer, 8 * rows + 8 + rows, corner_zero[at : at + 1])
            at += rows
        for buffer, rows, units, halo, at in ((q20, 4, 4, 24, 8), (q30a, 4, 4, 28, 12), (q31, 2, 4, 32, 18), (q30b, 2, 2, 36, 16)):
            put(buffer, rows * units, row_halo[halo : halo + units])
            put(buffer, (rows + 1) * units, col_halo[at : at + rows])
            put(buffer, (rows + 1) * units + rows, corner[at : at + 1])

        mask1 = dot(flags(q20), unit_matrix(CELL, 768, target20(0))) + dot(
            flags(q30a), unit_matrix(CELL, 768, target20(48))
        )
        keep(k1, mask1, 2, 20, 20, 5, 40)
        keep(k2a, dot(flags(q31), unit_matrix(CELL, 768, target31)), 2, 12, 12, 3, 24)
        keep(k2b, dot(flags(q30b), unit_matrix(CELL, 1536, target30b)), 4, 6, 6, 3, 24)
        pooled = [block_sums(c0, 8, f) for f in (2, 4, 8)] + [block_sums(c1, 4, f) for f in (2, 4)] + [block_sums(c2, 2, 2)]
        for l in range(3):
            strip[0, l, C1 : C1 + 48, :] = c1[l]
            strip[0, l, C2 : C2 + 32, :] = c2[l]
            strip[0, l, C3 : C3 + 32, :] = c3[l]
            strip[0, l, K1 : K1 + 48, :] = k1[l]
            strip[0, l, K2 : K2 + 32, :] = k2a[l] + k2b[l]
        row = SUMS
        for value in pooled:
            rows = value.shape[0]
            for l in range(3):
                strip[0, l, row : row + rows, :] = value[:, 128 * l : 128 * (l + 1)].astype(F32)
            row += rows
        strip_copy.start()

    strip_copy = remote(
        strip.at[0], strip.at[1], x_send.at[0], x_recv.at[0], b, tile_of(z, y, 1 - c)
    )

    places = [lax.rem(zz - z + 4 + NZ, NZ) for zz in range(NZ)]
    lane_no = lax.broadcasted_iota(jnp.int32, (RAW_ROWS, 128), 1)

    def line_up(ranges):
        for shard in range(N_TILE):
            first_row, phase = divmod(SHARD * shard, 128)
            if not any(first_row < 3 * hi and first_row + 109 > 3 * lo for lo, hi in ranges):
                continue
            blocks = [tiles[s, x_at, y_at, c_at, places[shard // 8]] for s, x_at, y_at, c_at in slots_of(shard)]
            value = jnp.concatenate(blocks, axis=0).astype(F32)
            if phase == 0:
                flat[first_row : first_row + RAW_ROWS, :] = value
                continue
            value = pltpu.roll(value, phase, 1)
            pltpu.store(flat.at[first_row : first_row + RAW_ROWS, :], value, mask=lane_no >= phase)
            pltpu.store(flat.at[first_row + 1 : first_row + 1 + RAW_ROWS, :], value, mask=lane_no < phase)

    def load_rows(row, count):
        return [flat[pl.ds(3 * row + jb, count, stride=3), :].astype(BF) for jb in range(3)]

    def rows_of(key, rows, j, at=0):
        n = CELL // j
        width = 256 if j == 192 else 128

        lanes = SPLITS[j, at]
        whole = jnp.concatenate(load_rows(ROW0[key], rows), axis=1)
        split = dot(whole, splits[:, lanes : lanes + n * width])
        parts = []
        for half in range(width // 128):
            for part in range(n):
                wide[half, pl.ds(part, rows, stride=n), :] = split[
                    :, part * width + 128 * half : part * width + 128 * (half + 1)
                ]
            parts.append(wide[half, 0 : rows * n, :])
        return parts[0] if len(parts) == 1 else jnp.concatenate(parts, axis=1)

    def place(weights, j, low, high):
        lanes = CELL * PLACES.index((j, low, high))
        return dot(weights, copies_of[0 : weights.shape[1], lanes : lanes + CELL])

    def taps(e, row0, pitch, weights, placed, seg, nxt_seg, nxt_width):
        count = len(placed)
        i = weights.shape[0] // 9

        def tap(value, a, bb):
            return value[(3 * a + bb) * i : (3 * a + bb + 1) * i]

        for a in range(3):
            for q in range(count):
                even = row0 + CELL * a + 2 * q * pitch
                e[even : even + i, seg : seg + CELL] = tap(placed[q], a, 1).astype(BF)
                odd = even + pitch
                value = tap(placed[q], a, 2)
                if q + 1 < count:
                    value = value + tap(placed[q + 1], a, 0)
                else:
                    e[odd : odd + i, nxt_seg : nxt_seg + nxt_width] = tap(weights, a, 0).astype(BF)
                e[odd : odd + i, seg : seg + CELL] = value.astype(BF)

    def fill_e3(kernels):
        for key, i, row0, pitch in kernels:
            for a in range(3):
                even = row0 + CELL * a
                odd = even + pitch
                for bb, at, seg in ((1, even, 0), (2, odd, 0), (0, odd, CELL)):
                    for jb, piece in enumerate(load_rows(ROW0[key] + (3 * a + bb) * i, i)):
                        e3[at : at + i, seg + 128 * jb : seg + 128 * (jb + 1)] = piece

    def fill_e2_21():
        w = rows_of((2, 1, 0), 432, 192)
        taps(e2, 0, 96, w, [place(w.astype(BF), 192, q, q + 1) for q in range(2)], 0, 384, 256)

    def fill_e2_31():
        w = rows_of((3, 1, 0), 216, 96)
        taps(e2, 0, 96, w, [place(w.astype(BF), 96, q, q + 1) for q in range(2)], 640, 1024, 128)

    def fill_e2_mid():
        w = rows_of((2, 0, 1), 216, 192)
        placed = [place(w.astype(BF), 192, q, q + 1) for q in range(2)]
        taps(e2, 1152, 96, w, placed, 0, 384, 256)
        w = rows_of((3, 0, 1), 54, 48)
        w_next = rows_of((3, 0, 1), 54, 48, 64)
        placed = [place(w.astype(BF), 48, 4 + q, 5 + q) for q in range(2)]
        taps(e2, 1152 + 48, 96, w_next, placed, 640, 1024 + 128, 128)

    def fill_e1_10():
        w = rows_of((1, 0, 0), 108, 96)
        taps(e1, 0, 48, w, [place(w.astype(BF), 96, q, q + 1) for q in range(4)], 0, 384, 128)

    def fill_e1_mid():
        w = rows_of((2, 0, 0), 54, 48) + 0.0
        w = w + rows_of((3, 0, 0), 54, 48, 48)
        taps(e1, 0, 48, w, [place(w.astype(BF), 96, q, q + 1) for q in range(4)], 512, 896, 128)

    def fill_up():
        u3[:, 0:384] = place(rows_of((0, 3, 0), 48, 48).astype(BF), 48, 0, 8).astype(BF)
        u3[:, 384:768] = place(rows_of((1, 3, 0), 96, 96).astype(BF), 96, 0, 4).astype(BF)
        u3[:, 768:1152] = place(rows_of((2, 3, 0), 192, 192).astype(BF), 192, 0, 2).astype(BF)
        w02 = rows_of((0, 2, 0), 24, 48).astype(BF)
        w12 = rows_of((1, 2, 0), 48, 96).astype(BF)
        for q in range(2):
            u2[192 * q : 192 * (q + 1), 0:384] = place(w02, 48, 4 * q, 4 * q + 4).astype(BF)
            u2[192 * q : 192 * (q + 1), 384:768] = place(w12, 96, 2 * q, 2 * q + 2).astype(BF)
        w01 = rows_of((0, 1, 0), 12, 48).astype(BF)
        for q in range(4):
            u1[96 * q : 96 * (q + 1), :] = place(w01, 48, 2 * q, 2 * q + 2).astype(BF)

    def reader(t, base):
        return lambda l, lo, hi: strip[t, l, base + lo : base + hi, :]

    def section_reader(buffer, t):
        return lambda l, lo, hi: buffer[t, l, lo:hi, :]

    def cells_of(read, total):
        return [read(l, 0, total) for l in range(3)]

    def shifted(read, rows, total, count):
        pieces = []
        for l in range(count):
            nxt[l, 0 : 8 * rows, :] = read(l, 1, 8 * rows + 1)
            for p in range(rows):
                nxt[l, 8 * p + 7 : 8 * p + 8, :] = read(l, 8 * rows + p, 8 * rows + p + 1)
            nxt[l, 8 * rows : total, :] = jnp.zeros((total - 8 * rows, 128), F32)
            pieces.append(nxt[l, 0:total, :])
        return pieces

    def lhs(pieces):
        return jnp.concatenate([piece.astype(BF) for piece in pieces], axis=1)

    def both(make):
        return jnp.concatenate([make(t) for t in range(2)], axis=0)

    def level_three(t):
        read = reader(t, C3)
        return lhs(cells_of(read, 32) + shifted(read, 2, 32, 3))

    def level_two(t):
        read = reader(t, C2)
        return lhs(cells_of(read, 32) + shifted(read, 3, 32, 2))

    def level_one(t):
        read = reader(t, C1)
        return lhs(cells_of(read, 48) + shifted(read, 5, 48, 1))

    def sums_of(t, *blocks):
        pieces = []
        for start, rows in blocks:
            pieces += [strip[t, l, SUMS + start : SUMS + start + rows, :] for l in range(3)]
        return lhs(pieces)

    def taps_of(own, own_weights, after, after_weights):
        whole = dot_nt(own, own_weights)
        last = dot_nt(after, jnp.concatenate([after_weights[CELL * a + 256 : CELL * (a + 1)] for a in range(3)], axis=0))
        pieces = []
        for a in range(3):
            pieces.append(whole[:, CELL * a : CELL * a + 256])
            pieces.append(whole[:, CELL * a + 256 : CELL * (a + 1)] + last[:, 128 * a : 128 * (a + 1)])
        return jnp.concatenate(pieces, axis=1)

    def rows_out(y, a, lo, hi):
        return y[lo:hi, CELL * a : CELL * (a + 1)]

    def upsampled(y, p, base):
        lo = base + 8 * p
        even = rows_out(y, 1, lo, lo + 8)
        return even, rows_out(y, 2, lo, lo + 8) + rows_out(y, 0, lo + 8, lo + 16)

    def section(buffer, t, y, rows, y_base, kept):
        view = buffer.at[t]
        for p in range(rows):
            even, odd = upsampled(y, p, y_base)
            put(view, 16 * p, even)
            put(view, 16 * p + 8, odd)
        put(view, 16 * rows, rows_out(y, 1, y_base + 8 * rows, y_base + 8 * rows + 8))
        extra, base = 8 * (2 * rows + 1), y_base + 8 * (rows + 1)
        for p in range(rows + 1):
            put(view, extra + 2 * p, rows_out(y, 1, base + p, base + p + 1))
            if p < rows:
                odd = rows_out(y, 2, base + p, base + p + 1) + rows_out(y, 0, base + p + 1, base + p + 2)
                put(view, extra + 2 * p + 1, odd)
        for l in range(3):
            buffer[t, l] = jnp.where(strip[t, l, kept : kept + buffer.shape[2], :] > 0.5, buffer[t, l], 0.0)

    def direct():
        line_up(((0, 336), (606, 1230), (2850, 4578)))
        fill_e2_21()
        fill_e1_10()
        fill_up()
        fill_e3((((3, 2, 0), 192, 0, 192),))
        y3 = dot_nt(both(level_three), e3[0:1152, :])
        maps_two, maps_one = both(level_two), both(level_one)
        y2 = taps_of(maps_two[:, 0:384], e2[0:1152, 0:384], maps_two[:, 384:640], e2[0:1152, 384:640])
        y1 = taps_of(maps_one[:, 0:384], e1[:, 0:384], maps_one[:, 384:512], e1[:, 384:512])
        x3 = dot_nt(both(lambda t: sums_of(t, (48, 8), (72, 8), (80, 8))), u3[...])
        x2 = dot_nt(both(lambda t: sums_of(t, (32, 16), (56, 16))), u2[...])
        x1 = dot_nt(both(lambda t: sums_of(t, (0, 32))), u1[...])
        for t in (1, 0):
            view = acc.at[t]
            for p in range(4):
                even, odd = upsampled(y1, p, 48 * t)
                put(view, 16 * p, even)
                put(view, 16 * p + 8, odd)
            for p in range(2):
                even, odd = upsampled(y2, p, 32 * t)
                put(view, 64 + 16 * p, even + x1[32 * t + 16 * p : 32 * t + 16 * p + 8])
                put(view, 72 + 16 * p, odd + x1[32 * t + 16 * p + 8 : 32 * t + 16 * p + 16])
            even, odd = upsampled(y3, 0, 32 * t)
            put(view, 96, even + x2[16 * t : 16 * t + 8])
            put(view, 104, odd + x2[16 * t + 8 : 16 * t + 16])
            put(view, 112, x3[8 * t : 8 * t + 8])

    def chained():
        line_up(((336, 606), (1230, 2850)))
        fill_e2_31()
        fill_e2_mid()
        fill_e1_mid()
        fill_e3((((3, 1, 1), 96, 1152, 96), ((3, 0, 2), 48, 1152 + 192, 48)))
        maps_two = both(level_two)
        y2_maps = taps_of(maps_two[:, 0:384], e2[1152:2304, 0:384], maps_two[:, 384:640], e2[1152:2304, 384:640])
        y3 = dot_nt(both(level_three), e3[1152:2304, :])
        for t in range(2):
            section(sg2, t, y3, 1, 32 * t, K2)

        def grads_two(t):
            read = section_reader(sg2, t)
            return lhs(cells_of(read, 32) + shifted(read, 3, 32, 2))

        grads = both(grads_two)
        y2 = y2_maps + taps_of(
            grads[:, 128:384], e2[1152:2304, 768:1024], grads[:, 512:640], e2[1152:2304, 1152:1280]
        )
        for t in range(2):
            section(sg1, t, y2, 2, 32 * t, K1)

        def grads_one(t):
            read = section_reader(sg1, t)
            return lhs(cells_of(read, 48) + shifted(read, 5, 48, 1))

        ones = both(grads_one)
        y1 = taps_of(ones[:, 0:384], e1[:, 512:896], ones[:, 384:512], e1[:, 896:1024])
        y2 = taps_of(grads[:, 0:256], e2[0:1152, 640:896], grads[:, 384:512], e2[0:1152, 1024:1152])
        for t in (1, 0):
            view = acc.at[t]
            for p in range(4):
                even, odd = upsampled(y1, p, 48 * t)
                put(view, 16 * p, even)
                put(view, 16 * p + 8, odd)
            for p in range(2):
                even, odd = upsampled(y2, p, 32 * t)
                put(view, 64 + 16 * p, even)
                put(view, 72 + 16 * p, odd)

    def emit(ref, rows, base, maps_of):
        for l in range(3):
            out[l, 0 : 8 * rows, :] = (
                maps_of[l, 0 : 8 * rows, :] + acc[0, l, base : base + 8 * rows, :] + acc_in[l, base : base + 8 * rows, :]
            )
        for cell in range(8):
            for l in range(3):
                lane0 = CELL * cell + 128 * l
                if rows == 1:
                    piece = out[l, cell : cell + 1, :]
                else:
                    piece = out[l, pl.ds(cell, rows, stride=8), :]
                ref[:, lane0 : lane0 + 128] = piece.astype(BF)

    class Part:
        def __init__(self, s, lo, size, sem):
            self.s, self.lo, self.size, self.used = s, lo, size, sem
            self.u, self.v = (b, y) if s == 0 else (y, b)
            self.pending, self.second = [], []

        def holds(self, x_of):
            return (x_of != 3) | (c == self.s)

        def send(self, ref, x_to, tile_to, x_of=None):
            copy = remote(ref, ref, s_send.at[self.used], s_recv.at[self.used], x_to, tile_to)
            self.used += 1
            self.pending.append((copy, x_of))
            self.when(x_of, copy.start)
            return copy

        def when(self, x_of, act):
            if x_of is None:
                act()
            else:
                pl.when(self.holds(x_of))(act)

        def send_bundle(self, u_of, to_u, to_v):
            zs = pl.ds(self.lo, self.size)
            if self.s == 0:
                return self.send(tiles.at[0, u_of, y, c, zs], to_u, tile_of(z, to_v, c), u_of)
            return self.send(tiles.at[1, b, u_of, c, zs], to_v, tile_of(z, to_u, c), b)

        def spread(self, u_of):
            self.second.append((u_of, [(d, self.send_bundle(u_of, self.u, wrap(self.v + d, 4))) for d in (2, 1, 3)]))

        def start(self):
            self.first = [(d, self.send_bundle(self.u, wrap(self.u + d, 4), self.v)) for d in (2, 1, 3)]

        def pass_on(self):
            for d, copy in self.first:
                u_of = wrap(self.u - d, 4)
                self.when(u_of if self.s == 0 else b, copy.wait_recv)
                self.spread(u_of)

        def cross(self):
            zs = pl.ds(self.lo, self.size)
            self.across = []
            for u_of, copies_in in self.second:
                for d, copy in copies_in:
                    self.when(u_of if self.s == 0 else wrap(b - d, 4), copy.wait_recv)
                ref = tiles.at[0, u_of, :, c, zs] if self.s == 0 else tiles.at[1, :, u_of, c, zs]
                self.across.append(self.send(ref, b, tile_of(z, y, 1 - c)))

        def arrived(self):
            for copy in self.across:
                copy.wait_recv()

        def sent(self):
            for copy, x_of in self.pending:
                self.when(x_of, copy.wait_send)

    for copy in near:
        copy.wait_recv()
    far = [
        remote(
            tiles.at[:, b, y, c, pl.ds(lo, size)], tiles.at[:, b, y, c, pl.ds(to, size)], z_send.at[8 + n], z_recv.at[8 + n],
            b, tile_of(wrap(z + d, NZ), y, c),
        )
        for n, (lo, size, to, d) in enumerate(((5, 4, 9, -4), (1, 3, 13, 4)))
    ]
    for copy in far:
        copy.start()
    parts = [Part(s, lo, size, 19 * (2 * n + s)) for n, (lo, size) in enumerate(Z_PARTS) for s in range(2)]
    for part in parts[:2]:
        part.start()
    for part in parts[:2]:
        part.spread(part.u)
    own_maps()
    for (j, at), lanes in SPLITS.items():
        width = 256 if j == 192 else 128

        def split_target(col):
            part, lane = col // width, lax.rem(col, width) - at
            return jnp.where((lane >= 0) & (lane < j), part * j + lane, -1)

        splits[:, lanes : lanes + CELL // j * width] = unit_matrix(CELL, CELL // j * width, split_target)
    for number, (j, low, high) in enumerate(PLACES):

        def place_target(col):
            which = col // j
            return jnp.where((which >= low) & (which < high), lax.rem(col, j), -1)

        rows = 256 if j == 192 else 128
        copies_of[0:rows, CELL * number : CELL * (number + 1)] = unit_matrix(rows, CELL, place_target)

    for part in parts[:2]:
        part.pass_on()
    for copy in far:
        copy.wait_recv()
    for part in parts[2:]:
        part.start()
    for part in parts[2:]:
        part.spread(part.u)
    for part in parts[2:]:
        part.pass_on()
    for part in parts:
        part.cross()
    strip_copy.wait_recv()
    for part in parts:
        part.arrived()
    pl.when(c == 0)(direct)
    pl.when(c == 1)(chained)
    acc_copy = remote(acc.at[1], acc_in, x_send.at[1], x_recv.at[1], b, tile_of(z, y, 1 - c))
    acc_copy.start()
    for part in parts:
        part.sent()
    for copy in near + far + first + [strip_copy]:
        copy.wait_send()
    acc_copy.wait_recv()
    emit(o4, 1, 112, c3)
    emit(o3, 2, 96, c2)
    emit(o2, 4, 64, c1)
    emit(o1, 8, 0, c0)
    acc_copy.wait_send()


def finish_kernel(*refs):
    for n in range(4):
        refs[4 + n][...] = refs[n][...]


ANY = pl.BlockSpec(memory_space=pl.ANY)
VMEM = pl.BlockSpec(memory_space=pltpu.VMEM)
TILES = (2, 4, 4, 2, NZ, 16, 128)


def per_device(*operands):
    maps = operands[:12]

    def cells(rows):
        return pltpu.VMEM((3, rows, 128), F32)

    def buffer(*shape):
        return pltpu.VMEM(shape, BF)

    def sems(count):
        return pltpu.SemaphoreType.DMA((count,))

    results = [jax.ShapeDtypeStruct(g.shape, BF) for g in maps[:4]]
    done = pl.pallas_call(
        exchange_kernel,
        out_shape=[pltpu.VMEM(g.shape, BF) for g in maps[:4]],
        in_specs=[ANY] * 13,
        out_specs=[VMEM] * 4,
        scratch_shapes=[buffer(*m.shape) for m in maps] + [
            buffer(SHARD),
            buffer(*TILES), buffer(48, CELL), buffer(32, CELL), buffer(32, CELL),
            pltpu.VMEM((RAW_ROWS, 128), F32), pltpu.VMEM((FLAT_ROWS, 128), F32),
            pltpu.VMEM((48, CELL), F32), pltpu.VMEM((32, CELL), F32), buffer(48, CELL), buffer(32, CELL),
            buffer(2304, 768), buffer(2304, 1280), buffer(1152, 1024),
            buffer(384, 1152), buffer(384, 768), buffer(384, 384),
            pltpu.VMEM((2, 1024, 128), F32), buffer(CELL, 4096), buffer(256, CELL * len(PLACES)),
            cells(64), cells(48), cells(32), cells(32),
            pltpu.VMEM((2, 3, 48, 128), F32), pltpu.VMEM((2, 3, 32, 128), F32),
            cells(32), cells(32), cells(16), cells(16), cells(48), cells(32), cells(32), cells(48), cells(64),
            pltpu.VMEM((2, 3, STRIP, 128), F32), pltpu.VMEM((2, 3, 120, 128), F32), cells(120),
            sems(13), sems(3), sems(3), sems(10), sems(10), sems(38 * len(Z_PARTS)), sems(38 * len(Z_PARTS)), sems(2), sems(2),
        ],
        compiler_params=pltpu.CompilerParams(
            collective_id=0, has_side_effects=True, vmem_limit_bytes=60 * 2**20
        ),
        name="exchange",
    )(*operands)
    return pl.pallas_call(
        finish_kernel,
        out_shape=results,
        in_specs=[VMEM] * 4,
        out_specs=[VMEM] * 4,
        compiler_params=pltpu.CompilerParams(vmem_limit_bytes=4 * 2**20),
        name="finish",
    )(*done)


def solution(mesh):
    maps = P("tile", "branch")
    return jax.shard_map(
        per_device, mesh=mesh, in_specs=(maps,) * 12 + (P("tile"),), out_specs=(maps,) * 4, check_vma=False
    )
```
